256 devices in a mesh: row: 32 (over x, y, core), col: 8 (over z).
Axes of the slice: x: 4, y: 4, z: 8, core: 2. Of those that a mesh axis runs over, the one named last changes fastest.
Arguments:
- rhs: float32 [64, 16384], P(None, 'row'), may hold values from -60 to 60
- near_flags: int32 [32, 32], P('row', 'col'), may hold values from 0 to 1, as said below
- near_blocks: bfloat16 [32, 32, 512, 512], P('row', 'col'), may hold values from -0.0625 to 0.0625
- far_columns: bfloat16 [32, 32, 64, 512], P('row', 'col'), may hold values from -0.25 to 0.25
- row_basis: bfloat16 [32, 64, 512], P('row'), may hold values from -0.125 to 0.125
- self_term: float32 [16384], P('row'), may hold values from 1.5 to 3
- diag_inverse: float32 [32, 512, 512], P('row'), may hold values from -2 to 2
- lower_block: float32 [32, 512, 512], P('row'), may hold values from -3 to 3
Outputs:
- solution: float32 [64, 16384], P(None, 'row')
The draws below stay inside these ranges and needn't reach their ends.
Inputs may be any that keep to these rules, and one draw needn't show every extreme that they name: near_flags[i, i] and near_flags[i, i - 1], near_flags[i, i + 1] are 1.
All inputs are finite; a program needn't handle non-finite values.
Results may differ from the reference program's by a relative error of at most 0.00065.
Values may be sent and summed in bfloat16 or wider, within the bound.
A program may use at most 128 MiB of HBM per device.

```python
import math
import jax
import jax.numpy as jnp
from jax import lax

CLUSTER = 512
BASIS = 64
SYSTEMS = 64
CLUSTERS = 32
UNKNOWNS = 16384


def draw_rhs(key, part):
    key = jax.random.fold_in(key, 4)
    first_key, second_key, third_key = jax.random.split(key, 3)
    system_scale = jnp.exp(jax.random.uniform(first_key, (SYSTEMS, 1), jnp.float32, 0.0, math.log(10.0)))
    entry_scale = jnp.exp(jax.random.uniform(second_key, (1, UNKNOWNS), jnp.float32, 0.0, math.log(10.0)))
    values = jax.random.normal(third_key, (SYSTEMS, UNKNOWNS), jnp.float32)
    return jnp.clip(values, -5.5, 5.5) * system_scale * entry_scale / 10.0


def draw_near_flags(key, part):
    key = jax.random.fold_in(key, 1)
    row_ids = jnp.arange(CLUSTERS)[:, None]
    col_ids = jnp.arange(CLUSTERS)[None, :]
    adjacent = jnp.abs(row_ids - col_ids) <= 1
    random_bits = jax.random.randint(key, (CLUSTERS, CLUSTERS), 0, 4) == 0
    return jnp.where(adjacent | random_bits, 1, 0).astype(jnp.int32)


def factor_block(key, low_value, high_value, noise_scale):
    first_key, second_key = jax.random.split(key)
    diagonal_values = jnp.exp(jax.random.uniform(first_key, (CLUSTERS, 1, CLUSTER), jnp.float32, math.log(low_value), math.log(high_value)))
    noise = jnp.clip(jax.random.normal(second_key, (CLUSTERS, CLUSTER, CLUSTER), jnp.float32), -5.0, 5.0)
    identity = jnp.eye(CLUSTER, dtype=jnp.float32)[None]
    return identity * diagonal_values + noise * (noise_scale / math.sqrt(CLUSTER))


def draw_diag_inverse(key, part):
    key = jax.random.fold_in(key, 2)
    return factor_block(key, 0.4, 0.5, 0.15)


def draw_lower_block(key, part):
    key = jax.random.fold_in(key, 3)
    return factor_block(key, 1.75, 1.9, 0.4)


def level_of(own_key, extent, shards, smallest, high):
    level = 1.0
    for position, shards_of in shards:
        draws = jax.random.uniform(jax.random.fold_in(jax.random.fold_in(own_key, 6), position), (shards_of,), jnp.float32, smallest / len(shards), high / len(shards))
        level = level * jnp.repeat(jnp.exp(draws), extent[position] // shards_of).reshape((-1,) + (1,) * (len(extent) - 1 - position))
    return level


def gaussian(stream_key, dims, width, most, shards=(), kind=jnp.bfloat16):
    array = jax.random.normal(stream_key, dims, jnp.float32) * width
    if len(shards) > 0:
        array = level_of(stream_key, dims, shards, -0.22, 0.18) * array
    return jnp.clip(array, min=-most, max=most).astype(kind)


def setup_inputs(seed: int = 0) -> dict:
    arg_keys = jax.random.split(jax.random.key(seed), 9)
    return {
        "rhs": draw_rhs(jax.random.fold_in(arg_keys[8], 71), 0),
        "near_flags": draw_near_flags(jax.random.fold_in(arg_keys[8], 71), 0),
        "near_blocks": gaussian(arg_keys[2], (CLUSTERS, CLUSTERS, CLUSTER, CLUSTER), (16 * CLUSTER) ** -0.5, 0.0625, ((0, 32), (1, 8))),
        "far_columns": gaussian(arg_keys[3], (CLUSTERS, CLUSTERS, BASIS, CLUSTER), CLUSTER ** -0.5, 0.25, ((0, 32), (1, 8))),
        "row_basis": gaussian(arg_keys[4], (CLUSTERS, BASIS, CLUSTER), (BASIS * CLUSTERS) ** -0.5, 0.125, ((0, 32),)),
        "self_term": jnp.clip(jnp.exp(math.log(3.0) - 0.6931472 * jax.random.uniform(arg_keys[5], (UNKNOWNS,), jnp.float32) ** level_of(arg_keys[5], (UNKNOWNS,), ((0, 32),), -0.2, 0.2)), 1.5, 3.0),
        "diag_inverse": draw_diag_inverse(jax.random.fold_in(arg_keys[8], 71), 0),
        "lower_block": draw_lower_block(jax.random.fold_in(arg_keys[8], 71), 0),
    }


epsilon = 1e-06
highest = lax.Precision.HIGHEST

def column_norm(vector):
    return jnp.sqrt(lax.optimization_barrier(jnp.sum(vector * vector, axis=1)) + epsilon)

def apply_matrix(solved, near_flags, near_blocks, far_columns, row_basis, self_term):
    rounded = lax.optimization_barrier(solved.astype(jnp.bfloat16)).astype(jnp.float32)
    grouped = rounded.reshape(SYSTEMS, CLUSTERS, CLUSTER)

    def one_row(inputs):
        flag_row, block_row, column_row, basis_row = inputs
        weight = flag_row.astype(jnp.float32)
        near_in = grouped * weight[None, :, None]
        far_in = grouped - near_in
        near_part = jnp.einsum('skb,kbd->sd', near_in, block_row.astype(jnp.float32))
        far_coef = jnp.einsum('skb,krb->sr', far_in, column_row.astype(jnp.float32))
        coef_round = far_coef.astype(jnp.bfloat16)
        return near_part + jnp.dot(coef_round, basis_row, preferred_element_type=jnp.float32)
    coupled = lax.map(one_row, (near_flags, near_blocks, far_columns, row_basis))
    coupled = jnp.transpose(coupled, (1, 0, 2)).reshape(SYSTEMS, UNKNOWNS)
    return self_term[None, :] * solved + coupled

def precondition(vector, diag_inverse, lower_block):
    blocks = jnp.transpose(vector.reshape(SYSTEMS, CLUSTERS, CLUSTER), (1, 0, 2))

    def advance(previous, inputs):
        value, inverse, lower = inputs
        current = jnp.dot(value - jnp.dot(previous, lower, precision=highest), inverse, precision=highest)
        return (current, current)
    start = jnp.zeros((SYSTEMS, CLUSTER), jnp.float32)
    final_state, outcome = lax.scan(advance, start, (blocks, diag_inverse, lower_block))
    return jnp.transpose(outcome, (1, 0, 2)).reshape(SYSTEMS, UNKNOWNS)

def least_squares(beta, proj_one, norm_one, cross, proj_two, norm_two):
    radius_one = jnp.sqrt(proj_one * proj_one + norm_one * norm_one)
    cos_one = proj_one / radius_one
    sin_one = norm_one / radius_one
    upper = cos_one * cross + sin_one * proj_two
    middle = cos_one * proj_two - sin_one * cross
    radius_two = jnp.sqrt(middle * middle + norm_two * norm_two)
    weight_two = -(middle / radius_two) * sin_one * beta / radius_two
    weight_one = (cos_one * beta - upper * weight_two) / radius_one
    return (weight_one, weight_two)

def reference(rhs, near_flags, near_blocks, far_columns, row_basis, self_term, diag_inverse, lower_block):
    beta = column_norm(rhs)
    first = rhs / beta[:, None]
    pre_one = precondition(first, diag_inverse, lower_block)
    image = apply_matrix(pre_one, near_flags, near_blocks, far_columns, row_basis, self_term)
    proj_one = lax.optimization_barrier(jnp.sum(first * image, axis=1))
    image = image - proj_one[:, None] * first
    norm_one = column_norm(image)
    second = image / norm_one[:, None]
    pre_two = precondition(second, diag_inverse, lower_block)
    image = apply_matrix(pre_two, near_flags, near_blocks, far_columns, row_basis, self_term)
    cross = lax.optimization_barrier(jnp.sum(first * image, axis=1))
    proj_two = lax.optimization_barrier(jnp.sum(second * image, axis=1))
    image = image - cross[:, None] * first - proj_two[:, None] * second
    norm_two = column_norm(image)
    weight_one, weight_two = least_squares(beta, proj_one, norm_one, cross, proj_two, norm_two)
    return pre_one * weight_one[:, None] + pre_two * weight_two[:, None]
```

```python
import functools

import jax
import jax.numpy as jnp
from jax import lax
from jax.experimental import pallas as pl
from jax.experimental.pallas import tpu as pltpu
from jax.sharding import PartitionSpec as P

epsilon = 1e-06
f32 = jnp.float32
bf16 = jnp.bfloat16
MESH = pl.DeviceIdType.MESH
SYS = 8


def stacked(x):
    high = x.astype(bf16).astype(f32)
    return jnp.concatenate([high, x - high], axis=0).astype(bf16)


def times(x, mat):
    y = jnp.dot(stacked(x), mat, preferred_element_type=f32)
    n, c = x.shape[0], mat.shape[1] // 2
    y = y[:n] + y[n:]
    return y[:, :c] + y[:, c:]


def put_split(ref, rows, m):
    c = m.shape[1]
    high = m.astype(bf16)
    ref[rows, :c] = high
    ref[rows, c:] = (m - high.astype(f32)).astype(bf16)


def total(x):
    return jnp.sum(x, axis=1, keepdims=True)


def least_squares(beta, proj_one, norm_one, cross, proj_two, norm_two):
    radius_one = jnp.sqrt(proj_one * proj_one + norm_one * norm_one)
    cos_one = proj_one / radius_one
    sin_one = norm_one / radius_one
    upper = cos_one * cross + sin_one * proj_two
    middle = cos_one * proj_two - sin_one * cross
    radius_two = jnp.sqrt(middle * middle + norm_two * norm_two)
    weight_two = -(middle / radius_two) * sin_one * beta / radius_two
    weight_one = (cos_one * beta - upper * weight_two) / radius_one
    return (weight_one, weight_two)


def kernel(
    rows, cols, tile,
    rhs, flags, near, far, basis, selft, dinv, low, out,
    dsp, mats, m0, crecv, csend, ebuf, prev, pcur, piece, zbuf, pbuf, part, stile, gath, fsend, fin,
    m_send, m_recv, c_send, c_recv, p_send, p_recv, z_send, z_recv, r_send, r_recv, g_send, g_recv,
    f_send, f_recv,
):
    row = lax.axis_index("row")
    col = lax.axis_index("col")
    chip = row // 2
    core = row % 2
    last = rows // 2 - 1
    per = rows // cols
    home = row // per
    c = dinv.shape[-1]
    half = c // 2
    rank = basis.shape[1]

    bar = pltpu.get_barrier_semaphore()

    def tell(r, k):
        pl.semaphore_signal(bar, inc=1, device_id=(r, k), device_id_type=MESH)

    @pl.loop(1, rows)
    def _(t):
        tell(lax.rem(row + t, rows), col)

    @pl.loop(1, cols)
    def _(t):
        tell(row, lax.rem(col + t, cols))

    @pl.loop(0, rows)
    def _(t):
        r = per * col + t // cols
        k = t % cols

        @pl.when(jnp.logical_or(r != row, k != col))
        def _():
            tell(r, k)

    @pl.when(chip > 0)
    def _():
        tell(2 * chip - 1, col)

    @pl.when(core == 1)
    def _():
        tell(row - 1, col)

    expected = (rows - 1) + (cols - 1) + rows
    expected = expected - jnp.where(home == col, 1, 0)
    expected = expected + jnp.where(core == 0, 1, jnp.where(chip < last, 2, 0))
    pl.semaphore_wait(bar, expected)

    def spread(turn):
        @pl.loop(1, rows)
        def _(t):
            pltpu.make_async_remote_copy(
                src_ref=stile.at[turn], dst_ref=gath.at[turn, t - 1],
                send_sem=g_send.at[turn], recv_sem=g_recv.at[turn],
                device_id=(lax.rem(row + t, rows), col), device_id_type=MESH,
            ).start()

    def arrive(turn):
        pltpu.make_async_copy(gath.at[turn], gath.at[turn], g_recv.at[turn]).wait()

    v = rhs[pl.ds(pl.multiple_of(col * SYS, SYS), SYS), :]
    stile[0] = jnp.broadcast_to(total(v * v), (SYS, 128))
    spread(0)

    @pl.loop(0, c // tile)
    def _(t):
        at = pl.ds(pl.multiple_of(t * tile, tile), tile)
        put_split(dsp, at, dinv[0, at, :])

    place = 1 - core

    def to_sibling(t):
        at = pl.ds(pl.multiple_of(t * tile, tile), tile)
        return pltpu.make_async_remote_copy(
            src_ref=mats.at[1, at], dst_ref=m0.at[at],
            send_sem=m_send.at[t], recv_sem=m_recv.at[t],
            device_id=(row - core + 1, col), device_id_type=MESH,
        )

    @pl.loop(0, c // tile)
    def _(t):
        at = pl.ds(pl.multiple_of(t * tile, tile), tile)
        put_split(mats.at[place], at, times(low[0, at, :], dsp[...]))

        @pl.when(core == 0)
        def _():
            to_sibling(t).start()

    @pl.when(core == 1)
    def _():
        @pl.loop(0, c // tile)
        def _(t):
            to_sibling(t).wait_recv()
            at = pl.ds(pl.multiple_of(t * tile, tile), tile)
            both = jnp.concatenate([m0[at, :c], m0[at, c:]], axis=0)
            y = jnp.dot(both, mats[0], preferred_element_type=f32)
            y = y[:tile] + y[tile:]
            put_split(mats.at[1], at, y[:, :c] + y[:, c:])

    sign = jnp.where(core == 0, -1.0, 1.0).astype(f32)

    def c_copy(app):
        return pltpu.make_async_remote_copy(
            src_ref=csend.at[app], dst_ref=crecv.at[app],
            send_sem=c_send.at[app], recv_sem=c_recv.at[app],
            device_id=(row - core + 1, col), device_id_type=MESH,
        )

    def p_copy(app, to):
        return pltpu.make_async_remote_copy(
            src_ref=pcur.at[app], dst_ref=prev.at[app],
            send_sem=p_send.at[app, to], recv_sem=p_recv.at[app],
            device_id=(2 * chip + 2 + to, col), device_id_type=MESH,
        )

    def chain(app, vec):
        own = times(vec, dsp[...])

        @pl.when(core == 0)
        def _():
            csend[app] = own
            c_copy(app).start()
            ebuf[...] = own

        @pl.when(core == 1)
        def _():
            c_copy(app).wait_recv()
            ebuf[...] = own - times(crecv[app], mats[0])

        @pl.when(chip == 0)
        def _():
            pcur[app] = ebuf[...]

        @pl.when(chip > 0)
        def _():
            p_copy(app, 0).wait_recv()
            pcur[app] = ebuf[...] + sign * times(prev[app], mats[1])

        @pl.when(jnp.logical_and(core == 1, chip < last))
        def _():
            p_copy(app, 1).start()
            p_copy(app, 0).start()

    def z_copy(app, t):
        return pltpu.make_async_remote_copy(
            src_ref=piece.at[app], dst_ref=zbuf.at[app, lax.rem(row, per), col],
            send_sem=z_send.at[app, t], recv_sem=z_recv.at[app, lax.rem(row, per)],
            device_id=(lax.rem(row + t, rows), home), device_id_type=MESH,
        )

    def r_copy(app, t):
        to = lax.rem(col + t, cols)
        return pltpu.make_async_remote_copy(
            src_ref=pbuf.at[app, to], dst_ref=part.at[app, t - 1],
            send_sem=r_send.at[app], recv_sem=r_recv.at[app],
            device_id=(row, to), device_id_type=MESH,
        )

    def apply_matrix(app, pre):
        piece[app] = jnp.concatenate([pre[:, :half], pre[:, half:]], axis=0).astype(bf16)

        @pl.when(home == col)
        def _():
            pltpu.make_async_copy(
                piece.at[app], zbuf.at[app, lax.rem(row, per), col], z_recv.at[app, lax.rem(row, per)]
            ).start()

        @pl.when(home != col)
        def _():
            z_copy(app, 0).start()

        @pl.loop(1, rows)
        def _(t):
            z_copy(app, t).start()

        near_sum = jnp.zeros((SYS * cols, c), f32)
        far_sum = jnp.zeros((SYS * cols, rank), f32)
        for j in range(per):
            pltpu.make_async_copy(zbuf.at[app, j], zbuf.at[app, j], z_recv.at[app, j]).wait()
            z = zbuf[app, j].astype(f32)
            z = jnp.concatenate(
                [z[:, :SYS].reshape(SYS * cols, half), z[:, SYS:].reshape(SYS * cols, half)], axis=1
            )
            near_in = z * flags[0, j].astype(f32)
            far_in = (z - near_in).astype(bf16)
            near_sum += jnp.dot(near_in.astype(bf16), near[0, j], preferred_element_type=f32)
            far_sum += lax.dot_general(
                far_in, far[0, j], (((1,), (1,)), ((), ())), preferred_element_type=f32
            )
        pbuf[app, :, :, :c] = near_sum.reshape(cols, SYS, c)
        pbuf[app, :, :, c:] = jnp.concatenate(
            [far_sum, jnp.zeros((SYS * cols, 128 - rank), f32)], axis=1
        ).reshape(cols, SYS, 128)

        @pl.loop(1, cols)
        def _(t):
            r_copy(app, t).start()

        pltpu.make_async_copy(part.at[app], part.at[app], r_recv.at[app]).wait()
        both = pbuf[app, col]
        for t in range(cols - 1):
            both += part[app, t]
        far_part = jnp.dot(
            both[:, c:c + rank].astype(bf16), basis[0], preferred_element_type=f32
        )
        return selft[...] * pre + both[:, :c] + far_part

    lane = lax.broadcasted_iota(jnp.int32, (SYS, 128), 1)

    arrive(0)
    own_square = stile[0]
    squares = own_square
    for t in range(rows - 1):
        squares += gath[0, t]
    beta_tile = jnp.sqrt(squares + epsilon)
    beta = beta_tile[:, :1]
    first = v / beta
    chain(0, first)
    pre_one = pcur[0]
    image = apply_matrix(0, pre_one)

    def along(size):
        return jnp.sqrt(size) / beta_tile

    root = along(own_square)[:, :1]
    height = total(first * image)
    some = root > 1e-15
    scaled = jnp.where(some, height / jnp.where(some, root, 1.0), 0.0)
    slope = jnp.where(some, scaled / jnp.where(some, root, 1.0), 0.0)
    left = image - slope * first
    rest = jnp.sqrt(total(left * left))
    stile[1] = jnp.where(lane == 0, height, jnp.where(lane == 1, scaled, jnp.where(lane == 2, rest, 0.0)))

    @pl.when(chip > 0)
    def _():
        spread(1)

    chain(1, image)

    @pl.when(chip == 0)
    def _():
        spread(1)

    arrive(1)
    heights = stile[1]
    for t in range(rows - 1):
        heights += gath[1, t]
    proj_one = heights[:, :1]
    weight = jnp.where(lane == 1, proj_one, 0.0)
    keep = jnp.where(jnp.logical_or(lane == 1, lane == 2), 1.0, 0.0)

    def term(x, size):
        y = (x - weight * along(size)) * keep
        return y * y

    squares = term(stile[1], own_square)
    for t in range(rows - 1):
        squares += term(gath[1, t], gath[0, t])
    norm_one = jnp.sqrt(total(squares) + epsilon)
    second = (image - proj_one * first) / norm_one
    pre_two = (pcur[1] - proj_one * pre_one) / norm_one
    image = apply_matrix(1, pre_two)

    stile[2] = jnp.where(
        lane == 0, total(first * image), jnp.where(lane == 1, total(second * image), 0.0)
    )
    spread(2)
    arrive(2)
    heights = stile[2]
    for t in range(rows - 1):
        heights += gath[2, t]
    cross = heights[:, :1]
    proj_two = heights[:, 1:2]
    image = image - cross * first - proj_two * second
    stile[3] = jnp.broadcast_to(total(image * image), (SYS, 128))
    spread(3)
    arrive(3)
    squares = stile[3]
    for t in range(rows - 1):
        squares += gath[3, t]
    norm_two = jnp.sqrt(squares[:, :1] + epsilon)
    weight_one, weight_two = least_squares(beta, proj_one, norm_one, cross, proj_two, norm_two)
    answer = pre_one * weight_one + pre_two * weight_two
    fsend[...] = answer

    def f_copy(t):
        return pltpu.make_async_remote_copy(
            src_ref=fsend, dst_ref=fin.at[t - 1], send_sem=f_send, recv_sem=f_recv,
            device_id=(row, lax.rem(col + t, cols)), device_id_type=MESH,
        )

    @pl.loop(1, cols)
    def _(t):
        f_copy(t).start()

    out[pl.ds(pl.multiple_of(col * SYS, SYS), SYS), :] = answer

    @pl.when(core == 0)
    def _():
        @pl.loop(0, c // tile)
        def _(t):
            to_sibling(t).wait_send()

    for app in range(2):
        @pl.when(core == 0)
        def _():
            c_copy(app).wait_send()

        @pl.when(jnp.logical_and(core == 1, chip < last))
        def _():
            p_copy(app, 0).wait_send()
            p_copy(app, 1).wait_send()

        @pl.when(home != col)
        def _():
            z_copy(app, 0).wait_send()

        @pl.loop(1, rows)
        def _(t):
            z_copy(app, t).wait_send()

        pltpu.make_async_copy(part.at[app], part.at[app], r_send.at[app]).wait()

    for turn in range(4):
        pltpu.make_async_copy(gath.at[turn], gath.at[turn], g_send.at[turn]).wait()

    pltpu.make_async_copy(fin, fin, f_recv).wait()
    for t in range(1, cols):
        at = lax.rem(col + cols - t, cols)
        out[pl.ds(pl.multiple_of(at * SYS, SYS), SYS), :] = fin[t - 1]
    pltpu.make_async_copy(fin, fin, f_send).wait()


def body(rows, cols, rhs, flags, near, far, basis, selft, dinv, low):
    c = dinv.shape[-1]
    per = rows // cols
    tile = min(128, c)
    vm = pltpu.VMEM
    dma = pltpu.SemaphoreType.DMA
    vmem = pl.BlockSpec(memory_space=pltpu.VMEM)
    smem = pl.BlockSpec(memory_space=pltpu.SMEM)
    return pl.pallas_call(
        functools.partial(kernel, rows, cols, tile),
        out_shape=jax.ShapeDtypeStruct(rhs.shape, f32),
        in_specs=[vmem, smem, vmem, vmem, vmem, vmem, vmem, vmem],
        out_specs=vmem,
        scratch_shapes=[
            vm((c, 2 * c), bf16),
            vm((2, c, 2 * c), bf16),
            vm((c, 2 * c), bf16),
            vm((2, SYS, c), f32),
            vm((2, SYS, c), f32),
            vm((SYS, c), f32),
            vm((2, SYS, c), f32),
            vm((2, SYS, c), f32),
            vm((2, 2 * SYS, c // 2), bf16),
            vm((2, per, cols, 2 * SYS, c // 2), bf16),
            vm((2, cols, SYS, c + 128), f32),
            vm((2, cols - 1, SYS, c + 128), f32),
            vm((4, SYS, 128), f32),
            vm((4, rows - 1, SYS, 128), f32),
            vm((SYS, c), f32),
            vm((cols - 1, SYS, c), f32),
            dma((c // tile,)), dma((c // tile,)),
            dma((2,)), dma((2,)),
            dma((2, 2)), dma((2,)),
            dma((2, rows)), dma((2, per)),
            dma((2,)), dma((2,)),
            dma((4,)), dma((4,)),
            dma(()), dma(()),
        ],
        compiler_params=pltpu.CompilerParams(
            collective_id=0, has_side_effects=True, vmem_limit_bytes=40 * 2**20
        ),
    )(rhs, flags, near, far, basis, selft.reshape(1, -1), dinv, low)


def solution(mesh):
    placed = (
        P(None, "row"),
        P("row", "col"),
        P("row", "col", None, None),
        P("row", "col", None, None),
        P("row", None, None),
        P("row"),
        P("row", None, None),
        P("row", None, None),
    )
    return jax.shard_map(
        functools.partial(body, mesh.shape["row"], mesh.shape["col"]),
        mesh=mesh, in_specs=placed, out_specs=P(None, "row"), check_vma=False,
    )
```

```python
import functools

import jax
import jax.numpy as jnp
from jax import lax
from jax.experimental import pallas as pl
from jax.experimental.pallas import tpu as pltpu
from jax.sharding import PartitionSpec as P

epsilon = 1e-06
f32 = jnp.float32
bf16 = jnp.bfloat16
MESH = pl.DeviceIdType.MESH
SYS = 8
GROUP = 4
HOPS = (2, 0)


def stacked(x):
    high = x.astype(bf16).astype(f32)
    return jnp.concatenate([high, x - high], axis=0).astype(bf16)


def times(x, mat):
    y = jnp.dot(stacked(x), mat, preferred_element_type=f32)
    n, c = x.shape[0], mat.shape[1] // 2
    y = y[:n] + y[n:]
    return y[:, :c] + y[:, c:]


def put_split(ref, rows, m):
    c = m.shape[1]
    high = m.astype(bf16)
    ref[rows, :c] = high
    ref[rows, c:] = (m - high.astype(f32)).astype(bf16)


def total(x):
    return jnp.sum(x, axis=1, keepdims=True)


def least_squares(beta, proj_one, norm_one, cross, proj_two, norm_two):
    radius_one = jnp.sqrt(proj_one * proj_one + norm_one * norm_one)
    cos_one = proj_one / radius_one
    sin_one = norm_one / radius_one
    upper = cos_one * cross + sin_one * proj_two
    middle = cos_one * proj_two - sin_one * cross
    radius_two = jnp.sqrt(middle * middle + norm_two * norm_two)
    weight_two = -(middle / radius_two) * sin_one * beta / radius_two
    weight_one = (cos_one * beta - upper * weight_two) / radius_one
    return (weight_one, weight_two)


def kernel(
    rows, cols, tile,
    rhs_hbm, flags, near_hbm, far_hbm, basis_hbm, selft_hbm, dinv_hbm, low_hbm, out,
    rhs, near, far, basis, selft, dinv, low, load,
    rbuf, sbuf, sol, roots, s_r_send, s_r_recv, s_e_send, s_e_recv, s_p_send,
    dsp, mats, m0, crecv, csend, ebuf, prev, pcur, piece, zbuf, pbuf, part, stile, gath, fsend, fin,
    m_send, m_recv, c_send, c_recv, p_send, p_recv, z_send, z_recv, r_send, r_recv, g_send, g_recv,
    f_send, f_recv,
):
    row = lax.axis_index("row")
    col = lax.axis_index("col")
    chip = row // 2
    core = row % 2
    last = rows // 2 - 1
    per = rows // cols
    home = row // per
    c = dinv.shape[-1]
    half = c // 2
    rank = basis.shape[0]
    group = chip // GROUP
    member = chip % GROUP
    groups = rows // 2 // GROUP
    at_end = jnp.logical_and(core == 1, member == GROUP - 1)
    gives = jnp.logical_and(core == 1, member < GROUP - 1)
    solver = 2 * GROUP * group + 2 * GROUP - 1

    loads = [
        pltpu.make_async_copy(source, target, load.at[n])
        for n, (source, target) in enumerate((
            (dinv_hbm.at[0], dinv), (low_hbm.at[0], low),
            (rhs_hbm.at[pl.ds(pl.multiple_of(col * SYS, SYS), SYS)], rhs),
            (near_hbm.at[0], near), (far_hbm.at[0], far), (basis_hbm.at[0], basis), (selft_hbm, selft),
        ))
    ]
    for copy in loads:
        copy.start()

    bar = pltpu.get_barrier_semaphore()

    def tell(r, k):
        pl.semaphore_signal(bar, inc=1, device_id=(r, k), device_id_type=MESH)

    @pl.loop(1, rows)
    def _(t):
        tell(lax.rem(row + t, rows), col)

    @pl.loop(1, cols)
    def _(t):
        tell(row, lax.rem(col + t, cols))

    @pl.loop(0, rows)
    def _(t):
        r = per * col + t // cols
        k = t % cols

        @pl.when(jnp.logical_or(r != row, k != col))
        def _():
            tell(r, k)

    @pl.when(chip > 0)
    def _():
        tell(2 * chip - 1, col)

    @pl.when(core == 1)
    def _():
        tell(row - 1, col)

    @pl.when(jnp.logical_not(at_end))
    def _():
        tell(solver, col)

    @pl.when(at_end)
    def _():
        for y in range(GROUP - 1):
            tell(2 * GROUP * group + 2 * y + 1, col)

    @pl.when(jnp.logical_and(at_end, group > 0))
    def _():
        tell(solver - 2 * GROUP, col)

    expected = (rows - 1) + (cols - 1) + rows
    expected = expected - jnp.where(home == col, 1, 0)
    expected = expected + jnp.where(core == 0, 1, jnp.where(chip < last, 2, 0))
    expected = expected + jnp.where(at_end, 2 * GROUP - 1 + jnp.where(group < groups - 1, 1, 0), 0)
    expected = expected + jnp.where(gives, 1, 0)

    def spread(turn):
        @pl.loop(1, rows)
        def _(t):
            pltpu.make_async_remote_copy(
                src_ref=stile.at[turn], dst_ref=gath.at[turn, t - 1],
                send_sem=g_send.at[turn], recv_sem=g_recv.at[turn],
                device_id=(lax.rem(row + t, rows), col), device_id_type=MESH,
            ).start()

    def arrive(turn):
        pltpu.make_async_copy(gath.at[turn], gath.at[turn], g_recv.at[turn]).wait()

    loads[0].wait()

    @pl.loop(0, c // tile)
    def _(t):
        at = pl.ds(pl.multiple_of(t * tile, tile), tile)
        put_split(dsp, at, dinv[at, :])

    place = 1 - core
    loads[1].wait()

    @pl.loop(0, c // tile)
    def _(t):
        at = pl.ds(pl.multiple_of(t * tile, tile), tile)
        put_split(mats.at[place], at, times(low[at, :], dsp[...]))

    loads[2].wait()
    v = rhs[...]
    stile[0] = jnp.broadcast_to(total(v * v), (SYS, 128))
    pl.semaphore_wait(bar, expected)

    def to_sibling(t):
        at = pl.ds(pl.multiple_of(t * tile, tile), tile)
        return pltpu.make_async_remote_copy(
            src_ref=mats.at[1, at], dst_ref=m0.at[at],
            send_sem=m_send.at[t], recv_sem=m_recv.at[t],
            device_id=(row - core + 1, col), device_id_type=MESH,
        )

    @pl.when(core == 0)
    def _():
        @pl.loop(0, c // tile)
        def _(t):
            to_sibling(t).start()

    spread(0)

    @pl.when(core == 1)
    def _():
        @pl.loop(0, c // tile)
        def _(t):
            to_sibling(t).wait_recv()
            at = pl.ds(pl.multiple_of(t * tile, tile), tile)
            both = jnp.concatenate([m0[at, :c], m0[at, c:]], axis=0)
            y = jnp.dot(both, mats[0], preferred_element_type=f32)
            y = y[:tile] + y[tile:]
            put_split(mats.at[1], at, y[:, :c] + y[:, c:])

    def matrix_copy(y):
        return pltpu.make_async_remote_copy(
            src_ref=mats.at[1], dst_ref=rbuf.at[y], send_sem=s_r_send, recv_sem=s_r_recv.at[y],
            device_id=(solver, col), device_id_type=MESH,
        )

    @pl.when(jnp.logical_and(gives, group >= HOPS[0]))
    def _():
        matrix_copy(member).start()

    sign = jnp.where(core == 0, -1.0, 1.0).astype(f32)

    def c_copy(app):
        return pltpu.make_async_remote_copy(
            src_ref=csend.at[app], dst_ref=crecv.at[app],
            send_sem=c_send.at[app], recv_sem=c_recv.at[app],
            device_id=(row - core + 1, col), device_id_type=MESH,
        )

    def p_copy(app, to):
        target = 2 * chip + 2 + to if to < 2 else solver + 2 * GROUP
        return pltpu.make_async_remote_copy(
            src_ref=pcur.at[app], dst_ref=prev.at[app],
            send_sem=p_send.at[app, to], recv_sem=p_recv.at[app],
            device_id=(target, col), device_id_type=MESH,
        )

    def term_copy(app, y):
        return pltpu.make_async_remote_copy(
            src_ref=ebuf.at[app], dst_ref=sbuf.at[app, y], send_sem=s_e_send.at[app],
            recv_sem=s_e_recv.at[app, y], device_id=(solver, col), device_id_type=MESH,
        )

    def step_copies(app, y):
        return [
            pltpu.make_async_remote_copy(
                src_ref=sol.at[app, y], dst_ref=prev.at[app],
                send_sem=s_p_send.at[app, 2 * y + k], recv_sem=p_recv.at[app],
                device_id=(2 * GROUP * group + 2 * y + 2 + k, col), device_id_type=MESH,
            )
            for k in range(2 if y < GROUP - 2 else 1)
        ]

    def both_of(a, b):
        return jnp.logical_and(a, b)

    def walked(app):
        return group < HOPS[app]

    def forwards(app):
        return both_of(chip < last, both_of(core == 1, jnp.logical_or(walked(app), at_end)))

    def leaps(app):
        return both_of(forwards(app), both_of(at_end, group + 1 >= HOPS[app]))

    def chain(app, vec):
        own = times(vec, dsp[...])
        solved = jnp.logical_not(walked(app))

        @pl.when(core == 0)
        def _():
            csend[app] = own
            c_copy(app).start()
            ebuf[app] = own

        @pl.when(core == 1)
        def _():
            c_copy(app).wait_recv()
            ebuf[app] = own - times(crecv[app], mats[0])

        @pl.when(both_of(gives, solved))
        def _():
            term_copy(app, member).start()

        @pl.when(both_of(at_end, solved))
        def _():
            if app == 0:
                for y in range(GROUP - 1):
                    matrix_copy(y).wait_recv()
            else:
                @pl.when(walked(0))
                def _():
                    for y in range(GROUP - 1):
                        matrix_copy(y).wait_recv()

            for y in range(GROUP - 1):
                term_copy(app, y).wait_recv()

            @pl.when(group == 0)
            def _():
                sol[app, 0] = sbuf[app, 0]

            @pl.when(group > 0)
            def _():
                p_copy(app, 0).wait_recv()
                sol[app, 0] = sbuf[app, 0] + times(prev[app], rbuf[0])

            for y in range(GROUP - 1):
                @pl.when(group == groups - 1)
                def _():
                    for copy in step_copies(app, y):
                        copy.start()

                if y < GROUP - 2:
                    sol[app, y + 1] = sbuf[app, y + 1] + times(sol[app, y], rbuf[y + 1])
                else:
                    pcur[app] = ebuf[app] + times(sol[app, y], mats[1])

        @pl.when(jnp.logical_not(both_of(at_end, solved)))
        def _():
            @pl.when(chip == 0)
            def _():
                pcur[app] = ebuf[app]

            @pl.when(chip > 0)
            def _():
                p_copy(app, 0).wait_recv()
                pcur[app] = ebuf[app] + sign * times(prev[app], mats[1])

        @pl.when(leaps(app))
        def _():
            p_copy(app, 2).start()

        @pl.when(forwards(app))
        def _():
            p_copy(app, 1).start()
            p_copy(app, 0).start()

        @pl.when(both_of(both_of(at_end, solved), group < groups - 1))
        def _():
            for y in range(GROUP - 1):
                for copy in step_copies(app, y):
                    copy.start()

        if app == 0:
            @pl.when(both_of(gives, walked(0)))
            def _():
                matrix_copy(member).start()

    def far_row(t):
        return lax.rem(row + t + rows // 2, rows)

    def goes(t):
        return jnp.logical_or(home != col, far_row(t) != row)

    def z_copy(app, t):
        return pltpu.make_async_remote_copy(
            src_ref=piece.at[app], dst_ref=zbuf.at[app, lax.rem(row, per), col],
            send_sem=z_send.at[app, t], recv_sem=z_recv.at[app, lax.rem(row, per)],
            device_id=(far_row(t), home), device_id_type=MESH,
        )

    def r_copy(app, t):
        to = lax.rem(col + t, cols)
        return pltpu.make_async_remote_copy(
            src_ref=pbuf.at[app, to], dst_ref=part.at[app, t - 1],
            send_sem=r_send.at[app], recv_sem=r_recv.at[app],
            device_id=(row, to), device_id_type=MESH,
        )

    def apply_matrix(app, pre, meanwhile):
        piece[app] = jnp.concatenate([pre[:, :half], pre[:, half:]], axis=0).astype(bf16)

        @pl.when(home == col)
        def _():
            pltpu.make_async_copy(
                piece.at[app], zbuf.at[app, lax.rem(row, per), col], z_recv.at[app, lax.rem(row, per)]
            ).start()

        @pl.loop(0, rows)
        def _(t):
            @pl.when(goes(t))
            def _():
                z_copy(app, t).start()

        meanwhile()

        near_sum = jnp.zeros((SYS * cols, c), f32)
        far_sum = jnp.zeros((SYS * cols, rank), f32)
        for j in range(per):
            pltpu.make_async_copy(zbuf.at[app, j], zbuf.at[app, j], z_recv.at[app, j]).wait()
            z = zbuf[app, j].astype(f32)
            z = jnp.concatenate(
                [z[:, :SYS].reshape(SYS * cols, half), z[:, SYS:].reshape(SYS * cols, half)], axis=1
            )
            near_in = z * flags[0, j].astype(f32)
            far_in = (z - near_in).astype(bf16)
            near_sum += jnp.dot(near_in.astype(bf16), near[j], preferred_element_type=f32)
            far_sum += lax.dot_general(
                far_in, far[j], (((1,), (1,)), ((), ())), preferred_element_type=f32
            )
        pbuf[app, :, :, :c] = near_sum.reshape(cols, SYS, c)
        pbuf[app, :, :, c:] = jnp.concatenate(
            [far_sum, jnp.zeros((SYS * cols, 128 - rank), f32)], axis=1
        ).reshape(cols, SYS, 128)

        @pl.loop(1, cols)
        def _(t):
            r_copy(app, t).start()

        pltpu.make_async_copy(part.at[app], part.at[app], r_recv.at[app]).wait()
        both = pbuf[app, col]
        for t in range(cols - 1):
            both += part[app, t]
        far_part = jnp.dot(
            both[:, c:c + rank].astype(bf16), basis[...], preferred_element_type=f32
        )
        return selft[...] * pre + both[:, :c] + far_part

    lane = lax.broadcasted_iota(jnp.int32, (SYS, 128), 1)

    arrive(0)
    own_square = stile[0]
    squares = own_square
    for t in range(rows - 1):
        squares += gath[0, t]
    beta_tile = jnp.sqrt(squares + epsilon)
    beta = beta_tile[:, :1]
    first = v / beta
    chain(0, first)
    pre_one = pcur[0]

    def wait_loads():
        for copy in loads[3:]:
            copy.wait()
        roots[rows - 1] = jnp.sqrt(own_square) / beta_tile
        for t in range(rows - 1):
            roots[t] = jnp.sqrt(gath[0, t]) / beta_tile

    image = apply_matrix(0, pre_one, wait_loads)

    root = roots[rows - 1][:, :1]
    some = root > 1e-15
    unit_one = jnp.where(some, first / jnp.where(some, root, 1.0), 0.0)
    along = total(unit_one * image)
    left = image - along * unit_one
    rest = jnp.sqrt(total(left * left))

    def lanes(*values):
        tile = jnp.zeros((SYS, 128), f32)
        for at, value in values:
            tile = jnp.where(lane == at, value, tile)
        return tile

    stile[1] = lanes((0, total(first * image)), (1, along), (2, rest))

    @pl.when(chip > 0)
    def _():
        spread(1)

    chain(1, image)

    @pl.when(chip == 0)
    def _():
        spread(1)

    arrive(1)
    heights = stile[1]
    for t in range(rows - 1):
        heights += gath[1, t]
    proj_one = heights[:, :1]
    weight = jnp.where(lane == 1, proj_one, 0.0)
    keep = jnp.where(jnp.logical_or(lane == 1, lane == 2), 1.0, 0.0)

    def term(tile, size):
        y = (tile - weight * size) * keep
        return y * y

    squares = term(stile[1], roots[rows - 1])
    for t in range(rows - 1):
        squares += term(gath[1, t], roots[t])
    norm_one = jnp.sqrt(total(squares) + epsilon)
    second = (image - proj_one * first) / norm_one
    pre_two = (pcur[1] - proj_one * pre_one) / norm_one
    frame = []

    def local_frame():
        turn = total(unit_one * second)
        across = second - turn * unit_one
        again = total(unit_one * across)
        across = across - again * unit_one
        turn = turn + again
        size = jnp.sqrt(total(across * across))
        some = size > 1e-15
        unit_two = jnp.where(some, across / jnp.where(some, size, 1.0), 0.0)
        frame.extend((turn, size, unit_two))

    image = apply_matrix(1, pre_two, local_frame)
    turn, size, unit_two = frame
    along_one = total(unit_one * image)
    left = image - along_one * unit_one
    along_two = total(unit_two * left)
    left = left - along_two * unit_two
    stile[2] = lanes(
        (0, total(first * image)), (1, total(second * image)),
        (2, along_one), (4, along_two), (6, jnp.sqrt(total(left * left))),
        (66, turn), (68, size),
    )
    spread(2)
    arrive(2)
    heights = stile[2]
    for t in range(rows - 1):
        heights += gath[2, t]
    cross = heights[:, :1]
    proj_two = heights[:, 1:2]
    weight = jnp.where(lane == 2, cross, 0.0)
    keep = jnp.where(
        jnp.logical_or(lane == 2, jnp.logical_or(lane == 4, lane == 6)), 1.0, 0.0
    )

    def term_two(tile, size):
        y = (tile - weight * size - proj_two * pltpu.roll(tile, 64, 1)) * keep
        return y * y

    squares = term_two(stile[2], roots[rows - 1])
    for t in range(rows - 1):
        squares += term_two(gath[2, t], roots[t])
    norm_two = jnp.sqrt(total(squares) + epsilon)
    weight_one, weight_two = least_squares(beta, proj_one, norm_one, cross, proj_two, norm_two)
    answer = pre_one * weight_one + pre_two * weight_two
    fsend[...] = answer

    def f_copy(t):
        return pltpu.make_async_remote_copy(
            src_ref=fsend, dst_ref=fin.at[t - 1], send_sem=f_send, recv_sem=f_recv,
            device_id=(row, lax.rem(col + t, cols)), device_id_type=MESH,
        )

    @pl.loop(1, cols)
    def _(t):
        f_copy(t).start()

    out[pl.ds(pl.multiple_of(col * SYS, SYS), SYS), :] = answer

    @pl.when(core == 0)
    def _():
        @pl.loop(0, c // tile)
        def _(t):
            to_sibling(t).wait_send()

    @pl.when(gives)
    def _():
        matrix_copy(member).wait_send()

    for app in range(2):
        @pl.when(core == 0)
        def _():
            c_copy(app).wait_send()

        @pl.when(forwards(app))
        def _():
            p_copy(app, 0).wait_send()
            p_copy(app, 1).wait_send()

        @pl.when(leaps(app))
        def _():
            p_copy(app, 2).wait_send()

        @pl.when(both_of(gives, jnp.logical_not(walked(app))))
        def _():
            term_copy(app, member).wait_send()

        @pl.when(both_of(at_end, jnp.logical_not(walked(app))))
        def _():
            for y in range(GROUP - 1):
                for copy in step_copies(app, y):
                    copy.wait_send()

        @pl.loop(0, rows)
        def _(t):
            @pl.when(goes(t))
            def _():
                z_copy(app, t).wait_send()

        pltpu.make_async_copy(part.at[app], part.at[app], r_send.at[app]).wait()

    for n in range(3):
        pltpu.make_async_copy(gath.at[n], gath.at[n], g_send.at[n]).wait()

    pltpu.make_async_copy(fin, fin, f_recv).wait()
    for t in range(1, cols):
        at = lax.rem(col + cols - t, cols)
        out[pl.ds(pl.multiple_of(at * SYS, SYS), SYS), :] = fin[t - 1]
    pltpu.make_async_copy(fin, fin, f_send).wait()


def body(rows, cols, rhs, flags, near, far, basis, selft, dinv, low):
    c = dinv.shape[-1]
    per = rows // cols
    tile = min(128, c)
    vm = pltpu.VMEM
    dma = pltpu.SemaphoreType.DMA
    vmem = pl.BlockSpec(memory_space=pltpu.VMEM)
    smem = pl.BlockSpec(memory_space=pltpu.SMEM)
    hbm = pl.BlockSpec(memory_space=pl.ANY)
    rank = basis.shape[1]
    return pl.pallas_call(
        functools.partial(kernel, rows, cols, tile),
        out_shape=jax.ShapeDtypeStruct(rhs.shape, f32),
        in_specs=[hbm, smem] + [hbm] * 6,
        out_specs=vmem,
        scratch_shapes=[
            vm((SYS, c), f32), vm((per, c, c), bf16), vm((per, rank, c), bf16), vm((rank, c), bf16),
            vm((1, c), f32), vm((c, c), f32), vm((c, c), f32), dma((7,)),
            vm((GROUP - 1, c, 2 * c), bf16),
            vm((2, GROUP - 1, SYS, c), f32),
            vm((2, GROUP - 1, SYS, c), f32),
            vm((rows, SYS, 128), f32),
            dma(()), dma((GROUP - 1,)), dma((2,)), dma((2, GROUP - 1)), dma((2, 2 * GROUP)),
            vm((c, 2 * c), bf16),
            vm((2, c, 2 * c), bf16),
            vm((c, 2 * c), bf16),
            vm((2, SYS, c), f32),
            vm((2, SYS, c), f32),
            vm((2, SYS, c), f32),
            vm((2, SYS, c), f32),
            vm((2, SYS, c), f32),
            vm((2, 2 * SYS, c // 2), bf16),
            vm((2, per, cols, 2 * SYS, c // 2), bf16),
            vm((2, cols, SYS, c + 128), f32),
            vm((2, cols - 1, SYS, c + 128), f32),
            vm((3, SYS, 128), f32),
            vm((3, rows - 1, SYS, 128), f32),
            vm((SYS, c), f32),
            vm((cols - 1, SYS, c), f32),
            dma((c // tile,)), dma((c // tile,)),
            dma((2,)), dma((2,)),
            dma((2, 3)), dma((2,)),
            dma((2, rows)), dma((2, per)),
            dma((2,)), dma((2,)),
            dma((3,)), dma((3,)),
            dma(()), dma(()),
        ],
        compiler_params=pltpu.CompilerParams(
            collective_id=0, has_side_effects=True, vmem_limit_bytes=60 * 2**20
        ),
    )(rhs, flags, near, far, basis, selft.reshape(1, -1), dinv, low)


def solution(mesh):
    placed = (
        P(None, "row"),
        P("row", "col"),
        P("row", "col", None, None),
        P("row", "col", None, None),
        P("row", None, None),
        P("row"),
        P("row", None, None),
        P("row", None, None),
    )
    return jax.shard_map(
        functools.partial(body, mesh.shape["row"], mesh.shape["col"]),
        mesh=mesh, in_specs=placed, out_specs=P(None, "row"), check_vma=False,
    )
```

```python
import functools

import jax
import jax.numpy as jnp
from jax import lax
from jax.experimental import pallas as pl
from jax.experimental.pallas import tpu as pltpu
from jax.sharding import PartitionSpec as P

epsilon = 1e-06
f32 = jnp.float32
bf16 = jnp.bfloat16
MESH = pl.DeviceIdType.MESH
SYS = 8
GROUP = 4
HOPS = (2, 0)


def stacked(x):
    high = x.astype(bf16).astype(f32)
    return jnp.concatenate([high, x - high], axis=0).astype(bf16)


def times(x, mat):
    y = jnp.dot(stacked(x), mat, preferred_element_type=f32)
    n, c = x.shape[0], mat.shape[1] // 2
    y = y[:n] + y[n:]
    return y[:, :c] + y[:, c:]


def put_split(ref, rows, m):
    c = m.shape[1]
    high = m.astype(bf16)
    ref[rows, :c] = high
    ref[rows, c:] = (m - high.astype(f32)).astype(bf16)


def total(x):
    return jnp.sum(x, axis=1, keepdims=True)


def least_squares(beta, proj_one, norm_one, cross, proj_two, norm_two):
    radius_one = jnp.sqrt(proj_one * proj_one + norm_one * norm_one)
    cos_one = proj_one / radius_one
    sin_one = norm_one / radius_one
    upper = cos_one * cross + sin_one * proj_two
    middle = cos_one * proj_two - sin_one * cross
    radius_two = jnp.sqrt(middle * middle + norm_two * norm_two)
    weight_two = -(middle / radius_two) * sin_one * beta / radius_two
    weight_one = (cos_one * beta - upper * weight_two) / radius_one
    return (weight_one, weight_two)


def kernel(
    rows, cols, tile,
    rhs_hbm, flags, near_hbm, far_hbm, basis_hbm, selft_hbm, dinv_hbm, low_hbm, out,
    rhs, near, far, basis, selft, dinv, low, load,
    rbuf, sbuf, sol, roots, s_r_send, s_r_recv, s_e_send, s_e_recv, s_p_send,
    dsp, mats, m0, crecv, csend, ebuf, prev, pcur, piece, gbuf, zbuf, pbuf, part, stile, gath, fsend, fin,
    m_send, m_recv, c_send, c_recv, p_send, p_recv, z_send, z_recv, q_send, q_recv, x_send, x_recv, r_send, r_recv, g_send, g_recv,
    f_send, f_recv,
):
    row = lax.axis_index("row")
    col = lax.axis_index("col")
    chip = row // 2
    core = row % 2
    last = rows // 2 - 1
    per = rows // cols
    home = row // per
    c = dinv.shape[-1]
    half = c // 2
    rank = basis.shape[0]
    group = chip // GROUP
    member = chip % GROUP
    groups = rows // 2 // GROUP
    at_end = jnp.logical_and(core == 1, member == GROUP - 1)
    gives = jnp.logical_and(core == 1, member < GROUP - 1)
    solver = 2 * GROUP * group + 2 * GROUP - 1

    loads = [
        pltpu.make_async_copy(source, target, load.at[n])
        for n, (source, target) in enumerate((
            (dinv_hbm.at[0], dinv), (low_hbm.at[0], low),
            (rhs_hbm.at[pl.ds(pl.multiple_of(col * SYS, SYS), SYS)], rhs),
            (near_hbm.at[0], near), (far_hbm.at[0], far), (basis_hbm.at[0], basis), (selft_hbm, selft),
        ))
    ]
    for copy in loads:
        copy.start()

    bar = pltpu.get_barrier_semaphore()

    def tell(r, k):
        pl.semaphore_signal(bar, inc=1, device_id=(r, k), device_id_type=MESH)

    @pl.loop(1, rows)
    def _(t):
        tell(lax.rem(row + t, rows), col)

    @pl.loop(1, cols)
    def _(t):
        tell(row, lax.rem(col + t, cols))

    def spread(turn):
        @pl.loop(1, rows)
        def _(t):
            pltpu.make_async_remote_copy(
                src_ref=stile.at[turn], dst_ref=gath.at[turn, t - 1],
                send_sem=g_send.at[turn], recv_sem=g_recv.at[turn],
                device_id=(lax.rem(row + t, rows), col), device_id_type=MESH,
            ).start()

    def arrive(turn):
        pltpu.make_async_copy(gath.at[turn], gath.at[turn], g_recv.at[turn]).wait()

    loads[0].wait()

    @pl.loop(0, c // tile)
    def _(t):
        at = pl.ds(pl.multiple_of(t * tile, tile), tile)
        put_split(dsp, at, dinv[at, :])

    place = 1 - core
    loads[1].wait()

    @pl.loop(0, c // tile)
    def _(t):
        at = pl.ds(pl.multiple_of(t * tile, tile), tile)
        put_split(mats.at[place], at, times(low[at, :], dsp[...]))

    loads[2].wait()
    v = rhs[...]
    stile[0] = jnp.broadcast_to(total(v * v), (SYS, 128))
    pl.semaphore_wait(bar, rows + cols - 2)

    def to_sibling(t):
        at = pl.ds(pl.multiple_of(t * tile, tile), tile)
        return pltpu.make_async_remote_copy(
            src_ref=mats.at[1, at], dst_ref=m0.at[at],
            send_sem=m_send.at[t], recv_sem=m_recv.at[t],
            device_id=(row - core + 1, col), device_id_type=MESH,
        )

    @pl.when(core == 0)
    def _():
        @pl.loop(0, c // tile)
        def _(t):
            to_sibling(t).start()

    spread(0)

    @pl.when(core == 1)
    def _():
        @pl.loop(0, c // tile)
        def _(t):
            to_sibling(t).wait_recv()
            at = pl.ds(pl.multiple_of(t * tile, tile), tile)
            both = jnp.concatenate([m0[at, :c], m0[at, c:]], axis=0)
            y = jnp.dot(both, mats[0], preferred_element_type=f32)
            y = y[:tile] + y[tile:]
            put_split(mats.at[1], at, y[:, :c] + y[:, c:])

    def matrix_copy(y):
        return pltpu.make_async_remote_copy(
            src_ref=mats.at[1], dst_ref=rbuf.at[y], send_sem=s_r_send, recv_sem=s_r_recv.at[y],
            device_id=(solver, col), device_id_type=MESH,
        )

    @pl.when(jnp.logical_and(gives, group >= HOPS[0]))
    def _():
        matrix_copy(member).start()

    sign = jnp.where(core == 0, -1.0, 1.0).astype(f32)

    def c_copy(app):
        return pltpu.make_async_remote_copy(
            src_ref=csend.at[app], dst_ref=crecv.at[app],
            send_sem=c_send.at[app], recv_sem=c_recv.at[app],
            device_id=(row - core + 1, col), device_id_type=MESH,
        )

    def p_copy(app, to):
        target = 2 * chip + 2 + to if to < 2 else solver + 2 * GROUP
        return pltpu.make_async_remote_copy(
            src_ref=pcur.at[app], dst_ref=prev.at[app],
            send_sem=p_send.at[app, to], recv_sem=p_recv.at[app],
            device_id=(target, col), device_id_type=MESH,
        )

    def term_copy(app, y):
        return pltpu.make_async_remote_copy(
            src_ref=ebuf.at[app], dst_ref=sbuf.at[app, y], send_sem=s_e_send.at[app],
            recv_sem=s_e_recv.at[app, y], device_id=(solver, col), device_id_type=MESH,
        )

    def step_copies(app, y):
        return [
            pltpu.make_async_remote_copy(
                src_ref=sol.at[app, y], dst_ref=prev.at[app],
                send_sem=s_p_send.at[app, 2 * y + k], recv_sem=p_recv.at[app],
                device_id=(2 * GROUP * group + 2 * y + 2 + k, col), device_id_type=MESH,
            )
            for k in range(2 if y < GROUP - 2 else 1)
        ]

    def both_of(a, b):
        return jnp.logical_and(a, b)

    def walked(app):
        return group < HOPS[app]

    def forwards(app):
        return both_of(chip < last, both_of(core == 1, jnp.logical_or(walked(app), at_end)))

    def leaps(app):
        return both_of(forwards(app), both_of(at_end, group + 1 >= HOPS[app]))

    def chain(app, vec):
        own = times(vec, dsp[...])
        solved = jnp.logical_not(walked(app))

        @pl.when(core == 0)
        def _():
            csend[app] = own
            c_copy(app).start()
            ebuf[app] = own

        @pl.when(core == 1)
        def _():
            c_copy(app).wait_recv()
            ebuf[app] = own - times(crecv[app], mats[0])

        @pl.when(both_of(gives, solved))
        def _():
            term_copy(app, member).start()

        @pl.when(both_of(at_end, solved))
        def _():
            if app == 0:
                for y in range(GROUP - 1):
                    matrix_copy(y).wait_recv()
            else:
                @pl.when(walked(0))
                def _():
                    for y in range(GROUP - 1):
                        matrix_copy(y).wait_recv()

            for y in range(GROUP - 1):
                term_copy(app, y).wait_recv()

            @pl.when(group == 0)
            def _():
                sol[app, 0] = sbuf[app, 0]

            @pl.when(group > 0)
            def _():
                p_copy(app, 0).wait_recv()
                sol[app, 0] = sbuf[app, 0] + times(prev[app], rbuf[0])

            for y in range(GROUP - 1):
                @pl.when(group == groups - 1)
                def _():
                    for copy in step_copies(app, y):
                        copy.start()

                if y < GROUP - 2:
                    sol[app, y + 1] = sbuf[app, y + 1] + times(sol[app, y], rbuf[y + 1])
                else:
                    pcur[app] = ebuf[app] + times(sol[app, y], mats[1])

        @pl.when(jnp.logical_not(both_of(at_end, solved)))
        def _():
            @pl.when(chip == 0)
            def _():
                pcur[app] = ebuf[app]

            @pl.when(chip > 0)
            def _():
                p_copy(app, 0).wait_recv()
                pcur[app] = ebuf[app] + sign * times(prev[app], mats[1])

        @pl.when(leaps(app))
        def _():
            p_copy(app, 2).start()

        @pl.when(forwards(app))
        def _():
            p_copy(app, 1).start()
            p_copy(app, 0).start()

        @pl.when(both_of(both_of(at_end, solved), group < groups - 1))
        def _():
            for y in range(GROUP - 1):
                for copy in step_copies(app, y):
                    copy.start()

        if app == 0:
            @pl.when(both_of(gives, walked(0)))
            def _():
                matrix_copy(member).start()

    chips = rows // 2
    count = per // 2
    side = lax.rem(row, per) // count

    def far_row(t):
        return 2 * lax.rem(chip + t + chips // 2, chips) + side

    def piece_copy(app, t):
        return pltpu.make_async_remote_copy(
            src_ref=piece.at[app], dst_ref=gbuf.at[app, home, lax.rem(row, count)],
            send_sem=z_send.at[app, t], recv_sem=z_recv.at[app, home],
            device_id=(far_row(t), col), device_id_type=MESH,
        )

    def own_piece_copy(app):
        return pltpu.make_async_copy(
            piece.at[app], gbuf.at[app, home, lax.rem(row, count)], z_recv.at[app, home]
        )

    def plane_copy(app, k):
        return pltpu.make_async_remote_copy(
            src_ref=gbuf.at[app, k], dst_ref=zbuf.at[app, core, col],
            send_sem=q_send.at[app], recv_sem=q_recv.at[app],
            device_id=(row, k), device_id_type=MESH,
        )

    def core_copy(app):
        return pltpu.make_async_remote_copy(
            src_ref=zbuf.at[app, core], dst_ref=zbuf.at[app, core],
            send_sem=x_send.at[app], recv_sem=x_recv.at[app],
            device_id=(row + 1 - 2 * core, col), device_id_type=MESH,
        )

    def r_copy(app, t):
        to = lax.rem(col + t, cols)
        return pltpu.make_async_remote_copy(
            src_ref=pbuf.at[app, to], dst_ref=part.at[app, t - 1],
            send_sem=r_send.at[app], recv_sem=r_recv.at[app],
            device_id=(row, to), device_id_type=MESH,
        )

    def apply_matrix(app, pre, meanwhile):
        piece[app] = jnp.concatenate([pre[:, :half], pre[:, half:]], axis=0).astype(bf16)

        @pl.loop(0, chips)
        def _(t):
            @pl.when(far_row(t) != row)
            def _():
                piece_copy(app, t).start()

            @pl.when(far_row(t) == row)
            def _():
                own_piece_copy(app).start()

        meanwhile()

        @pl.loop(0, cols)
        def _(k):
            pltpu.make_async_copy(gbuf.at[app, k], gbuf.at[app, k], z_recv.at[app, k]).wait()

            @pl.when(k != col)
            def _():
                plane_copy(app, k).start()

            @pl.when(k == col)
            def _():
                pltpu.make_async_copy(gbuf.at[app, k], zbuf.at[app, core, col], q_recv.at[app]).start()

        def products(which):
            near_sum = jnp.zeros((SYS * cols, c), f32)
            far_sum = jnp.zeros((SYS * cols, rank), f32)
            for j in range(count):
                z = zbuf[app, which, :, j].astype(f32)
                z = jnp.concatenate(
                    [z[:, :SYS].reshape(SYS * cols, half), z[:, SYS:].reshape(SYS * cols, half)], axis=1
                )
                at = which * count + j
                near_in = z * flags[0, at].astype(f32)
                far_in = (z - near_in).astype(bf16)
                near_sum += jnp.dot(near_in.astype(bf16), near[at], preferred_element_type=f32)
                far_sum += lax.dot_general(
                    far_in, far[at], (((1,), (1,)), ((), ())), preferred_element_type=f32
                )
            return near_sum, far_sum

        pltpu.make_async_copy(zbuf.at[app, core], zbuf.at[app, core], q_recv.at[app]).wait()
        core_copy(app).start()
        near_sum, far_sum = products(core)
        core_copy(app).wait_recv()
        near_other, far_other = products(1 - core)
        near_sum += near_other
        far_sum += far_other
        pbuf[app, :, :, :c] = near_sum.reshape(cols, SYS, c)
        pbuf[app, :, :, c:] = jnp.concatenate(
            [far_sum, jnp.zeros((SYS * cols, 128 - rank), f32)], axis=1
        ).reshape(cols, SYS, 128)

        @pl.loop(1, cols)
        def _(t):
            r_copy(app, t).start()

        pltpu.make_async_copy(part.at[app], part.at[app], r_recv.at[app]).wait()
        both = pbuf[app, col]
        for t in range(cols - 1):
            both += part[app, t]
        far_part = jnp.dot(
            both[:, c:c + rank].astype(bf16), basis[...], preferred_element_type=f32
        )
        return selft[...] * pre + both[:, :c] + far_part

    lane = lax.broadcasted_iota(jnp.int32, (SYS, 128), 1)

    arrive(0)
    own_square = stile[0]
    squares = own_square
    for t in range(rows - 1):
        squares += gath[0, t]
    beta_tile = jnp.sqrt(squares + epsilon)
    beta = beta_tile[:, :1]
    first = v / beta
    chain(0, first)
    pre_one = pcur[0]

    def wait_loads():
        for copy in loads[3:]:
            copy.wait()
        roots[rows - 1] = jnp.sqrt(own_square) / beta_tile
        for t in range(rows - 1):
            roots[t] = jnp.sqrt(gath[0, t]) / beta_tile

    image = apply_matrix(0, pre_one, wait_loads)

    root = roots[rows - 1][:, :1]
    some = root > 1e-15
    unit_one = jnp.where(some, first / jnp.where(some, root, 1.0), 0.0)
    along = total(unit_one * image)
    left = image - along * unit_one
    rest = jnp.sqrt(total(left * left))

    def lanes(*values):
        tile = jnp.zeros((SYS, 128), f32)
        for at, value in values:
            tile = jnp.where(lane == at, value, tile)
        return tile

    stile[1] = lanes((0, total(first * image)), (1, along), (2, rest))

    @pl.when(chip > 0)
    def _():
        spread(1)

    chain(1, image)

    @pl.when(chip == 0)
    def _():
        spread(1)

    arrive(1)
    heights = stile[1]
    for t in range(rows - 1):
        heights += gath[1, t]
    proj_one = heights[:, :1]
    weight = jnp.where(lane == 1, proj_one, 0.0)
    keep = jnp.where(jnp.logical_or(lane == 1, lane == 2), 1.0, 0.0)

    def term(tile, size):
        y = (tile - weight * size) * keep
        return y * y

    squares = term(stile[1], roots[rows - 1])
    for t in range(rows - 1):
        squares += term(gath[1, t], roots[t])
    norm_one = jnp.sqrt(total(squares) + epsilon)
    second = (image - proj_one * first) / norm_one
    pre_two = (pcur[1] - proj_one * pre_one) / norm_one
    frame = []

    def local_frame():
        turn = total(unit_one * second)
        across = second - turn * unit_one
        again = total(unit_one * across)
        across = across - again * unit_one
        turn = turn + again
        size = jnp.sqrt(total(across * across))
        some = size > 1e-15
        unit_two = jnp.where(some, across / jnp.where(some, size, 1.0), 0.0)
        frame.extend((turn, size, unit_two))

    image = apply_matrix(1, pre_two, local_frame)
    turn, size, unit_two = frame
    along_one = total(unit_one * image)
    left = image - along_one * unit_one
    along_two = total(unit_two * left)
    left = left - along_two * unit_two
    stile[2] = lanes(
        (0, total(first * image)), (1, total(second * image)),
        (2, along_one), (4, along_two), (6, jnp.sqrt(total(left * left))),
        (66, turn), (68, size),
    )
    spread(2)
    arrive(2)
    heights = stile[2]
    for t in range(rows - 1):
        heights += gath[2, t]
    cross = heights[:, :1]
    proj_two = heights[:, 1:2]
    weight = jnp.where(lane == 2, cross, 0.0)
    keep = jnp.where(
        jnp.logical_or(lane == 2, jnp.logical_or(lane == 4, lane == 6)), 1.0, 0.0
    )

    def term_two(tile, size):
        y = (tile - weight * size - proj_two * pltpu.roll(tile, 64, 1)) * keep
        return y * y

    squares = term_two(stile[2], roots[rows - 1])
    for t in range(rows - 1):
        squares += term_two(gath[2, t], roots[t])
    norm_two = jnp.sqrt(total(squares) + epsilon)
    weight_one, weight_two = least_squares(beta, proj_one, norm_one, cross, proj_two, norm_two)
    answer = pre_one * weight_one + pre_two * weight_two
    fsend[...] = answer

    def f_copy(t):
        return pltpu.make_async_remote_copy(
            src_ref=fsend, dst_ref=fin.at[t - 1], send_sem=f_send, recv_sem=f_recv,
            device_id=(row, lax.rem(col + t, cols)), device_id_type=MESH,
        )

    @pl.loop(1, cols)
    def _(t):
        f_copy(t).start()

    out[pl.ds(pl.multiple_of(col * SYS, SYS), SYS), :] = answer

    @pl.when(core == 0)
    def _():
        @pl.loop(0, c // tile)
        def _(t):
            to_sibling(t).wait_send()

    @pl.when(gives)
    def _():
        matrix_copy(member).wait_send()

    for app in range(2):
        @pl.when(core == 0)
        def _():
            c_copy(app).wait_send()

        @pl.when(forwards(app))
        def _():
            p_copy(app, 0).wait_send()
            p_copy(app, 1).wait_send()

        @pl.when(leaps(app))
        def _():
            p_copy(app, 2).wait_send()

        @pl.when(both_of(gives, jnp.logical_not(walked(app))))
        def _():
            term_copy(app, member).wait_send()

        @pl.when(both_of(at_end, jnp.logical_not(walked(app))))
        def _():
            for y in range(GROUP - 1):
                for copy in step_copies(app, y):
                    copy.wait_send()

        @pl.loop(0, chips)
        def _(t):
            @pl.when(far_row(t) != row)
            def _():
                piece_copy(app, t).wait_send()

        sent = zbuf.at[app, 0, pl.ds(0, cols - 1)]
        pltpu.make_async_copy(sent, sent, q_send.at[app]).wait()
        core_copy(app).wait_send()

        pltpu.make_async_copy(part.at[app], part.at[app], r_send.at[app]).wait()

    for n in range(3):
        pltpu.make_async_copy(gath.at[n], gath.at[n], g_send.at[n]).wait()

    pltpu.make_async_copy(fin, fin, f_recv).wait()
    for t in range(1, cols):
        at = lax.rem(col + cols - t, cols)
        out[pl.ds(pl.multiple_of(at * SYS, SYS), SYS), :] = fin[t - 1]
    pltpu.make_async_copy(fin, fin, f_send).wait()


def body(rows, cols, rhs, flags, near, far, basis, selft, dinv, low):
    c = dinv.shape[-1]
    per = rows // cols
    tile = min(128, c)
    vm = pltpu.VMEM
    dma = pltpu.SemaphoreType.DMA
    vmem = pl.BlockSpec(memory_space=pltpu.VMEM)
    smem = pl.BlockSpec(memory_space=pltpu.SMEM)
    hbm = pl.BlockSpec(memory_space=pl.ANY)
    rank = basis.shape[1]
    return pl.pallas_call(
        functools.partial(kernel, rows, cols, tile),
        out_shape=jax.ShapeDtypeStruct(rhs.shape, f32),
        in_specs=[hbm, smem] + [hbm] * 6,
        out_specs=vmem,
        scratch_shapes=[
            vm((SYS, c), f32), vm((per, c, c), bf16), vm((per, rank, c), bf16), vm((rank, c), bf16),
            vm((1, c), f32), vm((c, c), f32), vm((c, c), f32), dma((7,)),
            vm((GROUP - 1, c, 2 * c), bf16),
            vm((2, GROUP - 1, SYS, c), f32),
            vm((2, GROUP - 1, SYS, c), f32),
            vm((rows, SYS, 128), f32),
            dma(()), dma((GROUP - 1,)), dma((2,)), dma((2, GROUP - 1)), dma((2, 2 * GROUP)),
            vm((c, 2 * c), bf16),
            vm((2, c, 2 * c), bf16),
            vm((c, 2 * c), bf16),
            vm((2, SYS, c), f32),
            vm((2, SYS, c), f32),
            vm((2, SYS, c), f32),
            vm((2, SYS, c), f32),
            vm((2, SYS, c), f32),
            vm((2, 2 * SYS, c // 2), bf16),
            vm((2, cols, per // 2, 2 * SYS, c // 2), bf16),
            vm((2, 2, cols, per // 2, 2 * SYS, c // 2), bf16),
            vm((2, cols, SYS, c + 128), f32),
            vm((2, cols - 1, SYS, c + 128), f32),
            vm((3, SYS, 128), f32),
            vm((3, rows - 1, SYS, 128), f32),
            vm((SYS, c), f32),
            vm((cols - 1, SYS, c), f32),
            dma((c // tile,)), dma((c // tile,)),
            dma((2,)), dma((2,)),
            dma((2, 3)), dma((2,)),
            dma((2, rows // 2)), dma((2, cols)),
            dma((2,)), dma((2,)),
            dma((2,)), dma((2,)),
            dma((2,)), dma((2,)),
            dma((3,)), dma((3,)),
            dma(()), dma(()),
        ],
        compiler_params=pltpu.CompilerParams(
            collective_id=0, has_side_effects=True, vmem_limit_bytes=60 * 2**20
        ),
    )(rhs, flags, near, far, basis, selft.reshape(1, -1), dinv, low)


def solution(mesh):
    placed = (
        P(None, "row"),
        P("row", "col"),
        P("row", "col", None, None),
        P("row", "col", None, None),
        P("row", None, None),
        P("row"),
        P("row", None, None),
        P("row", None, None),
    )
    return jax.shard_map(
        functools.partial(body, mesh.shape["row"], mesh.shape["col"]),
        mesh=mesh, in_specs=placed, out_specs=P(None, "row"), check_vma=False,
    )
```

```python
import functools

import jax
import jax.numpy as jnp
from jax import lax
from jax.experimental import pallas as pl
from jax.experimental.pallas import tpu as pltpu
from jax.sharding import PartitionSpec as P

epsilon = 1e-06
SCALE = 2.0 ** -13
f32 = jnp.float32
bf16 = jnp.bfloat16
MESH = pl.DeviceIdType.MESH
SYS = 8
GROUP = 4
HOPS = (1, 0)


def stacked(x):
    high = x.astype(bf16).astype(f32)
    return jnp.concatenate([high, x - high], axis=0).astype(bf16)


def times(x, mat):
    y = jnp.dot(stacked(x), mat, preferred_element_type=f32)
    n, c = x.shape[0], mat.shape[1] // 2
    y = y[:n] + y[n:]
    return y[:, :c] + y[:, c:]


def put_split(ref, rows, m):
    c = m.shape[1]
    high = m.astype(bf16)
    ref[rows, :c] = high
    ref[rows, c:] = (m - high.astype(f32)).astype(bf16)


def total(x):
    return jnp.sum(x, axis=1, keepdims=True)


def least_squares(beta, proj_one, norm_one, cross, proj_two, norm_two):
    radius_one = jnp.sqrt(proj_one * proj_one + norm_one * norm_one)
    cos_one = proj_one / radius_one
    sin_one = norm_one / radius_one
    upper = cos_one * cross + sin_one * proj_two
    middle = cos_one * proj_two - sin_one * cross
    radius_two = jnp.sqrt(middle * middle + norm_two * norm_two)
    weight_two = -(middle / radius_two) * sin_one * beta / radius_two
    weight_one = (cos_one * beta - upper * weight_two) / radius_one
    return (weight_one, weight_two)


def kernel(
    rows, cols, tile,
    rhs_hbm, flags, near_hbm, far_hbm, basis_hbm, selft_hbm, dinv_hbm, low_hbm, out,
    rhs, near, far, basis, selft, dinv, low, load,
    rbuf, sbuf, sol, roots, pres, blocks, s_q_send, s_q_recv, b_send, b_recv, s_r_send, s_r_recv, s_e_send, s_e_recv, s_p_send,
    dsp, mats, m0, crecv, csend, ebuf, prev, pcur, piece, gbuf, zbuf, pbuf, part, stile, gath, fsend, fin,
    m_send, m_recv, c_send, c_recv, p_send, p_recv, z_send, z_recv, q_send, q_recv, x_send, x_recv, r_send, r_recv, g_send, g_recv,
    f_send, f_recv,
):
    row = lax.axis_index("row")
    col = lax.axis_index("col")
    chip = row // 2
    core = row % 2
    last = rows // 2 - 1
    per = rows // cols
    home = row // per
    c = dinv.shape[-1]
    half = c // 2
    rank = basis.shape[0]
    group = chip // GROUP
    member = chip % GROUP
    groups = rows // 2 // GROUP
    at_end = jnp.logical_and(core == 1, member == GROUP - 1)
    gives = jnp.logical_and(core == 1, member < GROUP - 1)
    solver = 2 * GROUP * group + 2 * GROUP - 1

    loads = [
        pltpu.make_async_copy(source, target, load.at[n])
        for n, (source, target) in enumerate((
            (dinv_hbm.at[0], dinv), (low_hbm.at[0], low),
            (rhs_hbm.at[pl.ds(pl.multiple_of(col * SYS, SYS), SYS)], rhs),
            (near_hbm.at[0], near), (far_hbm.at[0], far), (basis_hbm.at[0], basis), (selft_hbm, selft),
        ))
    ]
    for copy in loads:
        copy.start()

    bar = pltpu.get_barrier_semaphore()

    def tell(r, k):
        pl.semaphore_signal(bar, inc=1, device_id=(r, k), device_id_type=MESH)

    @pl.loop(1, rows)
    def _(t):
        tell(lax.rem(row + t, rows), col)

    @pl.loop(1, cols)
    def _(t):
        tell(row, lax.rem(col + t, cols))

    def spread(turn):
        @pl.loop(1, rows)
        def _(t):
            pltpu.make_async_remote_copy(
                src_ref=stile.at[turn], dst_ref=gath.at[turn, t - 1],
                send_sem=g_send.at[turn], recv_sem=g_recv.at[turn],
                device_id=(lax.rem(row + t, rows), col), device_id_type=MESH,
            ).start()

    def arrive(turn):
        pltpu.make_async_copy(gath.at[turn], gath.at[turn], g_recv.at[turn]).wait()

    loads[0].wait()

    @pl.loop(0, c // tile)
    def _(t):
        at = pl.ds(pl.multiple_of(t * tile, tile), tile)
        put_split(dsp, at, dinv[at, :])

    place = 1 - core
    loads[1].wait()

    @pl.loop(0, c // tile)
    def _(t):
        at = pl.ds(pl.multiple_of(t * tile, tile), tile)
        put_split(mats.at[place], at, times(low[at, :], dsp[...]))

    loads[2].wait()
    v = rhs[...]
    stile[0] = jnp.broadcast_to(total(v * v), (SYS, 128))
    pl.semaphore_wait(bar, rows + cols - 2)

    def to_sibling(t):
        at = pl.ds(pl.multiple_of(t * tile, tile), tile)
        return pltpu.make_async_remote_copy(
            src_ref=mats.at[1, at], dst_ref=m0.at[at],
            send_sem=m_send.at[t], recv_sem=m_recv.at[t],
            device_id=(row - core + 1, col), device_id_type=MESH,
        )

    tiles = c // tile
    odd = lax.rem(col, 2)

    def tile_at(u):
        return lax.rem(u + odd * (tiles // 2), tiles)

    @pl.when(core == 0)
    def _():
        @pl.loop(0, tiles)
        def _(u):
            to_sibling(tile_at(u)).start()

    def half_rows(which):
        return pl.ds(pl.multiple_of(which * half, half), half)

    def matrix_copy(y):
        return pltpu.make_async_remote_copy(
            src_ref=mats.at[1, half_rows(odd)], dst_ref=rbuf.at[y, half_rows(odd)],
            send_sem=s_r_send, recv_sem=s_r_recv.at[y],
            device_id=(solver, col), device_id_type=MESH,
        )

    spread(0)

    @pl.when(core == 1)
    def _():
        @pl.loop(0, tiles)
        def _(u):
            t = tile_at(u)
            to_sibling(t).wait_recv()
            at = pl.ds(pl.multiple_of(t * tile, tile), tile)
            both = jnp.concatenate([m0[at, :c], m0[at, c:]], axis=0)
            y = jnp.dot(both, mats[0], preferred_element_type=f32)
            y = y[:tile] + y[tile:]
            put_split(mats.at[1], at, y[:, :c] + y[:, c:])

            @pl.when(jnp.logical_and(u == tiles // 2 - 1, jnp.logical_and(gives, group >= HOPS[0])))
            def _():
                matrix_copy(member).start()

    quarter = half // 2

    def quarter_rows(which, d):
        return pl.ds(pl.multiple_of(which * half + d * quarter, quarter), quarter)

    def pass_copy(y, d):
        at = quarter_rows(odd, d)
        return pltpu.make_async_remote_copy(
            src_ref=rbuf.at[y, at], dst_ref=rbuf.at[y, at], send_sem=s_q_send,
            recv_sem=s_q_recv.at[d, y],
            device_id=(row, lax.rem(col + (1 if d == 0 else cols - 1), cols)), device_id_type=MESH,
        )

    def take_matrices():
        for y in [0] + list(range(GROUP - 2, 0, -1)):
            matrix_copy(y).wait_recv()
            for d in range(2):
                pass_copy(y, d).start()
        for y in range(GROUP - 1):
            for d in range(2):
                there = rbuf.at[y, quarter_rows(1 - odd, d)]
                pltpu.make_async_copy(there, there, s_q_recv.at[d, y]).wait()

    sign = jnp.where(core == 0, -1.0, 1.0).astype(f32)

    def c_copy(app):
        return pltpu.make_async_remote_copy(
            src_ref=csend.at[app], dst_ref=crecv.at[app],
            send_sem=c_send.at[app], recv_sem=c_recv.at[app],
            device_id=(row - core + 1, col), device_id_type=MESH,
        )

    def p_copy(app, to):
        target = 2 * chip + 2 + to if to < 2 else solver + 2 * GROUP
        return pltpu.make_async_remote_copy(
            src_ref=pcur.at[app], dst_ref=prev.at[app],
            send_sem=p_send.at[app, to], recv_sem=p_recv.at[app],
            device_id=(target, col), device_id_type=MESH,
        )

    def term_copy(app, y):
        return pltpu.make_async_remote_copy(
            src_ref=ebuf.at[app], dst_ref=sbuf.at[app, y], send_sem=s_e_send.at[app],
            recv_sem=s_e_recv.at[app, y], device_id=(solver, col), device_id_type=MESH,
        )

    def step_copies(app, y):
        return [
            pltpu.make_async_remote_copy(
                src_ref=sol.at[app, y], dst_ref=prev.at[app],
                send_sem=s_p_send.at[app, 2 * y + k], recv_sem=p_recv.at[app],
                device_id=(2 * GROUP * group + 2 * y + 2 + k, col), device_id_type=MESH,
            )
            for k in range(2 if y < GROUP - 2 else 1)
        ]

    def both_of(a, b):
        return jnp.logical_and(a, b)

    def walked(app):
        return group < HOPS[app]

    def forwards(app):
        return both_of(chip < last, both_of(core == 1, jnp.logical_or(walked(app), at_end)))

    def leaps(app):
        return both_of(forwards(app), both_of(at_end, group + 1 >= HOPS[app]))

    def chain(app, vec):
        own = times(vec, dsp[...])
        solved = jnp.logical_not(walked(app))

        @pl.when(core == 0)
        def _():
            csend[app] = own
            c_copy(app).start()
            ebuf[app] = own

        @pl.when(core == 1)
        def _():
            c_copy(app).wait_recv()
            ebuf[app] = own - times(crecv[app], mats[0])

        @pl.when(both_of(gives, solved))
        def _():
            term_copy(app, member).start()

        @pl.when(both_of(at_end, solved))
        def _():
            if app == 0:
                take_matrices()

            for y in range(GROUP - 1):
                term_copy(app, y).wait_recv()

            @pl.when(group == 0)
            def _():
                sol[app, 0] = sbuf[app, 0]

            @pl.when(group > 0)
            def _():
                p_copy(app, 0).wait_recv()
                sol[app, 0] = sbuf[app, 0] + times(prev[app], rbuf[0])

            for y in range(GROUP - 1):
                @pl.when(group == groups - 1)
                def _():
                    for copy in step_copies(app, y):
                        copy.start()

                if y < GROUP - 2:
                    sol[app, y + 1] = sbuf[app, y + 1] + times(sol[app, y], rbuf[y + 1])
                else:
                    pcur[app] = ebuf[app] + times(sol[app, y], mats[1])

        @pl.when(jnp.logical_not(both_of(at_end, solved)))
        def _():
            @pl.when(chip == 0)
            def _():
                pcur[app] = ebuf[app]

            @pl.when(chip > 0)
            def _():
                p_copy(app, 0).wait_recv()
                pcur[app] = ebuf[app] + sign * times(prev[app], mats[1])

        @pl.when(leaps(app))
        def _():
            p_copy(app, 2).start()

        @pl.when(forwards(app))
        def _():
            p_copy(app, 1).start()
            p_copy(app, 0).start()

        @pl.when(both_of(both_of(at_end, solved), group < groups - 1))
        def _():
            for y in range(GROUP - 1):
                for copy in step_copies(app, y):
                    copy.start()

        if app == 0:
            @pl.when(both_of(gives, walked(0)))
            def _():
                matrix_copy(member).start()

    chips = rows // 2
    count = per // 2
    side = lax.rem(row, per) // count

    def far_row(t):
        return 2 * lax.rem(chip + t + chips // 2, chips) + side

    def piece_copy(app, t):
        return pltpu.make_async_remote_copy(
            src_ref=piece.at[app], dst_ref=gbuf.at[app, home, lax.rem(row, count)],
            send_sem=z_send.at[app, t], recv_sem=z_recv.at[app, home],
            device_id=(far_row(t), col), device_id_type=MESH,
        )

    def own_piece_copy(app):
        return pltpu.make_async_copy(
            piece.at[app], gbuf.at[app, home, lax.rem(row, count)], z_recv.at[app, home]
        )

    def plane_copy(app, k):
        return pltpu.make_async_remote_copy(
            src_ref=gbuf.at[app, k], dst_ref=zbuf.at[app, core, col],
            send_sem=q_send.at[app], recv_sem=q_recv.at[app],
            device_id=(row, k), device_id_type=MESH,
        )

    def core_copy(app):
        return pltpu.make_async_remote_copy(
            src_ref=zbuf.at[app, core], dst_ref=zbuf.at[app, core],
            send_sem=x_send.at[app], recv_sem=x_recv.at[app],
            device_id=(row + 1 - 2 * core, col), device_id_type=MESH,
        )

    def r_copy(app, t):
        to = lax.rem(col + t, cols)
        return pltpu.make_async_remote_copy(
            src_ref=pbuf.at[app, to], dst_ref=part.at[app, t - 1],
            send_sem=r_send.at[app], recv_sem=r_recv.at[app],
            device_id=(row, to), device_id_type=MESH,
        )

    def block_copy(app, t):
        return pltpu.make_async_remote_copy(
            src_ref=pres.at[app], dst_ref=blocks.at[app, t - 1],
            send_sem=b_send.at[app], recv_sem=b_recv.at[app],
            device_id=(row, lax.rem(col + t, cols)), device_id_type=MESH,
        )

    def apply_matrix(app, pre, meanwhile):
        piece[app] = jnp.concatenate([pre[:, :half], pre[:, half:]], axis=0).astype(bf16)

        @pl.loop(0, chips)
        def _(t):
            @pl.when(far_row(t) != row)
            def _():
                piece_copy(app, t).start()

            @pl.when(far_row(t) == row)
            def _():
                own_piece_copy(app).start()

        meanwhile()

        @pl.loop(0, cols)
        def _(k):
            pltpu.make_async_copy(gbuf.at[app, k], gbuf.at[app, k], z_recv.at[app, k]).wait()

            @pl.when(k != col)
            def _():
                plane_copy(app, k).start()

            @pl.when(k == col)
            def _():
                pltpu.make_async_copy(gbuf.at[app, k], zbuf.at[app, core, col], q_recv.at[app]).start()

        def products(which):
            near_sum = jnp.zeros((SYS * cols, c), f32)
            far_sum = jnp.zeros((SYS * cols, rank), f32)
            for j in range(count):
                z = zbuf[app, which, :, j].astype(f32)
                z = jnp.concatenate(
                    [z[:, :SYS].reshape(SYS * cols, half), z[:, SYS:].reshape(SYS * cols, half)], axis=1
                )
                at = which * count + j
                near_in = z * flags[0, at].astype(f32)
                far_in = (z - near_in).astype(bf16)
                near_sum += jnp.dot(near_in.astype(bf16), near[at], preferred_element_type=f32)
                far_sum += lax.dot_general(
                    far_in, far[at], (((1,), (1,)), ((), ())), preferred_element_type=f32
                )
            return near_sum, far_sum

        pltpu.make_async_copy(zbuf.at[app, core], zbuf.at[app, core], q_recv.at[app]).wait()
        core_copy(app).start()
        near_sum, far_sum = products(core)
        core_copy(app).wait_recv()
        near_other, far_other = products(1 - core)
        near_sum += near_other
        far_sum += far_other
        pbuf[app, :, :, :c] = near_sum.reshape(cols, SYS, c)
        pbuf[app, :, :, c:] = jnp.concatenate(
            [far_sum, jnp.zeros((SYS * cols, 128 - rank), f32)], axis=1
        ).reshape(cols, SYS, 128)

        @pl.loop(1, cols)
        def _(t):
            r_copy(app, t).start()

        @pl.loop(1, cols)
        def _(t):
            block_copy(app, t).start()

        pltpu.make_async_copy(part.at[app], part.at[app], r_recv.at[app]).wait()
        both = pbuf[app, col]
        for t in range(cols - 1):
            both += part[app, t]
        far_part = jnp.dot(
            both[:, c:c + rank].astype(bf16), basis[...], preferred_element_type=f32
        )
        return selft[...] * pre + both[:, :c] + far_part

    lane = lax.broadcasted_iota(jnp.int32, (SYS, 128), 1)

    chain(0, v * SCALE)
    arrive(0)
    own_square = stile[0]
    squares = own_square
    for t in range(rows - 1):
        squares += gath[0, t]
    beta_tile = jnp.sqrt(squares + epsilon)
    beta = beta_tile[:, :1]
    first = v / beta
    pre_one = pcur[0] * (1.0 / SCALE / beta)
    pres[0] = pre_one

    def wait_loads():
        for copy in loads[3:]:
            copy.wait()
        roots[rows - 1] = jnp.sqrt(own_square) / beta_tile
        for t in range(rows - 1):
            roots[t] = jnp.sqrt(gath[0, t]) / beta_tile

        @pl.when(both_of(at_end, walked(0)))
        def _():
            take_matrices()

    image = apply_matrix(0, pre_one, wait_loads)

    root = roots[rows - 1][:, :1]
    some = root > 1e-15
    unit_one = jnp.where(some, first / jnp.where(some, root, 1.0), 0.0)
    along = total(unit_one * image)
    left = image - along * unit_one
    rest = jnp.sqrt(total(left * left))

    def lanes(*values):
        tile = jnp.zeros((SYS, 128), f32)
        for at, value in values:
            tile = jnp.where(lane == at, value, tile)
        return tile

    stile[1] = lanes((0, total(first * image)), (1, along), (2, rest))

    @pl.when(chip > 0)
    def _():
        spread(1)

    chain(1, image)

    @pl.when(chip == 0)
    def _():
        spread(1)

    arrive(1)
    heights = stile[1]
    for t in range(rows - 1):
        heights += gath[1, t]
    proj_one = heights[:, :1]
    weight = jnp.where(lane == 1, proj_one, 0.0)
    keep = jnp.where(jnp.logical_or(lane == 1, lane == 2), 1.0, 0.0)

    def term(tile, size):
        y = (tile - weight * size) * keep
        return y * y

    squares = term(stile[1], roots[rows - 1])
    for t in range(rows - 1):
        squares += term(gath[1, t], roots[t])
    norm_one = jnp.sqrt(total(squares) + epsilon)
    second = (image - proj_one * first) / norm_one
    pre_two = (pcur[1] - proj_one * pre_one) / norm_one
    pres[1] = pre_two
    frame = []

    def local_frame():
        turn = total(unit_one * second)
        across = second - turn * unit_one
        again = total(unit_one * across)
        across = across - again * unit_one
        turn = turn + again
        size = jnp.sqrt(total(across * across))
        some = size > 1e-15
        unit_two = jnp.where(some, across / jnp.where(some, size, 1.0), 0.0)
        frame.extend((turn, size, unit_two))

    image = apply_matrix(1, pre_two, local_frame)
    turn, size, unit_two = frame
    along_one = total(unit_one * image)
    left = image - along_one * unit_one
    along_two = total(unit_two * left)
    left = left - along_two * unit_two
    stile[2] = lanes(
        (0, total(first * image)), (1, total(second * image)),
        (2, along_one), (4, along_two), (6, jnp.sqrt(total(left * left))),
        (66, turn), (68, size),
    )
    spread(2)
    arrive(2)
    heights = stile[2]
    for t in range(rows - 1):
        heights += gath[2, t]
    cross = heights[:, :1]
    proj_two = heights[:, 1:2]
    weight = jnp.where(lane == 2, cross, 0.0)
    keep = jnp.where(
        jnp.logical_or(lane == 2, jnp.logical_or(lane == 4, lane == 6)), 1.0, 0.0
    )

    def term_two(tile, size):
        y = (tile - weight * size - proj_two * pltpu.roll(tile, 64, 1)) * keep
        return y * y

    squares = term_two(stile[2], roots[rows - 1])
    for t in range(rows - 1):
        squares += term_two(gath[2, t], roots[t])
    norm_two = jnp.sqrt(total(squares) + epsilon)
    weight_one, weight_two = least_squares(beta, proj_one, norm_one, cross, proj_two, norm_two)
    fsend[...] = lanes((0, weight_one), (1, weight_two))

    def f_copy(t):
        return pltpu.make_async_remote_copy(
            src_ref=fsend, dst_ref=fin.at[t - 1], send_sem=f_send, recv_sem=f_recv,
            device_id=(row, lax.rem(col + t, cols)), device_id_type=MESH,
        )

    @pl.loop(1, cols)
    def _(t):
        f_copy(t).start()

    out[pl.ds(pl.multiple_of(col * SYS, SYS), SYS), :] = pre_one * weight_one + pre_two * weight_two

    @pl.when(core == 0)
    def _():
        @pl.loop(0, c // tile)
        def _(t):
            to_sibling(t).wait_send()

    @pl.when(gives)
    def _():
        matrix_copy(member).wait_send()

    @pl.when(at_end)
    def _():
        passed = rbuf.at[:, pl.ds(0, half)]
        pltpu.make_async_copy(passed, passed, s_q_send).wait()

    for app in range(2):
        @pl.when(core == 0)
        def _():
            c_copy(app).wait_send()

        @pl.when(forwards(app))
        def _():
            p_copy(app, 0).wait_send()
            p_copy(app, 1).wait_send()

        @pl.when(leaps(app))
        def _():
            p_copy(app, 2).wait_send()

        @pl.when(both_of(gives, jnp.logical_not(walked(app))))
        def _():
            term_copy(app, member).wait_send()

        @pl.when(both_of(at_end, jnp.logical_not(walked(app))))
        def _():
            for y in range(GROUP - 1):
                for copy in step_copies(app, y):
                    copy.wait_send()

        @pl.loop(0, chips)
        def _(t):
            @pl.when(far_row(t) != row)
            def _():
                piece_copy(app, t).wait_send()

        sent = zbuf.at[app, 0, pl.ds(0, cols - 1)]
        pltpu.make_async_copy(sent, sent, q_send.at[app]).wait()
        core_copy(app).wait_send()

        pltpu.make_async_copy(part.at[app], part.at[app], r_send.at[app]).wait()
        pltpu.make_async_copy(blocks.at[app], blocks.at[app], b_send.at[app]).wait()
        pltpu.make_async_copy(blocks.at[app], blocks.at[app], b_recv.at[app]).wait()

    for n in range(3):
        pltpu.make_async_copy(gath.at[n], gath.at[n], g_send.at[n]).wait()

    pltpu.make_async_copy(fin, fin, f_recv).wait()
    for t in range(1, cols):
        at = lax.rem(col + cols - t, cols)
        out[pl.ds(pl.multiple_of(at * SYS, SYS), SYS), :] = (
            blocks[0, t - 1] * fin[t - 1, :, 0:1] + blocks[1, t - 1] * fin[t - 1, :, 1:2]
        )
    pltpu.make_async_copy(fin, fin, f_send).wait()


def body(rows, cols, rhs, flags, near, far, basis, selft, dinv, low):
    c = dinv.shape[-1]
    per = rows // cols
    tile = min(128, c)
    vm = pltpu.VMEM
    dma = pltpu.SemaphoreType.DMA
    vmem = pl.BlockSpec(memory_space=pltpu.VMEM)
    smem = pl.BlockSpec(memory_space=pltpu.SMEM)
    hbm = pl.BlockSpec(memory_space=pl.ANY)
    rank = basis.shape[1]
    return pl.pallas_call(
        functools.partial(kernel, rows, cols, tile),
        out_shape=jax.ShapeDtypeStruct(rhs.shape, f32),
        in_specs=[hbm, smem] + [hbm] * 6,
        out_specs=vmem,
        scratch_shapes=[
            vm((SYS, c), f32), vm((per, c, c), bf16), vm((per, rank, c), bf16), vm((rank, c), bf16),
            vm((1, c), f32), vm((c, c), f32), vm((c, c), f32), dma((7,)),
            vm((GROUP - 1, c, 2 * c), bf16),
            vm((2, GROUP - 1, SYS, c), f32),
            vm((2, GROUP - 1, SYS, c), f32),
            vm((rows, SYS, 128), f32),
            vm((2, SYS, c), f32),
            vm((2, cols - 1, SYS, c), f32),
            dma(()), dma((2, GROUP - 1)), dma((2,)), dma((2,)),
            dma(()), dma((GROUP - 1,)), dma((2,)), dma((2, GROUP - 1)), dma((2, 2 * GROUP)),
            vm((c, 2 * c), bf16),
            vm((2, c, 2 * c), bf16),
            vm((c, 2 * c), bf16),
            vm((2, SYS, c), f32),
            vm((2, SYS, c), f32),
            vm((2, SYS, c), f32),
            vm((2, SYS, c), f32),
            vm((2, SYS, c), f32),
            vm((2, 2 * SYS, c // 2), bf16),
            vm((2, cols, per // 2, 2 * SYS, c // 2), bf16),
            vm((2, 2, cols, per // 2, 2 * SYS, c // 2), bf16),
            vm((2, cols, SYS, c + 128), f32),
            vm((2, cols - 1, SYS, c + 128), f32),
            vm((3, SYS, 128), f32),
            vm((3, rows - 1, SYS, 128), f32),
            vm((SYS, 128), f32),
            vm((cols - 1, SYS, 128), f32),
            dma((c // tile,)), dma((c // tile,)),
            dma((2,)), dma((2,)),
            dma((2, 3)), dma((2,)),
            dma((2, rows // 2)), dma((2, cols)),
            dma((2,)), dma((2,)),
            dma((2,)), dma((2,)),
            dma((2,)), dma((2,)),
            dma((3,)), dma((3,)),
            dma(()), dma(()),
        ],
        compiler_params=pltpu.CompilerParams(
            collective_id=0, has_side_effects=True, vmem_limit_bytes=60 * 2**20
        ),
    )(rhs, flags, near, far, basis, selft.reshape(1, -1), dinv, low)


def solution(mesh):
    placed = (
        P(None, "row"),
        P("row", "col"),
        P("row", "col", None, None),
        P("row", "col", None, None),
        P("row", None, None),
        P("row"),
        P("row", None, None),
        P("row", None, None),
    )
    return jax.shard_map(
        functools.partial(body, mesh.shape["row"], mesh.shape["col"]),
        mesh=mesh, in_specs=placed, out_specs=P(None, "row"), check_vma=False,
    )
```

```python
import functools

import jax
import jax.numpy as jnp
from jax import lax
from jax.experimental import pallas as pl
from jax.experimental.pallas import tpu as pltpu
from jax.sharding import PartitionSpec as P

epsilon = 1e-06
SCALE = 2.0 ** -13
f32 = jnp.float32
bf16 = jnp.bfloat16
MESH = pl.DeviceIdType.MESH
SYS = 8
GROUP = 4
HOPS = (2, 0)


def stacked(x):
    high = x.astype(bf16).astype(f32)
    return jnp.concatenate([high, x - high], axis=0).astype(bf16)


def times(x, mat):
    y = jnp.dot(stacked(x), mat, preferred_element_type=f32)
    n, c = x.shape[0], mat.shape[1] // 2
    y = y[:n] + y[n:]
    return y[:, :c] + y[:, c:]


def put_split(ref, rows, m):
    c = m.shape[1]
    high = m.astype(bf16)
    ref[rows, :c] = high
    ref[rows, c:] = (m - high.astype(f32)).astype(bf16)


def total(x):
    return jnp.sum(x, axis=1, keepdims=True)


def least_squares(beta, proj_one, norm_one, cross, proj_two, norm_two):
    radius_one = jnp.sqrt(proj_one * proj_one + norm_one * norm_one)
    cos_one = proj_one / radius_one
    sin_one = norm_one / radius_one
    upper = cos_one * cross + sin_one * proj_two
    middle = cos_one * proj_two - sin_one * cross
    radius_two = jnp.sqrt(middle * middle + norm_two * norm_two)
    weight_two = -(middle / radius_two) * sin_one * beta / radius_two
    weight_one = (cos_one * beta - upper * weight_two) / radius_one
    return (weight_one, weight_two)


def kernel(
    rows, cols, tile,
    rhs_hbm, flags, near_hbm, far_hbm, basis_hbm, selft_hbm, dinv_hbm, low_hbm, out,
    rhs, near, far, basis, selft, dinv, low, load,
    rbuf, sbuf, sol, roots, pres, blocks, s_q_send, s_q_recv, b_send, b_recv, s_r_send, s_r_recv, s_e_send, s_e_recv, s_p_send,
    dsp, mats, m0, crecv, csend, ebuf, prev, pcur, piece, gbuf, zbuf, pbuf, part, stile, gath, fsend, fin,
    m_send, m_recv, c_send, c_recv, p_send, p_recv, z_send, z_recv, q_send, q_recv, x_send, x_recv, r_send, r_recv, g_send, g_recv,
    f_send, f_recv,
):
    row = lax.axis_index("row")
    col = lax.axis_index("col")
    chip = row // 2
    core = row % 2
    last = rows // 2 - 1
    per = rows // cols
    home = row // per
    c = dinv.shape[-1]
    half = c // 2
    rank = basis.shape[0]
    group = chip // GROUP
    member = chip % GROUP
    groups = rows // 2 // GROUP
    at_end = jnp.logical_and(core == 1, member == GROUP - 1)
    gives = jnp.logical_and(core == 1, member < GROUP - 1)
    solver = 2 * GROUP * group + 2 * GROUP - 1

    loads = [
        pltpu.make_async_copy(source, target, load.at[n])
        for n, (source, target) in enumerate((
            (dinv_hbm.at[0], dinv), (low_hbm.at[0], low),
            (rhs_hbm.at[pl.ds(pl.multiple_of(col * SYS, SYS), SYS)], rhs),
            (near_hbm.at[0], near), (far_hbm.at[0], far), (basis_hbm.at[0], basis), (selft_hbm, selft),
        ))
    ]
    for copy in loads:
        copy.start()

    bar = pltpu.get_barrier_semaphore()

    def tell(r, k):
        pl.semaphore_signal(bar, inc=1, device_id=(r, k), device_id_type=MESH)

    @pl.loop(1, rows)
    def _(t):
        tell(lax.rem(row + t, rows), col)

    @pl.loop(1, cols)
    def _(t):
        tell(row, lax.rem(col + t, cols))

    def spread(turn):
        @pl.loop(1, rows)
        def _(t):
            pltpu.make_async_remote_copy(
                src_ref=stile.at[turn], dst_ref=gath.at[turn, t - 1],
                send_sem=g_send.at[turn], recv_sem=g_recv.at[turn],
                device_id=(lax.rem(row + t, rows), col), device_id_type=MESH,
            ).start()

    def arrive(turn):
        pltpu.make_async_copy(gath.at[turn], gath.at[turn], g_recv.at[turn]).wait()

    loads[0].wait()

    @pl.loop(0, c // tile)
    def _(t):
        at = pl.ds(pl.multiple_of(t * tile, tile), tile)
        put_split(dsp, at, dinv[at, :])

    place = 1 - core
    loads[1].wait()

    @pl.loop(0, c // tile)
    def _(t):
        at = pl.ds(pl.multiple_of(t * tile, tile), tile)
        put_split(mats.at[place], at, times(low[at, :], dsp[...]))

    loads[2].wait()
    v = rhs[...]
    stile[0] = jnp.broadcast_to(total(v * v), (SYS, 128))
    pl.semaphore_wait(bar, rows + cols - 2)

    def to_sibling(t):
        at = pl.ds(pl.multiple_of(t * tile, tile), tile)
        return pltpu.make_async_remote_copy(
            src_ref=mats.at[1, at], dst_ref=m0.at[at],
            send_sem=m_send.at[t], recv_sem=m_recv.at[t],
            device_id=(row - core + 1, col), device_id_type=MESH,
        )

    tiles = c // tile
    odd = lax.rem(col, 2)

    def tile_at(u):
        return lax.rem(u + odd * (tiles // 2), tiles)

    def offer():
        @pl.loop(0, tiles)
        def _(u):
            to_sibling(tile_at(u)).start()

    direct = group == 0
    late = chip < GROUP // 2

    @pl.when(jnp.logical_and(core == 0, jnp.logical_not(late)))
    def _():
        offer()

    def half_rows(which):
        return pl.ds(pl.multiple_of(which * half, half), half)

    def matrix_copy(y):
        return pltpu.make_async_remote_copy(
            src_ref=mats.at[1, half_rows(odd)], dst_ref=rbuf.at[y, half_rows(odd)],
            send_sem=s_r_send, recv_sem=s_r_recv.at[y],
            device_id=(solver, col), device_id_type=MESH,
        )

    def form_pair():
        @pl.loop(0, tiles)
        def _(u):
            t = tile_at(u)
            to_sibling(t).wait_recv()
            at = pl.ds(pl.multiple_of(t * tile, tile), tile)
            both = jnp.concatenate([m0[at, :c], m0[at, c:]], axis=0)
            y = jnp.dot(both, mats[0], preferred_element_type=f32)
            y = y[:tile] + y[tile:]
            put_split(mats.at[1], at, y[:, :c] + y[:, c:])

            @pl.when(jnp.logical_and(u == tiles // 2 - 1, jnp.logical_and(gives, group > 0)))
            def _():
                matrix_copy(member).start()

    @pl.when(jnp.logical_and(core == 1, jnp.logical_not(late)))
    def _():
        form_pair()

    quarter = half // 2

    def quarter_rows(which, d):
        return pl.ds(pl.multiple_of(which * half + d * quarter, quarter), quarter)

    def pass_copy(y, d):
        at = quarter_rows(odd, d)
        return pltpu.make_async_remote_copy(
            src_ref=rbuf.at[y, at], dst_ref=rbuf.at[y, at], send_sem=s_q_send,
            recv_sem=s_q_recv.at[d, y],
            device_id=(row, lax.rem(col + (1 if d == 0 else cols - 1), cols)), device_id_type=MESH,
        )

    def take_matrices():
        for y in [0] + list(range(GROUP - 2, 0, -1)):
            matrix_copy(y).wait_recv()
            for d in range(2):
                pass_copy(y, d).start()
        for y in range(GROUP - 1):
            for d in range(2):
                there = rbuf.at[y, quarter_rows(1 - odd, d)]
                pltpu.make_async_copy(there, there, s_q_recv.at[d, y]).wait()

    sign = jnp.where(core == 0, -1.0, 1.0).astype(f32)

    def c_copy(app):
        return pltpu.make_async_remote_copy(
            src_ref=csend.at[app], dst_ref=crecv.at[app],
            send_sem=c_send.at[app], recv_sem=c_recv.at[app],
            device_id=(row - core + 1, col), device_id_type=MESH,
        )

    def p_copy(app, to):
        target = 2 * chip + 2 + to if to < 2 else solver + 2 * GROUP
        return pltpu.make_async_remote_copy(
            src_ref=pcur.at[app], dst_ref=prev.at[app],
            send_sem=p_send.at[app, to], recv_sem=p_recv.at[app],
            device_id=(target, col), device_id_type=MESH,
        )

    def term_copy(app, y):
        return pltpu.make_async_remote_copy(
            src_ref=ebuf.at[app], dst_ref=sbuf.at[app, y], send_sem=s_e_send.at[app],
            recv_sem=s_e_recv.at[app, y], device_id=(solver, col), device_id_type=MESH,
        )

    def step_copies(app, y):
        return [
            pltpu.make_async_remote_copy(
                src_ref=sol.at[app, y], dst_ref=prev.at[app],
                send_sem=s_p_send.at[app, 2 * y + k], recv_sem=p_recv.at[app],
                device_id=(2 * GROUP * group + 2 * y + 2 + k, col), device_id_type=MESH,
            )
            for k in range(2 if y < GROUP - 2 else 1)
        ]

    def both_of(a, b):
        return jnp.logical_and(a, b)

    def walked(app):
        return group < HOPS[app]

    def forwards(app):
        return both_of(chip < last, both_of(core == 1, jnp.logical_or(walked(app), at_end)))

    def forwards_to_one(app):
        return both_of(forwards(app), chip >= GROUP - 1) if app == 0 else forwards(app)

    def leaps(app):
        return both_of(forwards(app), both_of(at_end, group + 1 >= HOPS[app]))

    def chain(app, vec, between):
        own = times(vec, dsp[...])
        solved = jnp.logical_not(walked(app))

        @pl.when(core == 0)
        def _():
            csend[app] = own

            if app == 0:
                @pl.when(both_of(direct, chip > 0))
                def _():
                    p_copy(app, 0).wait_recv()
                    csend[app] = own - times(prev[app], mats[1])

            c_copy(app).start()
            ebuf[app] = csend[app]

        @pl.when(core == 1)
        def _():
            c_copy(app).wait_recv()
            ebuf[app] = own - times(crecv[app], mats[0])

        @pl.when(both_of(gives, solved))
        def _():
            term_copy(app, member).start()

        between()

        @pl.when(both_of(at_end, solved))
        def _():
            if app == 0:
                take_matrices()

            for y in range(GROUP - 1):
                term_copy(app, y).wait_recv()

            @pl.when(group == 0)
            def _():
                sol[app, 0] = sbuf[app, 0]

            @pl.when(group > 0)
            def _():
                p_copy(app, 0).wait_recv()
                sol[app, 0] = sbuf[app, 0] + times(prev[app], rbuf[0])

            for y in range(GROUP - 1):
                @pl.when(group == groups - 1)
                def _():
                    for copy in step_copies(app, y):
                        copy.start()

                if y < GROUP - 2:
                    sol[app, y + 1] = sbuf[app, y + 1] + times(sol[app, y], rbuf[y + 1])
                else:
                    pcur[app] = ebuf[app] + times(sol[app, y], mats[1])

        @pl.when(jnp.logical_not(both_of(at_end, solved)))
        def _():
            ready = direct if app == 0 else chip == 0

            @pl.when(ready)
            def _():
                pcur[app] = ebuf[app]

            @pl.when(jnp.logical_not(ready))
            def _():
                p_copy(app, 0).wait_recv()
                pcur[app] = ebuf[app] + sign * times(prev[app], mats[1])

        @pl.when(leaps(app))
        def _():
            p_copy(app, 2).start()

        @pl.when(forwards_to_one(app))
        def _():
            p_copy(app, 1).start()

        @pl.when(forwards(app))
        def _():
            p_copy(app, 0).start()

        @pl.when(both_of(both_of(at_end, solved), group < groups - 1))
        def _():
            for y in range(GROUP - 1):
                for copy in step_copies(app, y):
                    copy.start()

    chips = rows // 2
    count = per // 2
    side = lax.rem(row, per) // count

    def far_row(t):
        return 2 * lax.rem(chip + t + chips // 2, chips) + side

    def piece_copy(app, t):
        return pltpu.make_async_remote_copy(
            src_ref=piece.at[app], dst_ref=gbuf.at[app, home, lax.rem(row, count)],
            send_sem=z_send.at[app, t], recv_sem=z_recv.at[app, home],
            device_id=(far_row(t), col), device_id_type=MESH,
        )

    def own_piece_copy(app):
        return pltpu.make_async_copy(
            piece.at[app], gbuf.at[app, home, lax.rem(row, count)], z_recv.at[app, home]
        )

    def plane_copy(app, k):
        return pltpu.make_async_remote_copy(
            src_ref=gbuf.at[app, k], dst_ref=zbuf.at[app, core, col],
            send_sem=q_send.at[app], recv_sem=q_recv.at[app],
            device_id=(row, k), device_id_type=MESH,
        )

    def core_copy(app):
        return pltpu.make_async_remote_copy(
            src_ref=zbuf.at[app, core], dst_ref=zbuf.at[app, core],
            send_sem=x_send.at[app], recv_sem=x_recv.at[app],
            device_id=(row + 1 - 2 * core, col), device_id_type=MESH,
        )

    def r_copy(app, t):
        to = lax.rem(col + t, cols)
        return pltpu.make_async_remote_copy(
            src_ref=pbuf.at[app, to], dst_ref=part.at[app, t - 1],
            send_sem=r_send.at[app], recv_sem=r_recv.at[app],
            device_id=(row, to), device_id_type=MESH,
        )

    def send_blocks(app):
        @pl.loop(1, cols)
        def _(t):
            pltpu.make_async_remote_copy(
                src_ref=pres.at[app], dst_ref=blocks.at[app, t - 1],
                send_sem=b_send.at[app], recv_sem=b_recv.at[app],
                device_id=(row, lax.rem(col + t, cols)), device_id_type=MESH,
            ).start()

    def apply_matrix(app, pre, meanwhile):
        piece[app] = jnp.concatenate([pre[:, :half], pre[:, half:]], axis=0).astype(bf16)

        @pl.loop(0, chips)
        def _(t):
            @pl.when(far_row(t) != row)
            def _():
                piece_copy(app, t).start()

            @pl.when(far_row(t) == row)
            def _():
                own_piece_copy(app).start()

        meanwhile()

        @pl.loop(0, cols)
        def _(k):
            pltpu.make_async_copy(gbuf.at[app, k], gbuf.at[app, k], z_recv.at[app, k]).wait()

            @pl.when(k != col)
            def _():
                plane_copy(app, k).start()

            @pl.when(k == col)
            def _():
                pltpu.make_async_copy(gbuf.at[app, k], zbuf.at[app, core, col], q_recv.at[app]).start()

        def products(which):
            near_sum = jnp.zeros((SYS * cols, c), f32)
            far_sum = jnp.zeros((SYS * cols, rank), f32)
            for j in range(count):
                z = zbuf[app, which, :, j].astype(f32)
                z = jnp.concatenate(
                    [z[:, :SYS].reshape(SYS * cols, half), z[:, SYS:].reshape(SYS * cols, half)], axis=1
                )
                at = which * count + j
                near_in = z * flags[0, at].astype(f32)
                far_in = (z - near_in).astype(bf16)
                near_sum += jnp.dot(near_in.astype(bf16), near[at], preferred_element_type=f32)
                far_sum += lax.dot_general(
                    far_in, far[at], (((1,), (1,)), ((), ())), preferred_element_type=f32
                )
            return near_sum, far_sum

        pltpu.make_async_copy(zbuf.at[app, core], zbuf.at[app, core], q_recv.at[app]).wait()
        core_copy(app).start()
        near_sum, far_sum = products(core)
        core_copy(app).wait_recv()
        near_other, far_other = products(1 - core)
        near_sum += near_other
        far_sum += far_other
        pbuf[app, :, :, :c] = near_sum.reshape(cols, SYS, c)
        pbuf[app, :, :, c:] = jnp.concatenate(
            [far_sum, jnp.zeros((SYS * cols, 128 - rank), f32)], axis=1
        ).reshape(cols, SYS, 128)

        @pl.loop(1, cols)
        def _(t):
            r_copy(app, t).start()

        pltpu.make_async_copy(part.at[app], part.at[app], r_recv.at[app]).wait()
        both = pbuf[app, col]
        for t in range(cols - 1):
            both += part[app, t]
        far_part = jnp.dot(
            both[:, c:c + rank].astype(bf16), basis[...], preferred_element_type=f32
        )
        return selft[...] * pre + both[:, :c] + far_part

    lane = lax.broadcasted_iota(jnp.int32, (SYS, 128), 1)

    def spread_squares():
        @pl.when(group > 0)
        def _():
            spread(0)

    chain(0, v * SCALE, spread_squares)

    @pl.when(group == 0)
    def _():
        spread(0)


    @pl.when(both_of(late, core == 0))
    def _():
        offer()

    @pl.when(both_of(late, core == 1))
    def _():
        form_pair()

    @pl.when(both_of(gives, direct))
    def _():
        matrix_copy(member).start()

    arrive(0)
    own_square = stile[0]
    squares = own_square
    for t in range(rows - 1):
        squares += gath[0, t]
    beta_tile = jnp.sqrt(squares + epsilon)
    beta = beta_tile[:, :1]
    first = v / beta
    pre_one = pcur[0] * (1.0 / SCALE / beta)
    pres[0] = pre_one

    def wait_loads():
        for copy in loads[3:]:
            copy.wait()
        roots[rows - 1] = jnp.sqrt(own_square) / beta_tile
        for t in range(rows - 1):
            roots[t] = jnp.sqrt(gath[0, t]) / beta_tile

        @pl.when(both_of(at_end, walked(0)))
        def _():
            take_matrices()

    image = apply_matrix(0, pre_one, wait_loads)

    root = roots[rows - 1][:, :1]
    some = root > 1e-15
    unit_one = jnp.where(some, first / jnp.where(some, root, 1.0), 0.0)
    along = total(unit_one * image)
    left = image - along * unit_one
    rest = jnp.sqrt(total(left * left))

    def lanes(*values):
        tile = jnp.zeros((SYS, 128), f32)
        for at, value in values:
            tile = jnp.where(lane == at, value, tile)
        return tile

    stile[1] = lanes((0, total(first * image)), (1, along), (2, rest))

    first_solver = both_of(at_end, group == 0)

    def spread_heights():
        @pl.when(jnp.logical_not(first_solver))
        def _():
            spread(1)
            send_blocks(0)

    chain(1, image, spread_heights)

    @pl.when(first_solver)
    def _():
        spread(1)
        send_blocks(0)

    arrive(1)
    heights = stile[1]
    for t in range(rows - 1):
        heights += gath[1, t]
    proj_one = heights[:, :1]
    weight = jnp.where(lane == 1, proj_one, 0.0)
    keep = jnp.where(jnp.logical_or(lane == 1, lane == 2), 1.0, 0.0)

    def term(tile, size):
        y = (tile - weight * size) * keep
        return y * y

    squares = term(stile[1], roots[rows - 1])
    for t in range(rows - 1):
        squares += term(gath[1, t], roots[t])
    norm_one = jnp.sqrt(total(squares) + epsilon)
    second = (image - proj_one * first) / norm_one
    pre_two = (pcur[1] - proj_one * pre_one) / norm_one
    pres[1] = pre_two
    frame = []

    def local_frame():
        turn = total(unit_one * second)
        across = second - turn * unit_one
        again = total(unit_one * across)
        across = across - again * unit_one
        turn = turn + again
        size = jnp.sqrt(total(across * across))
        some = size > 1e-15
        unit_two = jnp.where(some, across / jnp.where(some, size, 1.0), 0.0)
        frame.extend((turn, size, unit_two))

    image = apply_matrix(1, pre_two, local_frame)
    turn, size, unit_two = frame
    along_one = total(unit_one * image)
    left = image - along_one * unit_one
    along_two = total(unit_two * left)
    left = left - along_two * unit_two
    stile[2] = lanes(
        (0, total(first * image)), (1, total(second * image)),
        (2, along_one), (4, along_two), (6, jnp.sqrt(total(left * left))),
        (66, turn), (68, size),
    )
    spread(2)
    send_blocks(1)
    arrive(2)
    heights = stile[2]
    for t in range(rows - 1):
        heights += gath[2, t]
    cross = heights[:, :1]
    proj_two = heights[:, 1:2]
    weight = jnp.where(lane == 2, cross, 0.0)
    keep = jnp.where(
        jnp.logical_or(lane == 2, jnp.logical_or(lane == 4, lane == 6)), 1.0, 0.0
    )

    def term_two(tile, size):
        y = (tile - weight * size - proj_two * pltpu.roll(tile, 64, 1)) * keep
        return y * y

    squares = term_two(stile[2], roots[rows - 1])
    for t in range(rows - 1):
        squares += term_two(gath[2, t], roots[t])
    norm_two = jnp.sqrt(total(squares) + epsilon)
    weight_one, weight_two = least_squares(beta, proj_one, norm_one, cross, proj_two, norm_two)
    fsend[...] = lanes((0, weight_one), (1, weight_two))

    def f_copy(t):
        return pltpu.make_async_remote_copy(
            src_ref=fsend, dst_ref=fin.at[t - 1], send_sem=f_send, recv_sem=f_recv,
            device_id=(row, lax.rem(col + t, cols)), device_id_type=MESH,
        )

    @pl.loop(1, cols)
    def _(t):
        f_copy(t).start()

    out[pl.ds(pl.multiple_of(col * SYS, SYS), SYS), :] = pre_one * weight_one + pre_two * weight_two

    @pl.when(core == 0)
    def _():
        @pl.loop(0, c // tile)
        def _(t):
            to_sibling(t).wait_send()

    @pl.when(gives)
    def _():
        matrix_copy(member).wait_send()

    @pl.when(at_end)
    def _():
        passed = rbuf.at[:, pl.ds(0, half)]
        pltpu.make_async_copy(passed, passed, s_q_send).wait()

    for app in range(2):
        @pl.when(core == 0)
        def _():
            c_copy(app).wait_send()

        @pl.when(forwards(app))
        def _():
            p_copy(app, 0).wait_send()

        @pl.when(forwards_to_one(app))
        def _():
            p_copy(app, 1).wait_send()

        @pl.when(leaps(app))
        def _():
            p_copy(app, 2).wait_send()

        @pl.when(both_of(gives, jnp.logical_not(walked(app))))
        def _():
            term_copy(app, member).wait_send()

        @pl.when(both_of(at_end, jnp.logical_not(walked(app))))
        def _():
            for y in range(GROUP - 1):
                for copy in step_copies(app, y):
                    copy.wait_send()

        @pl.loop(0, chips)
        def _(t):
            @pl.when(far_row(t) != row)
            def _():
                piece_copy(app, t).wait_send()

        sent = zbuf.at[app, 0, pl.ds(0, cols - 1)]
        pltpu.make_async_copy(sent, sent, q_send.at[app]).wait()
        core_copy(app).wait_send()

        pltpu.make_async_copy(part.at[app], part.at[app], r_send.at[app]).wait()
        pltpu.make_async_copy(blocks.at[app], blocks.at[app], b_send.at[app]).wait()
        pltpu.make_async_copy(blocks.at[app], blocks.at[app], b_recv.at[app]).wait()

    for n in range(3):
        pltpu.make_async_copy(gath.at[n], gath.at[n], g_send.at[n]).wait()

    pltpu.make_async_copy(fin, fin, f_recv).wait()
    for t in range(1, cols):
        at = lax.rem(col + cols - t, cols)
        out[pl.ds(pl.multiple_of(at * SYS, SYS), SYS), :] = (
            blocks[0, t - 1] * fin[t - 1, :, 0:1] + blocks[1, t - 1] * fin[t - 1, :, 1:2]
        )
    pltpu.make_async_copy(fin, fin, f_send).wait()


def body(rows, cols, rhs, flags, near, far, basis, selft, dinv, low):
    c = dinv.shape[-1]
    per = rows // cols
    tile = min(128, c)
    vm = pltpu.VMEM
    dma = pltpu.SemaphoreType.DMA
    vmem = pl.BlockSpec(memory_space=pltpu.VMEM)
    smem = pl.BlockSpec(memory_space=pltpu.SMEM)
    hbm = pl.BlockSpec(memory_space=pl.ANY)
    rank = basis.shape[1]
    return pl.pallas_call(
        functools.partial(kernel, rows, cols, tile),
        out_shape=jax.ShapeDtypeStruct(rhs.shape, f32),
        in_specs=[hbm, smem] + [hbm] * 6,
        out_specs=vmem,
        scratch_shapes=[
            vm((SYS, c), f32), vm((per, c, c), bf16), vm((per, rank, c), bf16), vm((rank, c), bf16),
            vm((1, c), f32), vm((c, c), f32), vm((c, c), f32), dma((7,)),
            vm((GROUP - 1, c, 2 * c), bf16),
            vm((2, GROUP - 1, SYS, c), f32),
            vm((2, GROUP - 1, SYS, c), f32),
            vm((rows, SYS, 128), f32),
            vm((2, SYS, c), f32),
            vm((2, cols - 1, SYS, c), f32),
            dma(()), dma((2, GROUP - 1)), dma((2,)), dma((2,)),
            dma(()), dma((GROUP - 1,)), dma((2,)), dma((2, GROUP - 1)), dma((2, 2 * GROUP)),
            vm((c, 2 * c), bf16),
            vm((2, c, 2 * c), bf16),
            vm((c, 2 * c), bf16),
            vm((2, SYS, c), f32),
            vm((2, SYS, c), f32),
            vm((2, SYS, c), f32),
            vm((2, SYS, c), f32),
            vm((2, SYS, c), f32),
            vm((2, 2 * SYS, c // 2), bf16),
            vm((2, cols, per // 2, 2 * SYS, c // 2), bf16),
            vm((2, 2, cols, per // 2, 2 * SYS, c // 2), bf16),
            vm((2, cols, SYS, c + 128), f32),
            vm((2, cols - 1, SYS, c + 128), f32),
            vm((3, SYS, 128), f32),
            vm((3, rows - 1, SYS, 128), f32),
            vm((SYS, 128), f32),
            vm((cols - 1, SYS, 128), f32),
            dma((c // tile,)), dma((c // tile,)),
            dma((2,)), dma((2,)),
            dma((2, 3)), dma((2,)),
            dma((2, rows // 2)), dma((2, cols)),
            dma((2,)), dma((2,)),
            dma((2,)), dma((2,)),
            dma((2,)), dma((2,)),
            dma((3,)), dma((3,)),
            dma(()), dma(()),
        ],
        compiler_params=pltpu.CompilerParams(
            collective_id=0, has_side_effects=True, vmem_limit_bytes=60 * 2**20
        ),
    )(rhs, flags, near, far, basis, selft.reshape(1, -1), dinv, low)


def solution(mesh):
    placed = (
        P(None, "row"),
        P("row", "col"),
        P("row", "col", None, None),
        P("row", "col", None, None),
        P("row", None, None),
        P("row"),
        P("row", None, None),
        P("row", None, None),
    )
    return jax.shard_map(
        functools.partial(body, mesh.shape["row"], mesh.shape["col"]),
        mesh=mesh, in_specs=placed, out_specs=P(None, "row"), check_vma=False,
    )
```

```python
import functools

import jax
import jax.numpy as jnp
from jax import lax
from jax.experimental import pallas as pl
from jax.experimental.pallas import tpu as pltpu
from jax.sharding import PartitionSpec as P

epsilon = 1e-06
SCALE = 2.0 ** -13
f32 = jnp.float32
bf16 = jnp.bfloat16
MESH = pl.DeviceIdType.MESH
SYS = 8
GROUP = 4
HOPS = (2, 0)


def stacked(x):
    high = x.astype(bf16).astype(f32)
    return jnp.concatenate([high, x - high], axis=0).astype(bf16)


def times(x, mat):
    y = jnp.dot(stacked(x), mat, preferred_element_type=f32)
    n, c = x.shape[0], mat.shape[1] // 2
    y = y[:n] + y[n:]
    return y[:, :c] + y[:, c:]


def put_split(ref, rows, m):
    c = m.shape[1]
    high = m.astype(bf16)
    ref[rows, :c] = high
    ref[rows, c:] = (m - high.astype(f32)).astype(bf16)


def total(x):
    return jnp.sum(x, axis=1, keepdims=True)


def least_squares(beta, proj_one, norm_one, cross, proj_two, norm_two):
    radius_one = jnp.sqrt(proj_one * proj_one + norm_one * norm_one)
    cos_one = proj_one / radius_one
    sin_one = norm_one / radius_one
    upper = cos_one * cross + sin_one * proj_two
    middle = cos_one * proj_two - sin_one * cross
    radius_two = jnp.sqrt(middle * middle + norm_two * norm_two)
    weight_two = -(middle / radius_two) * sin_one * beta / radius_two
    weight_one = (cos_one * beta - upper * weight_two) / radius_one
    return (weight_one, weight_two)


def kernel(
    rows, cols, tile,
    rhs_hbm, flags, near_hbm, far_hbm, basis_hbm, selft_hbm, dinv_hbm, low_hbm, out,
    rhs, near, far, basis, selft, dinv, low, load,
    rbuf, sbuf, sol, roots, pres, blocks, s_q_send, s_q_recv, b_send, b_recv, s_r_send, s_r_recv, s_e_send, s_e_recv, s_p_send,
    dsp, mats, m0, crecv, csend, ebuf, prev, pcur, piece, gbuf, zbuf, pbuf, part, stile, gath, fsend, fin,
    m_send, m_recv, c_send, c_recv, p_send, p_recv, z_send, z_recv, q_send, q_recv, x_send, x_recv, r_send, r_recv, g_send, g_recv,
    f_send, f_recv,
):
    row = lax.axis_index("row")
    col = lax.axis_index("col")
    chip = row // 2
    core = row % 2
    last = rows // 2 - 1
    per = rows // cols
    home = row // per
    c = dinv.shape[-1]
    half = c // 2
    rank = basis.shape[0]
    group = chip // GROUP
    member = chip % GROUP
    groups = rows // 2 // GROUP
    at_end = jnp.logical_and(core == 1, member == GROUP - 1)
    gives = jnp.logical_and(core == 1, member < GROUP - 1)
    solver = 2 * GROUP * group + 2 * GROUP - 1

    loads = [
        pltpu.make_async_copy(source, target, load.at[n])
        for n, (source, target) in enumerate((
            (dinv_hbm.at[0], dinv), (low_hbm.at[0], low),
            (rhs_hbm.at[pl.ds(pl.multiple_of(col * SYS, SYS), SYS)], rhs),
            (near_hbm.at[0], near), (far_hbm.at[0], far), (basis_hbm.at[0], basis), (selft_hbm, selft),
        ))
    ]
    for copy in loads:
        copy.start()

    bar = pltpu.get_barrier_semaphore()

    def tell(r, k):
        pl.semaphore_signal(bar, inc=1, device_id=(r, k), device_id_type=MESH)

    @pl.loop(1, rows)
    def _(t):
        tell(lax.rem(row + t, rows), col)

    @pl.loop(1, cols)
    def _(t):
        tell(row, lax.rem(col + t, cols))

    def spread(turn):
        @pl.loop(1, rows)
        def _(t):
            pltpu.make_async_remote_copy(
                src_ref=stile.at[turn], dst_ref=gath.at[turn, t - 1],
                send_sem=g_send.at[turn], recv_sem=g_recv.at[turn],
                device_id=(lax.rem(row + t, rows), col), device_id_type=MESH,
            ).start()

    def arrive(turn):
        pltpu.make_async_copy(gath.at[turn], gath.at[turn], g_recv.at[turn]).wait()

    loads[0].wait()

    @pl.loop(0, c // tile)
    def _(t):
        at = pl.ds(pl.multiple_of(t * tile, tile), tile)
        put_split(dsp, at, dinv[at, :])

    place = 1 - core
    loads[1].wait()

    @pl.loop(0, c // tile)
    def _(t):
        at = pl.ds(pl.multiple_of(t * tile, tile), tile)
        put_split(mats.at[place], at, times(low[at, :], dsp[...]))

    loads[2].wait()
    v = rhs[...]
    stile[0] = jnp.broadcast_to(total(v * v), (SYS, 128))
    pl.semaphore_wait(bar, rows + cols - 2)

    def to_sibling(t):
        at = pl.ds(pl.multiple_of(t * tile, tile), tile)
        return pltpu.make_async_remote_copy(
            src_ref=mats.at[1, at], dst_ref=m0.at[at],
            send_sem=m_send.at[t], recv_sem=m_recv.at[t],
            device_id=(row - core + 1, col), device_id_type=MESH,
        )

    tiles = c // tile
    odd = lax.rem(col, 2)

    def tile_at(u):
        return lax.rem(u + odd * (tiles // 2), tiles)

    def offer():
        @pl.loop(0, tiles)
        def _(u):
            to_sibling(tile_at(u)).start()

    direct = group == 0
    late = chip < GROUP // 2

    @pl.when(jnp.logical_and(core == 0, jnp.logical_not(late)))
    def _():
        offer()

    def half_rows(which):
        return pl.ds(pl.multiple_of(which * half, half), half)

    def matrix_copy(y):
        return pltpu.make_async_remote_copy(
            src_ref=mats.at[1, half_rows(odd)], dst_ref=rbuf.at[y, half_rows(odd)],
            send_sem=s_r_send, recv_sem=s_r_recv.at[y],
            device_id=(solver, col), device_id_type=MESH,
        )

    def form_pair():
        @pl.loop(0, tiles)
        def _(u):
            t = tile_at(u)
            to_sibling(t).wait_recv()
            at = pl.ds(pl.multiple_of(t * tile, tile), tile)
            both = jnp.concatenate([m0[at, :c], m0[at, c:]], axis=0)
            y = jnp.dot(both, mats[0], preferred_element_type=f32)
            y = y[:tile] + y[tile:]
            put_split(mats.at[1], at, y[:, :c] + y[:, c:])

            @pl.when(jnp.logical_and(u == tiles // 2 - 1, jnp.logical_and(gives, group > 0)))
            def _():
                matrix_copy(member).start()

    @pl.when(jnp.logical_and(core == 1, jnp.logical_not(late)))
    def _():
        form_pair()

    quarter = half // 2

    def quarter_rows(which, d):
        return pl.ds(pl.multiple_of(which * half + d * quarter, quarter), quarter)

    def pass_copy(y, d):
        at = quarter_rows(odd, d)
        return pltpu.make_async_remote_copy(
            src_ref=rbuf.at[y, at], dst_ref=rbuf.at[y, at], send_sem=s_q_send,
            recv_sem=s_q_recv.at[d, y],
            device_id=(row, lax.rem(col + (1 if d == 0 else cols - 1), cols)), device_id_type=MESH,
        )

    def take_matrices():
        for y in [0] + list(range(GROUP - 2, 0, -1)):
            matrix_copy(y).wait_recv()
            for d in range(2):
                pass_copy(y, d).start()
        for y in range(GROUP - 1):
            for d in range(2):
                there = rbuf.at[y, quarter_rows(1 - odd, d)]
                pltpu.make_async_copy(there, there, s_q_recv.at[d, y]).wait()

    sign = jnp.where(core == 0, -1.0, 1.0).astype(f32)

    def c_copy(app):
        return pltpu.make_async_remote_copy(
            src_ref=csend.at[app], dst_ref=crecv.at[app],
            send_sem=c_send.at[app], recv_sem=c_recv.at[app],
            device_id=(row - core + 1, col), device_id_type=MESH,
        )

    def p_copy(app, to):
        target = 2 * chip + 2 + to if to < 2 else solver + 2 * GROUP
        return pltpu.make_async_remote_copy(
            src_ref=pcur.at[app], dst_ref=prev.at[app],
            send_sem=p_send.at[app, to], recv_sem=p_recv.at[app],
            device_id=(target, col), device_id_type=MESH,
        )

    def term_copy(app, y):
        return pltpu.make_async_remote_copy(
            src_ref=ebuf.at[app], dst_ref=sbuf.at[app, y], send_sem=s_e_send.at[app],
            recv_sem=s_e_recv.at[app, y], device_id=(solver, col), device_id_type=MESH,
        )

    def step_copies(app, y):
        return [
            pltpu.make_async_remote_copy(
                src_ref=sol.at[app, y], dst_ref=prev.at[app],
                send_sem=s_p_send.at[app, 2 * y + k], recv_sem=p_recv.at[app],
                device_id=(2 * GROUP * group + 2 * y + 2 + k, col), device_id_type=MESH,
            )
            for k in range(2 if y < GROUP - 2 else 1)
        ]

    def both_of(a, b):
        return jnp.logical_and(a, b)

    def walked(app):
        return group < HOPS[app]

    def forwards(app):
        return both_of(chip < last, both_of(core == 1, jnp.logical_or(walked(app), at_end)))

    def forwards_to_one(app):
        return both_of(forwards(app), chip >= GROUP - 1) if app == 0 else forwards(app)

    def leaps(app):
        return both_of(forwards(app), both_of(at_end, group + 1 >= HOPS[app]))

    def chain(app, vec, between):
        own = times(vec, dsp[...])
        solved = jnp.logical_not(walked(app))

        @pl.when(core == 0)
        def _():
            csend[app] = own

            if app == 0:
                @pl.when(both_of(direct, chip > 0))
                def _():
                    p_copy(app, 0).wait_recv()
                    csend[app] = own - times(prev[app], mats[1])

            c_copy(app).start()
            ebuf[app] = csend[app]

        @pl.when(core == 1)
        def _():
            c_copy(app).wait_recv()
            ebuf[app] = own - times(crecv[app], mats[0])

        @pl.when(both_of(gives, solved))
        def _():
            term_copy(app, member).start()

        between()

        @pl.when(both_of(at_end, solved))
        def _():
            if app == 0:
                take_matrices()

            for y in range(GROUP - 1):
                term_copy(app, y).wait_recv()

            @pl.when(group == 0)
            def _():
                sol[app, 0] = sbuf[app, 0]

            @pl.when(group > 0)
            def _():
                p_copy(app, 0).wait_recv()
                sol[app, 0] = sbuf[app, 0] + times(prev[app], rbuf[0])

            for y in range(GROUP - 1):
                @pl.when(group == groups - 1)
                def _():
                    for copy in step_copies(app, y):
                        copy.start()

                if y < GROUP - 2:
                    sol[app, y + 1] = sbuf[app, y + 1] + times(sol[app, y], rbuf[y + 1])
                else:
                    pcur[app] = ebuf[app] + times(sol[app, y], mats[1])

        @pl.when(jnp.logical_not(both_of(at_end, solved)))
        def _():
            ready = direct if app == 0 else chip == 0

            @pl.when(ready)
            def _():
                pcur[app] = ebuf[app]

            @pl.when(jnp.logical_not(ready))
            def _():
                p_copy(app, 0).wait_recv()
                pcur[app] = ebuf[app] + sign * times(prev[app], mats[1])

        @pl.when(leaps(app))
        def _():
            p_copy(app, 2).start()

        @pl.when(forwards_to_one(app))
        def _():
            p_copy(app, 1).start()

        @pl.when(forwards(app))
        def _():
            p_copy(app, 0).start()

        @pl.when(both_of(both_of(at_end, solved), group < groups - 1))
        def _():
            for y in range(GROUP - 1):
                for copy in step_copies(app, y):
                    copy.start()

    chips = rows // 2
    count = per // 2
    side = lax.rem(row, per) // count

    def far_row(t):
        return 2 * lax.rem(chip + t + chips // 2, chips) + side

    def piece_copy(app, t):
        return pltpu.make_async_remote_copy(
            src_ref=piece.at[app], dst_ref=gbuf.at[app, home, lax.rem(row, count)],
            send_sem=z_send.at[app, t], recv_sem=z_recv.at[app, home],
            device_id=(far_row(t), col), device_id_type=MESH,
        )

    def own_piece_copy(app):
        return pltpu.make_async_copy(
            piece.at[app], gbuf.at[app, home, lax.rem(row, count)], z_recv.at[app, home]
        )

    def plane_copy(app, k):
        return pltpu.make_async_remote_copy(
            src_ref=gbuf.at[app, k], dst_ref=zbuf.at[app, core, col],
            send_sem=q_send.at[app], recv_sem=q_recv.at[app],
            device_id=(row, k), device_id_type=MESH,
        )

    far_first = sorted(range(1, cols), key=lambda t: -min(t, cols - t))

    def core_copy(app):
        return pltpu.make_async_remote_copy(
            src_ref=zbuf.at[app, core], dst_ref=zbuf.at[app, core],
            send_sem=x_send.at[app], recv_sem=x_recv.at[app],
            device_id=(row + 1 - 2 * core, col), device_id_type=MESH,
        )

    def r_copy(app, t):
        to = lax.rem(col + t, cols)
        return pltpu.make_async_remote_copy(
            src_ref=pbuf.at[app, to], dst_ref=part.at[app, t - 1],
            send_sem=r_send.at[app], recv_sem=r_recv.at[app],
            device_id=(row, to), device_id_type=MESH,
        )

    def send_blocks(app):
        for t in far_first:
            pltpu.make_async_remote_copy(
                src_ref=pres.at[app], dst_ref=blocks.at[app, t - 1],
                send_sem=b_send.at[app], recv_sem=b_recv.at[app],
                device_id=(row, lax.rem(col + t, cols)), device_id_type=MESH,
            ).start()

    def apply_matrix(app, pre, meanwhile):
        piece[app] = jnp.concatenate([pre[:, :half], pre[:, half:]], axis=0).astype(bf16)

        @pl.loop(0, chips)
        def _(t):
            @pl.when(far_row(t) != row)
            def _():
                piece_copy(app, t).start()

            @pl.when(far_row(t) == row)
            def _():
                own_piece_copy(app).start()

        meanwhile()

        @pl.loop(0, cols)
        def _(k):
            pltpu.make_async_copy(gbuf.at[app, k], gbuf.at[app, k], z_recv.at[app, k]).wait()

            @pl.when(k != col)
            def _():
                plane_copy(app, k).start()

            @pl.when(k == col)
            def _():
                pltpu.make_async_copy(gbuf.at[app, k], zbuf.at[app, core, col], q_recv.at[app]).start()

        def products(which):
            near_sum = jnp.zeros((SYS * cols, c), f32)
            far_sum = jnp.zeros((SYS * cols, rank), f32)
            for j in range(count):
                z = zbuf[app, which, :, j].astype(f32)
                z = jnp.concatenate(
                    [z[:, :SYS].reshape(SYS * cols, half), z[:, SYS:].reshape(SYS * cols, half)], axis=1
                )
                at = which * count + j
                near_in = z * flags[0, at].astype(f32)
                far_in = (z - near_in).astype(bf16)
                near_sum += jnp.dot(near_in.astype(bf16), near[at], preferred_element_type=f32)
                far_sum += lax.dot_general(
                    far_in, far[at], (((1,), (1,)), ((), ())), preferred_element_type=f32
                )
            return near_sum, far_sum

        pltpu.make_async_copy(zbuf.at[app, core], zbuf.at[app, core], q_recv.at[app]).wait()
        core_copy(app).start()
        near_sum, far_sum = products(core)
        core_copy(app).wait_recv()
        near_other, far_other = products(1 - core)
        near_sum += near_other
        far_sum += far_other
        pbuf[app, :, :, :c] = near_sum.reshape(cols, SYS, c)
        pbuf[app, :, :, c:] = jnp.concatenate(
            [far_sum, jnp.zeros((SYS * cols, 128 - rank), f32)], axis=1
        ).reshape(cols, SYS, 128)

        for t in far_first:
            r_copy(app, t).start()

        pltpu.make_async_copy(part.at[app], part.at[app], r_recv.at[app]).wait()
        both = pbuf[app, col]
        for t in range(cols - 1):
            both += part[app, t]
        far_part = jnp.dot(
            both[:, c:c + rank].astype(bf16), basis[...], preferred_element_type=f32
        )
        return selft[...] * pre + both[:, :c] + far_part

    lane = lax.broadcasted_iota(jnp.int32, (SYS, 128), 1)

    def spread_squares():
        @pl.when(group > 0)
        def _():
            spread(0)

    chain(0, v * SCALE, spread_squares)

    @pl.when(group == 0)
    def _():
        spread(0)


    @pl.when(both_of(late, core == 0))
    def _():
        offer()

    @pl.when(both_of(late, core == 1))
    def _():
        form_pair()

    @pl.when(both_of(gives, direct))
    def _():
        matrix_copy(member).start()

    arrive(0)
    own_square = stile[0]
    squares = own_square
    for t in range(rows - 1):
        squares += gath[0, t]
    beta_tile = jnp.sqrt(squares + epsilon)
    beta = beta_tile[:, :1]
    first = v / beta
    pre_one = pcur[0] * (1.0 / SCALE / beta)
    pres[0] = pre_one

    def wait_loads():
        for copy in loads[3:]:
            copy.wait()
        roots[rows - 1] = jnp.sqrt(own_square) / beta_tile
        for t in range(rows - 1):
            roots[t] = jnp.sqrt(gath[0, t]) / beta_tile

        @pl.when(both_of(at_end, walked(0)))
        def _():
            take_matrices()

    image = apply_matrix(0, pre_one, wait_loads)

    root = roots[rows - 1][:, :1]
    some = root > 1e-15
    unit_one = jnp.where(some, first / jnp.where(some, root, 1.0), 0.0)
    along = total(unit_one * image)
    left = image - along * unit_one
    rest = jnp.sqrt(total(left * left))

    def lanes(*values):
        tile = jnp.zeros((SYS, 128), f32)
        for at, value in values:
            tile = jnp.where(lane == at, value, tile)
        return tile

    stile[1] = lanes((0, total(first * image)), (1, along), (2, rest))

    first_solver = both_of(at_end, group == 0)

    def spread_heights():
        @pl.when(jnp.logical_not(first_solver))
        def _():
            spread(1)
            send_blocks(0)

    chain(1, image, spread_heights)

    @pl.when(first_solver)
    def _():
        spread(1)
        send_blocks(0)

    arrive(1)
    heights = stile[1]
    for t in range(rows - 1):
        heights += gath[1, t]
    proj_one = heights[:, :1]
    weight = jnp.where(lane == 1, proj_one, 0.0)
    keep = jnp.where(jnp.logical_or(lane == 1, lane == 2), 1.0, 0.0)

    def term(tile, size):
        y = (tile - weight * size) * keep
        return y * y

    squares = term(stile[1], roots[rows - 1])
    for t in range(rows - 1):
        squares += term(gath[1, t], roots[t])
    norm_one = jnp.sqrt(total(squares) + epsilon)
    second = (image - proj_one * first) / norm_one
    pre_two = (pcur[1] - proj_one * pre_one) / norm_one
    pres[1] = pre_two
    frame = []

    def local_frame():
        turn = total(unit_one * second)
        across = second - turn * unit_one
        again = total(unit_one * across)
        across = across - again * unit_one
        turn = turn + again
        size = jnp.sqrt(total(across * across))
        some = size > 1e-15
        unit_two = jnp.where(some, across / jnp.where(some, size, 1.0), 0.0)
        frame.extend((turn, size, unit_two))

    image = apply_matrix(1, pre_two, local_frame)
    turn, size, unit_two = frame
    along_one = total(unit_one * image)
    left = image - along_one * unit_one
    along_two = total(unit_two * left)
    left = left - along_two * unit_two
    stile[2] = lanes(
        (0, total(first * image)), (1, total(second * image)),
        (2, along_one), (4, along_two), (6, jnp.sqrt(total(left * left))),
        (66, turn), (68, size),
    )
    spread(2)
    send_blocks(1)
    arrive(2)
    heights = stile[2]
    for t in range(rows - 1):
        heights += gath[2, t]
    cross = heights[:, :1]
    proj_two = heights[:, 1:2]
    weight = jnp.where(lane == 2, cross, 0.0)
    keep = jnp.where(
        jnp.logical_or(lane == 2, jnp.logical_or(lane == 4, lane == 6)), 1.0, 0.0
    )

    def term_two(tile, size):
        y = (tile - weight * size - proj_two * pltpu.roll(tile, 64, 1)) * keep
        return y * y

    squares = term_two(stile[2], roots[rows - 1])
    for t in range(rows - 1):
        squares += term_two(gath[2, t], roots[t])
    norm_two = jnp.sqrt(total(squares) + epsilon)
    weight_one, weight_two = least_squares(beta, proj_one, norm_one, cross, proj_two, norm_two)
    fsend[...] = lanes((0, weight_one), (1, weight_two))

    def f_copy(t):
        return pltpu.make_async_remote_copy(
            src_ref=fsend, dst_ref=fin.at[t - 1], send_sem=f_send, recv_sem=f_recv,
            device_id=(row, lax.rem(col + t, cols)), device_id_type=MESH,
        )

    for t in far_first:
        f_copy(t).start()

    out[pl.ds(pl.multiple_of(col * SYS, SYS), SYS), :] = pre_one * weight_one + pre_two * weight_two

    @pl.when(core == 0)
    def _():
        @pl.loop(0, c // tile)
        def _(t):
            to_sibling(t).wait_send()

    @pl.when(gives)
    def _():
        matrix_copy(member).wait_send()

    @pl.when(at_end)
    def _():
        passed = rbuf.at[:, pl.ds(0, half)]
        pltpu.make_async_copy(passed, passed, s_q_send).wait()

    for app in range(2):
        @pl.when(core == 0)
        def _():
            c_copy(app).wait_send()

        @pl.when(forwards(app))
        def _():
            p_copy(app, 0).wait_send()

        @pl.when(forwards_to_one(app))
        def _():
            p_copy(app, 1).wait_send()

        @pl.when(leaps(app))
        def _():
            p_copy(app, 2).wait_send()

        @pl.when(both_of(gives, jnp.logical_not(walked(app))))
        def _():
            term_copy(app, member).wait_send()

        @pl.when(both_of(at_end, jnp.logical_not(walked(app))))
        def _():
            for y in range(GROUP - 1):
                for copy in step_copies(app, y):
                    copy.wait_send()

        @pl.loop(0, chips)
        def _(t):
            @pl.when(far_row(t) != row)
            def _():
                piece_copy(app, t).wait_send()

        sent = zbuf.at[app, 0, pl.ds(0, cols - 1)]
        pltpu.make_async_copy(sent, sent, q_send.at[app]).wait()
        core_copy(app).wait_send()

        pltpu.make_async_copy(part.at[app], part.at[app], r_send.at[app]).wait()
        pltpu.make_async_copy(blocks.at[app], blocks.at[app], b_send.at[app]).wait()
        pltpu.make_async_copy(blocks.at[app], blocks.at[app], b_recv.at[app]).wait()

    for n in range(3):
        pltpu.make_async_copy(gath.at[n], gath.at[n], g_send.at[n]).wait()

    pltpu.make_async_copy(fin, fin, f_recv).wait()
    for t in range(1, cols):
        at = lax.rem(col + cols - t, cols)
        out[pl.ds(pl.multiple_of(at * SYS, SYS), SYS), :] = (
            blocks[0, t - 1] * fin[t - 1, :, 0:1] + blocks[1, t - 1] * fin[t - 1, :, 1:2]
        )
    pltpu.make_async_copy(fin, fin, f_send).wait()


def body(rows, cols, rhs, flags, near, far, basis, selft, dinv, low):
    c = dinv.shape[-1]
    per = rows // cols
    tile = min(128, c)
    vm = pltpu.VMEM
    dma = pltpu.SemaphoreType.DMA
    vmem = pl.BlockSpec(memory_space=pltpu.VMEM)
    smem = pl.BlockSpec(memory_space=pltpu.SMEM)
    hbm = pl.BlockSpec(memory_space=pl.ANY)
    rank = basis.shape[1]
    return pl.pallas_call(
        functools.partial(kernel, rows, cols, tile),
        out_shape=jax.ShapeDtypeStruct(rhs.shape, f32),
        in_specs=[hbm, smem] + [hbm] * 6,
        out_specs=vmem,
        scratch_shapes=[
            vm((SYS, c), f32), vm((per, c, c), bf16), vm((per, rank, c), bf16), vm((rank, c), bf16),
            vm((1, c), f32), vm((c, c), f32), vm((c, c), f32), dma((7,)),
            vm((GROUP - 1, c, 2 * c), bf16),
            vm((2, GROUP - 1, SYS, c), f32),
            vm((2, GROUP - 1, SYS, c), f32),
            vm((rows, SYS, 128), f32),
            vm((2, SYS, c), f32),
            vm((2, cols - 1, SYS, c), f32),
            dma(()), dma((2, GROUP - 1)), dma((2,)), dma((2,)),
            dma(()), dma((GROUP - 1,)), dma((2,)), dma((2, GROUP - 1)), dma((2, 2 * GROUP)),
            vm((c, 2 * c), bf16),
            vm((2, c, 2 * c), bf16),
            vm((c, 2 * c), bf16),
            vm((2, SYS, c), f32),
            vm((2, SYS, c), f32),
            vm((2, SYS, c), f32),
            vm((2, SYS, c), f32),
            vm((2, SYS, c), f32),
            vm((2, 2 * SYS, c // 2), bf16),
            vm((2, cols, per // 2, 2 * SYS, c // 2), bf16),
            vm((2, 2, cols, per // 2, 2 * SYS, c // 2), bf16),
            vm((2, cols, SYS, c + 128), f32),
            vm((2, cols - 1, SYS, c + 128), f32),
            vm((3, SYS, 128), f32),
            vm((3, rows - 1, SYS, 128), f32),
            vm((SYS, 128), f32),
            vm((cols - 1, SYS, 128), f32),
            dma((c // tile,)), dma((c // tile,)),
            dma((2,)), dma((2,)),
            dma((2, 3)), dma((2,)),
            dma((2, rows // 2)), dma((2, cols)),
            dma((2,)), dma((2,)),
            dma((2,)), dma((2,)),
            dma((2,)), dma((2,)),
            dma((3,)), dma((3,)),
            dma(()), dma(()),
        ],
        compiler_params=pltpu.CompilerParams(
            collective_id=0, has_side_effects=True, vmem_limit_bytes=60 * 2**20
        ),
    )(rhs, flags, near, far, basis, selft.reshape(1, -1), dinv, low)


def solution(mesh):
    placed = (
        P(None, "row"),
        P("row", "col"),
        P("row", "col", None, None),
        P("row", "col", None, None),
        P("row", None, None),
        P("row"),
        P("row", None, None),
        P("row", None, None),
    )
    return jax.shard_map(
        functools.partial(body, mesh.shape["row"], mesh.shape["col"]),
        mesh=mesh, in_specs=placed, out_specs=P(None, "row"), check_vma=False,
    )
```

```python
import functools

import jax
import jax.numpy as jnp
from jax import lax
from jax.experimental import pallas as pl
from jax.experimental.pallas import tpu as pltpu
from jax.sharding import PartitionSpec as P

epsilon = 1e-06
PIECES = 4
SCALE = 2.0 ** -13
f32 = jnp.float32
bf16 = jnp.bfloat16
MESH = pl.DeviceIdType.MESH
SYS = 8
GROUP = 4
HOPS = (2, 0)


def stacked(x):
    high = x.astype(bf16).astype(f32)
    return jnp.concatenate([high, x - high], axis=0).astype(bf16)


def times(x, mat):
    y = jnp.dot(stacked(x), mat, preferred_element_type=f32)
    n, c = x.shape[0], mat.shape[1] // 2
    y = y[:n] + y[n:]
    return y[:, :c] + y[:, c:]


def put_split(ref, rows, m):
    c = m.shape[1]
    high = m.astype(bf16)
    ref[rows, :c] = high
    ref[rows, c:] = (m - high.astype(f32)).astype(bf16)


def total(x):
    return jnp.sum(x, axis=1, keepdims=True)


def least_squares(beta, proj_one, norm_one, cross, proj_two, norm_two):
    radius_one = jnp.sqrt(proj_one * proj_one + norm_one * norm_one)
    cos_one = proj_one / radius_one
    sin_one = norm_one / radius_one
    upper = cos_one * cross + sin_one * proj_two
    middle = cos_one * proj_two - sin_one * cross
    radius_two = jnp.sqrt(middle * middle + norm_two * norm_two)
    weight_two = -(middle / radius_two) * sin_one * beta / radius_two
    weight_one = (cos_one * beta - upper * weight_two) / radius_one
    return (weight_one, weight_two)


def kernel(
    rows, cols, tile,
    rhs_hbm, flags, near_hbm, far_hbm, basis_hbm, selft_hbm, dinv_hbm, low_hbm, out,
    rhs, near, far, basis, selft, dinv, low, load,
    rbuf, sbuf, sol, roots, pres, blocks, s_q_send, s_q_recv, b_send, b_recv, s_r_send, s_r_recv, s_e_send, s_e_recv, s_p_send,
    dsp, mats, m0, crecv, csend, ebuf, prev, pcur, piece, gbuf, zbuf, pbuf, part, stile, gath, fsend, fin,
    m_send, m_recv, c_send, c_recv, p_send, p_recv, z_send, z_recv, q_send, q_recv, x_send, x_recv, r_send, r_recv, g_send, g_recv,
    f_send, f_recv,
):
    row = lax.axis_index("row")
    col = lax.axis_index("col")
    chip = row // 2
    core = row % 2
    last = rows // 2 - 1
    per = rows // cols
    home = row // per
    c = dinv.shape[-1]
    half = c // 2
    rank = basis.shape[0]
    group = chip // GROUP
    member = chip % GROUP
    groups = rows // 2 // GROUP
    at_end = jnp.logical_and(core == 1, member == GROUP - 1)
    gives = jnp.logical_and(core == 1, member < GROUP - 1)
    solver = 2 * GROUP * group + 2 * GROUP - 1

    loads = [
        pltpu.make_async_copy(source, target, load.at[n])
        for n, (source, target) in enumerate((
            (dinv_hbm.at[0], dinv), (low_hbm.at[0], low),
            (rhs_hbm.at[pl.ds(pl.multiple_of(col * SYS, SYS), SYS)], rhs),
            (near_hbm.at[0], near), (far_hbm.at[0], far), (basis_hbm.at[0], basis), (selft_hbm, selft),
        ))
    ]
    for copy in loads:
        copy.start()

    bar = pltpu.get_barrier_semaphore()

    def tell(r, k):
        pl.semaphore_signal(bar, inc=1, device_id=(r, k), device_id_type=MESH)

    @pl.loop(1, rows)
    def _(t):
        tell(lax.rem(row + t, rows), col)

    @pl.loop(1, cols)
    def _(t):
        tell(row, lax.rem(col + t, cols))

    def spread(turn):
        @pl.loop(1, rows)
        def _(t):
            pltpu.make_async_remote_copy(
                src_ref=stile.at[turn], dst_ref=gath.at[turn, t - 1],
                send_sem=g_send.at[turn], recv_sem=g_recv.at[turn],
                device_id=(lax.rem(row + t, rows), col), device_id_type=MESH,
            ).start()

    def arrive(turn):
        pltpu.make_async_copy(gath.at[turn], gath.at[turn], g_recv.at[turn]).wait()

    loads[0].wait()

    @pl.loop(0, c // tile)
    def _(t):
        at = pl.ds(pl.multiple_of(t * tile, tile), tile)
        put_split(dsp, at, dinv[at, :])

    place = 1 - core
    loads[1].wait()

    @pl.loop(0, c // tile)
    def _(t):
        at = pl.ds(pl.multiple_of(t * tile, tile), tile)
        put_split(mats.at[place], at, times(low[at, :], dsp[...]))

    loads[2].wait()
    v = rhs[...]
    stile[0] = jnp.broadcast_to(total(v * v), (SYS, 128))
    pl.semaphore_wait(bar, rows + cols - 2)

    def to_sibling(t):
        at = pl.ds(pl.multiple_of(t * tile, tile), tile)
        return pltpu.make_async_remote_copy(
            src_ref=mats.at[1, at], dst_ref=m0.at[at],
            send_sem=m_send.at[t], recv_sem=m_recv.at[t],
            device_id=(row - core + 1, col), device_id_type=MESH,
        )

    tiles = c // tile
    odd = lax.rem(col, 2)

    def tile_at(u):
        return lax.rem(u + odd * (tiles // 2), tiles)

    def offer():
        @pl.loop(0, tiles)
        def _(u):
            to_sibling(tile_at(u)).start()

    direct = group == 0
    late = chip < GROUP // 2

    @pl.when(jnp.logical_and(core == 0, jnp.logical_not(late)))
    def _():
        offer()

    piece_rows = half // PIECES

    def part_rows(which, n):
        return pl.ds(pl.multiple_of(which * half + n * piece_rows, piece_rows), piece_rows)

    def matrix_copy(y, n):
        at = part_rows(odd, n)
        return pltpu.make_async_remote_copy(
            src_ref=mats.at[1, at], dst_ref=rbuf.at[y, at],
            send_sem=s_r_send, recv_sem=s_r_recv.at[y, n],
            device_id=(solver, col), device_id_type=MESH,
        )

    def form_pair():
        @pl.loop(0, tiles)
        def _(u):
            t = tile_at(u)
            to_sibling(t).wait_recv()
            at = pl.ds(pl.multiple_of(t * tile, tile), tile)
            both = jnp.concatenate([m0[at, :c], m0[at, c:]], axis=0)
            y = jnp.dot(both, mats[0], preferred_element_type=f32)
            y = y[:tile] + y[tile:]
            put_split(mats.at[1], at, y[:, :c] + y[:, c:])

            @pl.when(jnp.logical_and(u < tiles // 2, jnp.logical_and(gives, group > 0)))
            def _():
                each = PIECES // (tiles // 2)
                for n in range(each):
                    matrix_copy(member, u * each + n).start()

    @pl.when(jnp.logical_and(core == 1, jnp.logical_not(late)))
    def _():
        form_pair()

    def pass_copy(y, n):
        at = part_rows(odd, n)
        return pltpu.make_async_remote_copy(
            src_ref=rbuf.at[y, at], dst_ref=rbuf.at[y, at], send_sem=s_q_send,
            recv_sem=s_q_recv.at[y, n],
            device_id=(row, lax.rem(col + (1 if n % 2 == 0 else cols - 1), cols)), device_id_type=MESH,
        )

    def take_matrices():
        for n in range(PIECES):
            for y in [0] + list(range(GROUP - 2, 0, -1)):
                matrix_copy(y, n).wait_recv()
                pass_copy(y, n).start()
        for n in range(PIECES):
            for y in range(GROUP - 1):
                there = rbuf.at[y, part_rows(1 - odd, n)]
                pltpu.make_async_copy(there, there, s_q_recv.at[y, n]).wait()

    sign = jnp.where(core == 0, -1.0, 1.0).astype(f32)

    def c_copy(app):
        return pltpu.make_async_remote_copy(
            src_ref=csend.at[app], dst_ref=crecv.at[app],
            send_sem=c_send.at[app], recv_sem=c_recv.at[app],
            device_id=(row - core + 1, col), device_id_type=MESH,
        )

    def p_copy(app, to):
        target = 2 * chip + 2 + to if to < 2 else solver + 2 * GROUP
        return pltpu.make_async_remote_copy(
            src_ref=pcur.at[app], dst_ref=prev.at[app],
            send_sem=p_send.at[app, to], recv_sem=p_recv.at[app],
            device_id=(target, col), device_id_type=MESH,
        )

    def term_copy(app, y):
        return pltpu.make_async_remote_copy(
            src_ref=ebuf.at[app], dst_ref=sbuf.at[app, y], send_sem=s_e_send.at[app],
            recv_sem=s_e_recv.at[app, y], device_id=(solver, col), device_id_type=MESH,
        )

    def step_copies(app, y):
        return [
            pltpu.make_async_remote_copy(
                src_ref=sol.at[app, y], dst_ref=prev.at[app],
                send_sem=s_p_send.at[app, 2 * y + k], recv_sem=p_recv.at[app],
                device_id=(2 * GROUP * group + 2 * y + 2 + k, col), device_id_type=MESH,
            )
            for k in range(2 if y < GROUP - 2 else 1)
        ]

    def both_of(a, b):
        return jnp.logical_and(a, b)

    def walked(app):
        return group < HOPS[app]

    def forwards(app):
        return both_of(chip < last, both_of(core == 1, jnp.logical_or(walked(app), at_end)))

    def forwards_to_one(app):
        return both_of(forwards(app), chip >= GROUP - 1) if app == 0 else forwards(app)

    def leaps(app):
        return both_of(forwards(app), both_of(at_end, group + 1 >= HOPS[app]))

    def chain(app, vec, between):
        own = times(vec, dsp[...])
        solved = jnp.logical_not(walked(app))

        @pl.when(core == 0)
        def _():
            csend[app] = own

            if app == 0:
                @pl.when(both_of(direct, chip > 0))
                def _():
                    p_copy(app, 0).wait_recv()
                    csend[app] = own - times(prev[app], mats[1])

            c_copy(app).start()
            ebuf[app] = csend[app]

        @pl.when(core == 1)
        def _():
            c_copy(app).wait_recv()
            ebuf[app] = own - times(crecv[app], mats[0])

        @pl.when(both_of(gives, solved))
        def _():
            term_copy(app, member).start()

        between()

        @pl.when(both_of(at_end, solved))
        def _():
            if app == 0:
                take_matrices()

            for y in range(GROUP - 1):
                term_copy(app, y).wait_recv()

            @pl.when(group == 0)
            def _():
                sol[app, 0] = sbuf[app, 0]

            @pl.when(group > 0)
            def _():
                p_copy(app, 0).wait_recv()
                sol[app, 0] = sbuf[app, 0] + times(prev[app], rbuf[0])

            for y in range(GROUP - 1):
                @pl.when(group == groups - 1)
                def _():
                    for copy in step_copies(app, y):
                        copy.start()

                if y < GROUP - 2:
                    sol[app, y + 1] = sbuf[app, y + 1] + times(sol[app, y], rbuf[y + 1])
                else:
                    pcur[app] = ebuf[app] + times(sol[app, y], mats[1])

        @pl.when(jnp.logical_not(both_of(at_end, solved)))
        def _():
            ready = direct if app == 0 else chip == 0

            @pl.when(ready)
            def _():
                pcur[app] = ebuf[app]

            @pl.when(jnp.logical_not(ready))
            def _():
                p_copy(app, 0).wait_recv()
                pcur[app] = ebuf[app] + sign * times(prev[app], mats[1])

        @pl.when(leaps(app))
        def _():
            p_copy(app, 2).start()

        @pl.when(forwards_to_one(app))
        def _():
            p_copy(app, 1).start()

        @pl.when(forwards(app))
        def _():
            p_copy(app, 0).start()

        @pl.when(both_of(both_of(at_end, solved), group < groups - 1))
        def _():
            for y in range(GROUP - 1):
                for copy in step_copies(app, y):
                    copy.start()

    chips = rows // 2
    count = per // 2
    side = lax.rem(row, per) // count

    def far_row(t):
        return 2 * lax.rem(chip + t + chips // 2, chips) + side

    def piece_copy(app, t):
        return pltpu.make_async_remote_copy(
            src_ref=piece.at[app], dst_ref=gbuf.at[app, home, lax.rem(row, count)],
            send_sem=z_send.at[app, t], recv_sem=z_recv.at[app, home],
            device_id=(far_row(t), col), device_id_type=MESH,
        )

    def own_piece_copy(app):
        return pltpu.make_async_copy(
            piece.at[app], gbuf.at[app, home, lax.rem(row, count)], z_recv.at[app, home]
        )

    def plane_copy(app, k):
        return pltpu.make_async_remote_copy(
            src_ref=gbuf.at[app, k], dst_ref=zbuf.at[app, core, col],
            send_sem=q_send.at[app], recv_sem=q_recv.at[app],
            device_id=(row, k), device_id_type=MESH,
        )

    far_first = sorted(range(1, cols), key=lambda t: -min(t, cols - t))

    def core_copy(app):
        return pltpu.make_async_remote_copy(
            src_ref=zbuf.at[app, core], dst_ref=zbuf.at[app, core],
            send_sem=x_send.at[app], recv_sem=x_recv.at[app],
            device_id=(row + 1 - 2 * core, col), device_id_type=MESH,
        )

    def r_copy(app, t):
        to = lax.rem(col + t, cols)
        return pltpu.make_async_remote_copy(
            src_ref=pbuf.at[app, to], dst_ref=part.at[app, t - 1],
            send_sem=r_send.at[app], recv_sem=r_recv.at[app],
            device_id=(row, to), device_id_type=MESH,
        )

    def send_blocks(app):
        for t in far_first:
            pltpu.make_async_remote_copy(
                src_ref=pres.at[app], dst_ref=blocks.at[app, t - 1],
                send_sem=b_send.at[app], recv_sem=b_recv.at[app],
                device_id=(row, lax.rem(col + t, cols)), device_id_type=MESH,
            ).start()

    def apply_matrix(app, pre, meanwhile):
        piece[app] = jnp.concatenate([pre[:, :half], pre[:, half:]], axis=0).astype(bf16)

        @pl.loop(0, chips)
        def _(t):
            @pl.when(far_row(t) != row)
            def _():
                piece_copy(app, t).start()

            @pl.when(far_row(t) == row)
            def _():
                own_piece_copy(app).start()

        meanwhile()

        @pl.loop(0, cols)
        def _(k):
            pltpu.make_async_copy(gbuf.at[app, k], gbuf.at[app, k], z_recv.at[app, k]).wait()

            @pl.when(k != col)
            def _():
                plane_copy(app, k).start()

            @pl.when(k == col)
            def _():
                pltpu.make_async_copy(gbuf.at[app, k], zbuf.at[app, core, col], q_recv.at[app]).start()

        def products(which):
            near_sum = jnp.zeros((SYS * cols, c), f32)
            far_sum = jnp.zeros((SYS * cols, rank), f32)
            for j in range(count):
                z = zbuf[app, which, :, j].astype(f32)
                z = jnp.concatenate(
                    [z[:, :SYS].reshape(SYS * cols, half), z[:, SYS:].reshape(SYS * cols, half)], axis=1
                )
                at = which * count + j
                near_in = z * flags[0, at].astype(f32)
                far_in = (z - near_in).astype(bf16)
                near_sum += jnp.dot(near_in.astype(bf16), near[at], preferred_element_type=f32)
                far_sum += lax.dot_general(
                    far_in, far[at], (((1,), (1,)), ((), ())), preferred_element_type=f32
                )
            return near_sum, far_sum

        pltpu.make_async_copy(zbuf.at[app, core], zbuf.at[app, core], q_recv.at[app]).wait()
        core_copy(app).start()
        near_sum, far_sum = products(core)
        core_copy(app).wait_recv()
        near_other, far_other = products(1 - core)
        near_sum += near_other
        far_sum += far_other
        pbuf[app, :, :, :c] = near_sum.reshape(cols, SYS, c)
        pbuf[app, :, :, c:] = jnp.concatenate(
            [far_sum, jnp.zeros((SYS * cols, 128 - rank), f32)], axis=1
        ).reshape(cols, SYS, 128)

        for t in far_first:
            r_copy(app, t).start()

        pltpu.make_async_copy(part.at[app], part.at[app], r_recv.at[app]).wait()
        both = pbuf[app, col]
        for t in range(cols - 1):
            both += part[app, t]
        far_part = jnp.dot(
            both[:, c:c + rank].astype(bf16), basis[...], preferred_element_type=f32
        )
        return selft[...] * pre + both[:, :c] + far_part

    lane = lax.broadcasted_iota(jnp.int32, (SYS, 128), 1)

    def spread_squares():
        @pl.when(group > 0)
        def _():
            spread(0)

    chain(0, v * SCALE, spread_squares)

    @pl.when(group == 0)
    def _():
        spread(0)


    @pl.when(both_of(late, core == 0))
    def _():
        offer()

    @pl.when(both_of(late, core == 1))
    def _():
        form_pair()

    @pl.when(both_of(gives, direct))
    def _():
        for n in range(PIECES):
            matrix_copy(member, n).start()

    arrive(0)
    own_square = stile[0]
    squares = own_square
    for t in range(rows - 1):
        squares += gath[0, t]
    beta_tile = jnp.sqrt(squares + epsilon)
    beta = beta_tile[:, :1]
    first = v / beta
    pre_one = pcur[0] * (1.0 / SCALE / beta)
    pres[0] = pre_one

    def wait_loads():
        for copy in loads[3:]:
            copy.wait()
        roots[rows - 1] = jnp.sqrt(own_square) / beta_tile
        for t in range(rows - 1):
            roots[t] = jnp.sqrt(gath[0, t]) / beta_tile

        @pl.when(both_of(at_end, walked(0)))
        def _():
            take_matrices()

    image = apply_matrix(0, pre_one, wait_loads)

    root = roots[rows - 1][:, :1]
    some = root > 1e-15
    unit_one = jnp.where(some, first / jnp.where(some, root, 1.0), 0.0)
    along = total(unit_one * image)
    left = image - along * unit_one
    rest = jnp.sqrt(total(left * left))

    def lanes(*values):
        tile = jnp.zeros((SYS, 128), f32)
        for at, value in values:
            tile = jnp.where(lane == at, value, tile)
        return tile

    stile[1] = lanes((0, total(first * image)), (1, along), (2, rest))

    first_solver = both_of(at_end, group == 0)

    def spread_heights():
        @pl.when(jnp.logical_not(first_solver))
        def _():
            spread(1)
            send_blocks(0)

    chain(1, image, spread_heights)

    @pl.when(first_solver)
    def _():
        spread(1)
        send_blocks(0)

    arrive(1)
    heights = stile[1]
    for t in range(rows - 1):
        heights += gath[1, t]
    proj_one = heights[:, :1]
    weight = jnp.where(lane == 1, proj_one, 0.0)
    keep = jnp.where(jnp.logical_or(lane == 1, lane == 2), 1.0, 0.0)

    def term(tile, size):
        y = (tile - weight * size) * keep
        return y * y

    squares = term(stile[1], roots[rows - 1])
    for t in range(rows - 1):
        squares += term(gath[1, t], roots[t])
    norm_one = jnp.sqrt(total(squares) + epsilon)
    second = (image - proj_one * first) / norm_one
    pre_two = (pcur[1] - proj_one * pre_one) / norm_one
    pres[1] = pre_two
    frame = []

    def local_frame():
        turn = total(unit_one * second)
        across = second - turn * unit_one
        again = total(unit_one * across)
        across = across - again * unit_one
        turn = turn + again
        size = jnp.sqrt(total(across * across))
        some = size > 1e-15
        unit_two = jnp.where(some, across / jnp.where(some, size, 1.0), 0.0)
        frame.extend((turn, size, unit_two))

    image = apply_matrix(1, pre_two, local_frame)
    turn, size, unit_two = frame
    along_one = total(unit_one * image)
    left = image - along_one * unit_one
    along_two = total(unit_two * left)
    left = left - along_two * unit_two
    stile[2] = lanes(
        (0, total(first * image)), (1, total(second * image)),
        (2, along_one), (4, along_two), (6, jnp.sqrt(total(left * left))),
        (66, turn), (68, size),
    )
    spread(2)
    send_blocks(1)
    arrive(2)
    heights = stile[2]
    for t in range(rows - 1):
        heights += gath[2, t]
    cross = heights[:, :1]
    proj_two = heights[:, 1:2]
    weight = jnp.where(lane == 2, cross, 0.0)
    keep = jnp.where(
        jnp.logical_or(lane == 2, jnp.logical_or(lane == 4, lane == 6)), 1.0, 0.0
    )

    def term_two(tile, size):
        y = (tile - weight * size - proj_two * pltpu.roll(tile, 64, 1)) * keep
        return y * y

    squares = term_two(stile[2], roots[rows - 1])
    for t in range(rows - 1):
        squares += term_two(gath[2, t], roots[t])
    norm_two = jnp.sqrt(total(squares) + epsilon)
    weight_one, weight_two = least_squares(beta, proj_one, norm_one, cross, proj_two, norm_two)
    fsend[...] = lanes((0, weight_one), (1, weight_two))

    def f_copy(t):
        return pltpu.make_async_remote_copy(
            src_ref=fsend, dst_ref=fin.at[t - 1], send_sem=f_send, recv_sem=f_recv,
            device_id=(row, lax.rem(col + t, cols)), device_id_type=MESH,
        )

    for t in far_first:
        f_copy(t).start()

    out[pl.ds(pl.multiple_of(col * SYS, SYS), SYS), :] = pre_one * weight_one + pre_two * weight_two

    @pl.when(core == 0)
    def _():
        @pl.loop(0, c // tile)
        def _(t):
            to_sibling(t).wait_send()

    @pl.when(gives)
    def _():
        given = rbuf.at[0, pl.ds(0, half)]
        pltpu.make_async_copy(given, given, s_r_send).wait()

    @pl.when(at_end)
    def _():
        passed = rbuf.at[:, pl.ds(0, half)]
        pltpu.make_async_copy(passed, passed, s_q_send).wait()

    for app in range(2):
        @pl.when(core == 0)
        def _():
            c_copy(app).wait_send()

        @pl.when(forwards(app))
        def _():
            p_copy(app, 0).wait_send()

        @pl.when(forwards_to_one(app))
        def _():
            p_copy(app, 1).wait_send()

        @pl.when(leaps(app))
        def _():
            p_copy(app, 2).wait_send()

        @pl.when(both_of(gives, jnp.logical_not(walked(app))))
        def _():
            term_copy(app, member).wait_send()

        @pl.when(both_of(at_end, jnp.logical_not(walked(app))))
        def _():
            for y in range(GROUP - 1):
                for copy in step_copies(app, y):
                    copy.wait_send()

        @pl.loop(0, chips)
        def _(t):
            @pl.when(far_row(t) != row)
            def _():
                piece_copy(app, t).wait_send()

        sent = zbuf.at[app, 0, pl.ds(0, cols - 1)]
        pltpu.make_async_copy(sent, sent, q_send.at[app]).wait()
        core_copy(app).wait_send()

        pltpu.make_async_copy(part.at[app], part.at[app], r_send.at[app]).wait()
        pltpu.make_async_copy(blocks.at[app], blocks.at[app], b_send.at[app]).wait()
        pltpu.make_async_copy(blocks.at[app], blocks.at[app], b_recv.at[app]).wait()

    for n in range(3):
        pltpu.make_async_copy(gath.at[n], gath.at[n], g_send.at[n]).wait()

    pltpu.make_async_copy(fin, fin, f_recv).wait()
    for t in range(1, cols):
        at = lax.rem(col + cols - t, cols)
        out[pl.ds(pl.multiple_of(at * SYS, SYS), SYS), :] = (
            blocks[0, t - 1] * fin[t - 1, :, 0:1] + blocks[1, t - 1] * fin[t - 1, :, 1:2]
        )
    pltpu.make_async_copy(fin, fin, f_send).wait()


def body(rows, cols, rhs, flags, near, far, basis, selft, dinv, low):
    c = dinv.shape[-1]
    per = rows // cols
    tile = min(128, c)
    vm = pltpu.VMEM
    dma = pltpu.SemaphoreType.DMA
    vmem = pl.BlockSpec(memory_space=pltpu.VMEM)
    smem = pl.BlockSpec(memory_space=pltpu.SMEM)
    hbm = pl.BlockSpec(memory_space=pl.ANY)
    rank = basis.shape[1]
    return pl.pallas_call(
        functools.partial(kernel, rows, cols, tile),
        out_shape=jax.ShapeDtypeStruct(rhs.shape, f32),
        in_specs=[hbm, smem] + [hbm] * 6,
        out_specs=vmem,
        scratch_shapes=[
            vm((SYS, c), f32), vm((per, c, c), bf16), vm((per, rank, c), bf16), vm((rank, c), bf16),
            vm((1, c), f32), vm((c, c), f32), vm((c, c), f32), dma((7,)),
            vm((GROUP - 1, c, 2 * c), bf16),
            vm((2, GROUP - 1, SYS, c), f32),
            vm((2, GROUP - 1, SYS, c), f32),
            vm((rows, SYS, 128), f32),
            vm((2, SYS, c), f32),
            vm((2, cols - 1, SYS, c), f32),
            dma(()), dma((GROUP - 1, PIECES)), dma((2,)), dma((2,)),
            dma(()), dma((GROUP - 1, PIECES)), dma((2,)), dma((2, GROUP - 1)), dma((2, 2 * GROUP)),
            vm((c, 2 * c), bf16),
            vm((2, c, 2 * c), bf16),
            vm((c, 2 * c), bf16),
            vm((2, SYS, c), f32),
            vm((2, SYS, c), f32),
            vm((2, SYS, c), f32),
            vm((2, SYS, c), f32),
            vm((2, SYS, c), f32),
            vm((2, 2 * SYS, c // 2), bf16),
            vm((2, cols, per // 2, 2 * SYS, c // 2), bf16),
            vm((2, 2, cols, per // 2, 2 * SYS, c // 2), bf16),
            vm((2, cols, SYS, c + 128), f32),
            vm((2, cols - 1, SYS, c + 128), f32),
            vm((3, SYS, 128), f32),
            vm((3, rows - 1, SYS, 128), f32),
            vm((SYS, 128), f32),
            vm((cols - 1, SYS, 128), f32),
            dma((c // tile,)), dma((c // tile,)),
            dma((2,)), dma((2,)),
            dma((2, 3)), dma((2,)),
            dma((2, rows // 2)), dma((2, cols)),
            dma((2,)), dma((2,)),
            dma((2,)), dma((2,)),
            dma((2,)), dma((2,)),
            dma((3,)), dma((3,)),
            dma(()), dma(()),
        ],
        compiler_params=pltpu.CompilerParams(
            collective_id=0, has_side_effects=True, vmem_limit_bytes=60 * 2**20
        ),
    )(rhs, flags, near, far, basis, selft.reshape(1, -1), dinv, low)


def solution(mesh):
    placed = (
        P(None, "row"),
        P("row", "col"),
        P("row", "col", None, None),
        P("row", "col", None, None),
        P("row", None, None),
        P("row"),
        P("row", None, None),
        P("row", None, None),
    )
    return jax.shard_map(
        functools.partial(body, mesh.shape["row"], mesh.shape["col"]),
        mesh=mesh, in_specs=placed, out_specs=P(None, "row"), check_vma=False,
    )
```

```python
import functools

import jax
import jax.numpy as jnp
from jax import lax
from jax.experimental import pallas as pl
from jax.experimental.pallas import tpu as pltpu
from jax.sharding import PartitionSpec as P

epsilon = 1e-06
PIECES = 8
SCALE = 2.0 ** -13
f32 = jnp.float32
bf16 = jnp.bfloat16
MESH = pl.DeviceIdType.MESH
SYS = 8
GROUP = 4
HOPS = (2, 0)


def stacked(x):
    high = x.astype(bf16).astype(f32)
    return jnp.concatenate([high, x - high], axis=0).astype(bf16)


def times(x, mat):
    y = jnp.dot(stacked(x), mat, preferred_element_type=f32)
    n, c = x.shape[0], mat.shape[1] // 2
    y = y[:n] + y[n:]
    return y[:, :c] + y[:, c:]


def put_split(ref, rows, m):
    c = m.shape[1]
    high = m.astype(bf16)
    ref[rows, :c] = high
    ref[rows, c:] = (m - high.astype(f32)).astype(bf16)


def total(x):
    return jnp.sum(x, axis=1, keepdims=True)


def least_squares(beta, proj_one, norm_one, cross, proj_two, norm_two):
    radius_one = jnp.sqrt(proj_one * proj_one + norm_one * norm_one)
    cos_one = proj_one / radius_one
    sin_one = norm_one / radius_one
    upper = cos_one * cross + sin_one * proj_two
    middle = cos_one * proj_two - sin_one * cross
    radius_two = jnp.sqrt(middle * middle + norm_two * norm_two)
    weight_two = -(middle / radius_two) * sin_one * beta / radius_two
    weight_one = (cos_one * beta - upper * weight_two) / radius_one
    return (weight_one, weight_two)


def kernel(
    rows, cols, tile,
    rhs_hbm, flags, near_hbm, far_hbm, basis_hbm, selft_hbm, dinv_hbm, low_hbm, out,
    rhs, near, far, basis, selft, dinv, low, load,
    rbuf, sbuf, sol, roots, pres, blocks, s_q_send, s_q_recv, b_send, b_recv, s_r_send, s_r_recv, s_e_send, s_e_recv, s_p_send,
    dsp, mats, m0, crecv, csend, ebuf, prev, pcur, piece, gbuf, zbuf, pbuf, part, stile, gath, fsend, fin,
    m_send, m_recv, c_send, c_recv, p_send, p_recv, z_send, z_recv, q_send, q_recv, x_send, x_recv, r_send, r_recv, g_send, g_recv,
    f_send, f_recv,
):
    row = lax.axis_index("row")
    col = lax.axis_index("col")
    chip = row // 2
    core = row % 2
    last = rows // 2 - 1
    per = rows // cols
    home = row // per
    c = dinv.shape[-1]
    half = c // 2
    rank = basis.shape[0]
    group = chip // GROUP
    member = chip % GROUP
    groups = rows // 2 // GROUP
    at_end = jnp.logical_and(core == 1, member == GROUP - 1)
    gives = jnp.logical_and(core == 1, member < GROUP - 1)
    solver = 2 * GROUP * group + 2 * GROUP - 1

    loads = [
        pltpu.make_async_copy(source, target, load.at[n])
        for n, (source, target) in enumerate((
            (dinv_hbm.at[0], dinv), (low_hbm.at[0], low),
            (rhs_hbm.at[pl.ds(pl.multiple_of(col * SYS, SYS), SYS)], rhs),
            (near_hbm.at[0], near), (far_hbm.at[0], far), (basis_hbm.at[0], basis), (selft_hbm, selft),
        ))
    ]
    for copy in loads:
        copy.start()

    bar = pltpu.get_barrier_semaphore()

    def tell(r, k):
        pl.semaphore_signal(bar, inc=1, device_id=(r, k), device_id_type=MESH)

    @pl.loop(1, rows)
    def _(t):
        tell(lax.rem(row + t, rows), col)

    @pl.loop(1, cols)
    def _(t):
        tell(row, lax.rem(col + t, cols))

    def spread(turn):
        @pl.loop(1, rows)
        def _(t):
            pltpu.make_async_remote_copy(
                src_ref=stile.at[turn], dst_ref=gath.at[turn, t - 1],
                send_sem=g_send.at[turn], recv_sem=g_recv.at[turn],
                device_id=(lax.rem(row + t, rows), col), device_id_type=MESH,
            ).start()

    def arrive(turn):
        pltpu.make_async_copy(gath.at[turn], gath.at[turn], g_recv.at[turn]).wait()

    loads[0].wait()

    @pl.loop(0, c // tile)
    def _(t):
        at = pl.ds(pl.multiple_of(t * tile, tile), tile)
        put_split(dsp, at, dinv[at, :])

    place = 1 - core
    loads[1].wait()

    @pl.loop(0, c // tile)
    def _(t):
        at = pl.ds(pl.multiple_of(t * tile, tile), tile)
        put_split(mats.at[place], at, times(low[at, :], dsp[...]))

    loads[2].wait()
    v = rhs[...]
    stile[0] = jnp.broadcast_to(total(v * v), (SYS, 128))
    pl.semaphore_wait(bar, rows + cols - 2)

    def to_sibling(t):
        at = pl.ds(pl.multiple_of(t * tile, tile), tile)
        return pltpu.make_async_remote_copy(
            src_ref=mats.at[1, at], dst_ref=m0.at[at],
            send_sem=m_send.at[t], recv_sem=m_recv.at[t],
            device_id=(row - core + 1, col), device_id_type=MESH,
        )

    tiles = c // tile
    odd = lax.rem(col, 2)

    def tile_at(u):
        return lax.rem(u + odd * (tiles // 2), tiles)

    def offer():
        @pl.loop(0, tiles)
        def _(u):
            to_sibling(tile_at(u)).start()

    late = chip < GROUP // 2

    @pl.when(jnp.logical_and(core == 0, jnp.logical_not(late)))
    def _():
        offer()

    piece_rows = half // PIECES

    def part_rows(which, n):
        return pl.ds(pl.multiple_of(which * half + n * piece_rows, piece_rows), piece_rows)

    def matrix_copy(y, n):
        at = part_rows(odd, n)
        return pltpu.make_async_remote_copy(
            src_ref=mats.at[1, at], dst_ref=rbuf.at[y, at],
            send_sem=s_r_send, recv_sem=s_r_recv.at[y, n],
            device_id=(solver, col), device_id_type=MESH,
        )

    def form_pair():
        @pl.loop(0, tiles)
        def _(u):
            t = tile_at(u)
            to_sibling(t).wait_recv()
            at = pl.ds(pl.multiple_of(t * tile, tile), tile)
            both = jnp.concatenate([m0[at, :c], m0[at, c:]], axis=0)
            y = jnp.dot(both, mats[0], preferred_element_type=f32)
            y = y[:tile] + y[tile:]
            put_split(mats.at[1], at, y[:, :c] + y[:, c:])

            @pl.when(jnp.logical_and(u < tiles // 2, jnp.logical_and(gives, group > 0)))
            def _():
                each = PIECES // (tiles // 2)
                for n in range(each):
                    matrix_copy(member, u * each + n).start()

    @pl.when(jnp.logical_and(core == 1, jnp.logical_not(late)))
    def _():
        form_pair()

    def pass_copy(y, n):
        at = part_rows(odd, n)
        return pltpu.make_async_remote_copy(
            src_ref=rbuf.at[y, at], dst_ref=rbuf.at[y, at], send_sem=s_q_send,
            recv_sem=s_q_recv.at[y, n],
            device_id=(row, lax.rem(col + (1 if n % 2 == 0 else cols - 1), cols)), device_id_type=MESH,
        )

    def take_matrices():
        for n in range(PIECES):
            for y in [0] + list(range(GROUP - 2, 0, -1)):
                matrix_copy(y, n).wait_recv()
                pass_copy(y, n).start()
        for n in range(PIECES):
            for y in range(GROUP - 1):
                there = rbuf.at[y, part_rows(1 - odd, n)]
                pltpu.make_async_copy(there, there, s_q_recv.at[y, n]).wait()

    sign = jnp.where(core == 0, -1.0, 1.0).astype(f32)

    def c_copy(app):
        return pltpu.make_async_remote_copy(
            src_ref=csend.at[app], dst_ref=crecv.at[app],
            send_sem=c_send.at[app], recv_sem=c_recv.at[app],
            device_id=(row - core + 1, col), device_id_type=MESH,
        )

    def p_copy(app, to):
        target = 2 * chip + 2 + to if to < 2 else solver + 2 * GROUP
        return pltpu.make_async_remote_copy(
            src_ref=pcur.at[app], dst_ref=prev.at[app],
            send_sem=p_send.at[app, to], recv_sem=p_recv.at[app],
            device_id=(target, col), device_id_type=MESH,
        )

    def term_copy(app, y):
        return pltpu.make_async_remote_copy(
            src_ref=ebuf.at[app], dst_ref=sbuf.at[app, y], send_sem=s_e_send.at[app],
            recv_sem=s_e_recv.at[app, y], device_id=(solver, col), device_id_type=MESH,
        )

    def step_copies(app, y):
        return [
            pltpu.make_async_remote_copy(
                src_ref=sol.at[app, y], dst_ref=prev.at[app],
                send_sem=s_p_send.at[app, 2 * y + k], recv_sem=p_recv.at[app],
                device_id=(2 * GROUP * group + 2 * y + 2 + k, col), device_id_type=MESH,
            )
            for k in range(2 if y < GROUP - 2 else 1)
        ]

    def both_of(a, b):
        return jnp.logical_and(a, b)

    def walked(app):
        return group < HOPS[app]

    def forwards(app):
        return both_of(chip < last, both_of(core == 1, jnp.logical_or(walked(app), at_end)))

    def forwards_to_one(app):
        return both_of(forwards(app), chip >= GROUP // 2 - 1) if app == 0 else forwards(app)

    def leaps(app):
        return both_of(forwards(app), both_of(at_end, group + 1 >= HOPS[app]))

    def chain(app, vec, between):
        own = times(vec, dsp[...])
        solved = jnp.logical_not(walked(app))

        @pl.when(core == 0)
        def _():
            csend[app] = own

            if app == 0:
                @pl.when(both_of(late, chip > 0))
                def _():
                    p_copy(app, 0).wait_recv()
                    csend[app] = own - times(prev[app], mats[1])

            c_copy(app).start()
            ebuf[app] = csend[app]

        @pl.when(core == 1)
        def _():
            c_copy(app).wait_recv()
            ebuf[app] = own - times(crecv[app], mats[0])

        @pl.when(both_of(gives, solved))
        def _():
            term_copy(app, member).start()

        between()

        @pl.when(both_of(at_end, solved))
        def _():
            if app == 0:
                take_matrices()

            for y in range(GROUP - 1):
                term_copy(app, y).wait_recv()

            @pl.when(group == 0)
            def _():
                sol[app, 0] = sbuf[app, 0]

            @pl.when(group > 0)
            def _():
                p_copy(app, 0).wait_recv()
                sol[app, 0] = sbuf[app, 0] + times(prev[app], rbuf[0])

            for y in range(GROUP - 1):
                @pl.when(group == groups - 1)
                def _():
                    for copy in step_copies(app, y):
                        copy.start()

                if y < GROUP - 2:
                    sol[app, y + 1] = sbuf[app, y + 1] + times(sol[app, y], rbuf[y + 1])
                else:
                    pcur[app] = ebuf[app] + times(sol[app, y], mats[1])

        @pl.when(jnp.logical_not(both_of(at_end, solved)))
        def _():
            ready = late if app == 0 else chip == 0

            @pl.when(ready)
            def _():
                pcur[app] = ebuf[app]

            @pl.when(jnp.logical_not(ready))
            def _():
                p_copy(app, 0).wait_recv()
                pcur[app] = ebuf[app] + sign * times(prev[app], mats[1])

        @pl.when(leaps(app))
        def _():
            p_copy(app, 2).start()

        @pl.when(forwards_to_one(app))
        def _():
            p_copy(app, 1).start()

        @pl.when(forwards(app))
        def _():
            p_copy(app, 0).start()

        @pl.when(both_of(both_of(at_end, solved), group < groups - 1))
        def _():
            for y in range(GROUP - 1):
                for copy in step_copies(app, y):
                    copy.start()

    chips = rows // 2
    count = per // 2
    side = lax.rem(row, per) // count

    def far_row(t):
        return 2 * lax.rem(chip + t + chips // 2, chips) + side

    def piece_copy(app, t):
        return pltpu.make_async_remote_copy(
            src_ref=piece.at[app], dst_ref=gbuf.at[app, home, lax.rem(row, count)],
            send_sem=z_send.at[app, t], recv_sem=z_recv.at[app, home],
            device_id=(far_row(t), col), device_id_type=MESH,
        )

    def own_piece_copy(app):
        return pltpu.make_async_copy(
            piece.at[app], gbuf.at[app, home, lax.rem(row, count)], z_recv.at[app, home]
        )

    def plane_copy(app, k):
        return pltpu.make_async_remote_copy(
            src_ref=gbuf.at[app, k], dst_ref=zbuf.at[app, core, col],
            send_sem=q_send.at[app], recv_sem=q_recv.at[app],
            device_id=(row, k), device_id_type=MESH,
        )

    far_first = sorted(range(1, cols), key=lambda t: -min(t, cols - t))

    def core_copy(app):
        return pltpu.make_async_remote_copy(
            src_ref=zbuf.at[app, core], dst_ref=zbuf.at[app, core],
            send_sem=x_send.at[app], recv_sem=x_recv.at[app],
            device_id=(row + 1 - 2 * core, col), device_id_type=MESH,
        )

    def r_copy(app, t):
        to = lax.rem(col + t, cols)
        return pltpu.make_async_remote_copy(
            src_ref=pbuf.at[app, to], dst_ref=part.at[app, t - 1],
            send_sem=r_send.at[app], recv_sem=r_recv.at[app],
            device_id=(row, to), device_id_type=MESH,
        )

    def send_blocks(app):
        for t in far_first:
            pltpu.make_async_remote_copy(
                src_ref=pres.at[app], dst_ref=blocks.at[app, t - 1],
                send_sem=b_send.at[app], recv_sem=b_recv.at[app],
                device_id=(row, lax.rem(col + t, cols)), device_id_type=MESH,
            ).start()

    def apply_matrix(app, pre, meanwhile):
        piece[app] = jnp.concatenate([pre[:, :half], pre[:, half:]], axis=0).astype(bf16)

        @pl.loop(0, chips)
        def _(t):
            @pl.when(far_row(t) != row)
            def _():
                piece_copy(app, t).start()

            @pl.when(far_row(t) == row)
            def _():
                own_piece_copy(app).start()

        meanwhile()

        @pl.loop(0, cols)
        def _(k):
            pltpu.make_async_copy(gbuf.at[app, k], gbuf.at[app, k], z_recv.at[app, k]).wait()

            @pl.when(k != col)
            def _():
                plane_copy(app, k).start()

            @pl.when(k == col)
            def _():
                pltpu.make_async_copy(gbuf.at[app, k], zbuf.at[app, core, col], q_recv.at[app]).start()

        def products(which):
            near_sum = jnp.zeros((SYS * cols, c), f32)
            far_sum = jnp.zeros((SYS * cols, rank), f32)
            for j in range(count):
                z = zbuf[app, which, :, j].astype(f32)
                z = jnp.concatenate(
                    [z[:, :SYS].reshape(SYS * cols, half), z[:, SYS:].reshape(SYS * cols, half)], axis=1
                )
                at = which * count + j
                near_in = z * flags[0, at].astype(f32)
                far_in = (z - near_in).astype(bf16)
                near_sum += jnp.dot(near_in.astype(bf16), near[at], preferred_element_type=f32)
                far_sum += lax.dot_general(
                    far_in, far[at], (((1,), (1,)), ((), ())), preferred_element_type=f32
                )
            return near_sum, far_sum

        pltpu.make_async_copy(zbuf.at[app, core], zbuf.at[app, core], q_recv.at[app]).wait()
        core_copy(app).start()
        near_sum, far_sum = products(core)
        core_copy(app).wait_recv()
        near_other, far_other = products(1 - core)
        near_sum += near_other
        far_sum += far_other
        pbuf[app, :, :, :c] = near_sum.reshape(cols, SYS, c)
        pbuf[app, :, :, c:] = jnp.concatenate(
            [far_sum, jnp.zeros((SYS * cols, 128 - rank), f32)], axis=1
        ).reshape(cols, SYS, 128)

        for t in far_first:
            r_copy(app, t).start()

        pltpu.make_async_copy(part.at[app], part.at[app], r_recv.at[app]).wait()
        both = pbuf[app, col]
        for t in range(cols - 1):
            both += part[app, t]
        far_part = jnp.dot(
            both[:, c:c + rank].astype(bf16), basis[...], preferred_element_type=f32
        )
        return selft[...] * pre + both[:, :c] + far_part

    lane = lax.broadcasted_iota(jnp.int32, (SYS, 128), 1)

    def spread_squares():
        @pl.when(group > 0)
        def _():
            spread(0)

    chain(0, v * SCALE, spread_squares)

    @pl.when(group == 0)
    def _():
        spread(0)


    @pl.when(both_of(late, core == 0))
    def _():
        offer()

    @pl.when(both_of(late, core == 1))
    def _():
        form_pair()

    @pl.when(both_of(gives, group == 0))
    def _():
        for n in range(PIECES):
            matrix_copy(member, n).start()

    arrive(0)
    own_square = stile[0]
    squares = own_square
    for t in range(rows - 1):
        squares += gath[0, t]
    beta_tile = jnp.sqrt(squares + epsilon)
    beta = beta_tile[:, :1]
    first = v / beta
    pre_one = pcur[0] * (1.0 / SCALE / beta)
    pres[0] = pre_one

    def wait_loads():
        for copy in loads[3:]:
            copy.wait()
        roots[rows - 1] = jnp.sqrt(own_square) / beta_tile
        for t in range(rows - 1):
            roots[t] = jnp.sqrt(gath[0, t]) / beta_tile

        @pl.when(both_of(at_end, walked(0)))
        def _():
            take_matrices()

    image = apply_matrix(0, pre_one, wait_loads)

    root = roots[rows - 1][:, :1]
    some = root > 1e-15
    unit_one = jnp.where(some, first / jnp.where(some, root, 1.0), 0.0)
    along = total(unit_one * image)
    left = image - along * unit_one
    rest = jnp.sqrt(total(left * left))

    def lanes(*values):
        tile = jnp.zeros((SYS, 128), f32)
        for at, value in values:
            tile = jnp.where(lane == at, value, tile)
        return tile

    stile[1] = lanes((0, total(first * image)), (1, along), (2, rest))

    first_solver = both_of(at_end, group == 0)

    def spread_heights():
        @pl.when(jnp.logical_not(first_solver))
        def _():
            spread(1)
            send_blocks(0)

    chain(1, image, spread_heights)

    @pl.when(first_solver)
    def _():
        spread(1)
        send_blocks(0)

    arrive(1)
    heights = stile[1]
    for t in range(rows - 1):
        heights += gath[1, t]
    proj_one = heights[:, :1]
    weight = jnp.where(lane == 1, proj_one, 0.0)
    keep = jnp.where(jnp.logical_or(lane == 1, lane == 2), 1.0, 0.0)

    def term(tile, size):
        y = (tile - weight * size) * keep
        return y * y

    squares = term(stile[1], roots[rows - 1])
    for t in range(rows - 1):
        squares += term(gath[1, t], roots[t])
    norm_one = jnp.sqrt(total(squares) + epsilon)
    second = (image - proj_one * first) / norm_one
    pre_two = (pcur[1] - proj_one * pre_one) / norm_one
    pres[1] = pre_two
    frame = []

    def local_frame():
        turn = total(unit_one * second)
        across = second - turn * unit_one
        again = total(unit_one * across)
        across = across - again * unit_one
        turn = turn + again
        size = jnp.sqrt(total(across * across))
        some = size > 1e-15
        unit_two = jnp.where(some, across / jnp.where(some, size, 1.0), 0.0)
        frame.extend((turn, size, unit_two))

    image = apply_matrix(1, pre_two, local_frame)
    turn, size, unit_two = frame
    along_one = total(unit_one * image)
    left = image - along_one * unit_one
    along_two = total(unit_two * left)
    left = left - along_two * unit_two
    stile[2] = lanes(
        (0, total(first * image)), (1, total(second * image)),
        (2, along_one), (4, along_two), (6, jnp.sqrt(total(left * left))),
        (66, turn), (68, size),
    )
    spread(2)
    send_blocks(1)
    arrive(2)
    heights = stile[2]
    for t in range(rows - 1):
        heights += gath[2, t]
    cross = heights[:, :1]
    proj_two = heights[:, 1:2]
    weight = jnp.where(lane == 2, cross, 0.0)
    keep = jnp.where(
        jnp.logical_or(lane == 2, jnp.logical_or(lane == 4, lane == 6)), 1.0, 0.0
    )

    def term_two(tile, size):
        y = (tile - weight * size - proj_two * pltpu.roll(tile, 64, 1)) * keep
        return y * y

    squares = term_two(stile[2], roots[rows - 1])
    for t in range(rows - 1):
        squares += term_two(gath[2, t], roots[t])
    norm_two = jnp.sqrt(total(squares) + epsilon)
    weight_one, weight_two = least_squares(beta, proj_one, norm_one, cross, proj_two, norm_two)
    fsend[...] = lanes((0, weight_one), (1, weight_two))

    def f_copy(t):
        return pltpu.make_async_remote_copy(
            src_ref=fsend, dst_ref=fin.at[t - 1], send_sem=f_send, recv_sem=f_recv,
            device_id=(row, lax.rem(col + t, cols)), device_id_type=MESH,
        )

    for t in far_first:
        f_copy(t).start()

    out[pl.ds(pl.multiple_of(col * SYS, SYS), SYS), :] = pre_one * weight_one + pre_two * weight_two

    @pl.when(core == 0)
    def _():
        @pl.loop(0, c // tile)
        def _(t):
            to_sibling(t).wait_send()

    @pl.when(gives)
    def _():
        given = rbuf.at[0, pl.ds(0, half)]
        pltpu.make_async_copy(given, given, s_r_send).wait()

    @pl.when(at_end)
    def _():
        passed = rbuf.at[:, pl.ds(0, half)]
        pltpu.make_async_copy(passed, passed, s_q_send).wait()

    for app in range(2):
        @pl.when(core == 0)
        def _():
            c_copy(app).wait_send()

        @pl.when(forwards(app))
        def _():
            p_copy(app, 0).wait_send()

        @pl.when(forwards_to_one(app))
        def _():
            p_copy(app, 1).wait_send()

        @pl.when(leaps(app))
        def _():
            p_copy(app, 2).wait_send()

        @pl.when(both_of(gives, jnp.logical_not(walked(app))))
        def _():
            term_copy(app, member).wait_send()

        @pl.when(both_of(at_end, jnp.logical_not(walked(app))))
        def _():
            for y in range(GROUP - 1):
                for copy in step_copies(app, y):
                    copy.wait_send()

        @pl.loop(0, chips)
        def _(t):
            @pl.when(far_row(t) != row)
            def _():
                piece_copy(app, t).wait_send()

        sent = zbuf.at[app, 0, pl.ds(0, cols - 1)]
        pltpu.make_async_copy(sent, sent, q_send.at[app]).wait()
        core_copy(app).wait_send()

        pltpu.make_async_copy(part.at[app], part.at[app], r_send.at[app]).wait()
        pltpu.make_async_copy(blocks.at[app], blocks.at[app], b_send.at[app]).wait()
        pltpu.make_async_copy(blocks.at[app], blocks.at[app], b_recv.at[app]).wait()

    for n in range(3):
        pltpu.make_async_copy(gath.at[n], gath.at[n], g_send.at[n]).wait()

    pltpu.make_async_copy(fin, fin, f_recv).wait()
    for t in range(1, cols):
        at = lax.rem(col + cols - t, cols)
        out[pl.ds(pl.multiple_of(at * SYS, SYS), SYS), :] = (
            blocks[0, t - 1] * fin[t - 1, :, 0:1] + blocks[1, t - 1] * fin[t - 1, :, 1:2]
        )
    pltpu.make_async_copy(fin, fin, f_send).wait()


def body(rows, cols, rhs, flags, near, far, basis, selft, dinv, low):
    c = dinv.shape[-1]
    per = rows // cols
    tile = min(128, c)
    vm = pltpu.VMEM
    dma = pltpu.SemaphoreType.DMA
    vmem = pl.BlockSpec(memory_space=pltpu.VMEM)
    smem = pl.BlockSpec(memory_space=pltpu.SMEM)
    hbm = pl.BlockSpec(memory_space=pl.ANY)
    rank = basis.shape[1]
    return pl.pallas_call(
        functools.partial(kernel, rows, cols, tile),
        out_shape=jax.ShapeDtypeStruct(rhs.shape, f32),
        in_specs=[hbm, smem] + [hbm] * 6,
        out_specs=vmem,
        scratch_shapes=[
            vm((SYS, c), f32), vm((per, c, c), bf16), vm((per, rank, c), bf16), vm((rank, c), bf16),
            vm((1, c), f32), vm((c, c), f32), vm((c, c), f32), dma((7,)),
            vm((GROUP - 1, c, 2 * c), bf16),
            vm((2, GROUP - 1, SYS, c), f32),
            vm((2, GROUP - 1, SYS, c), f32),
            vm((rows, SYS, 128), f32),
            vm((2, SYS, c), f32),
            vm((2, cols - 1, SYS, c), f32),
            dma(()), dma((GROUP - 1, PIECES)), dma((2,)), dma((2,)),
            dma(()), dma((GROUP - 1, PIECES)), dma((2,)), dma((2, GROUP - 1)), dma((2, 2 * GROUP)),
            vm((c, 2 * c), bf16),
            vm((2, c, 2 * c), bf16),
            vm((c, 2 * c), bf16),
            vm((2, SYS, c), f32),
            vm((2, SYS, c), f32),
            vm((2, SYS, c), f32),
            vm((2, SYS, c), f32),
            vm((2, SYS, c), f32),
            vm((2, 2 * SYS, c // 2), bf16),
            vm((2, cols, per // 2, 2 * SYS, c // 2), bf16),
            vm((2, 2, cols, per // 2, 2 * SYS, c // 2), bf16),
            vm((2, cols, SYS, c + 128), f32),
            vm((2, cols - 1, SYS, c + 128), f32),
            vm((3, SYS, 128), f32),
            vm((3, rows - 1, SYS, 128), f32),
            vm((SYS, 128), f32),
            vm((cols - 1, SYS, 128), f32),
            dma((c // tile,)), dma((c // tile,)),
            dma((2,)), dma((2,)),
            dma((2, 3)), dma((2,)),
            dma((2, rows // 2)), dma((2, cols)),
            dma((2,)), dma((2,)),
            dma((2,)), dma((2,)),
            dma((2,)), dma((2,)),
            dma((3,)), dma((3,)),
            dma(()), dma(()),
        ],
        compiler_params=pltpu.CompilerParams(
            collective_id=0, has_side_effects=True, vmem_limit_bytes=60 * 2**20
        ),
    )(rhs, flags, near, far, basis, selft.reshape(1, -1), dinv, low)


def solution(mesh):
    placed = (
        P(None, "row"),
        P("row", "col"),
        P("row", "col", None, None),
        P("row", "col", None, None),
        P("row", None, None),
        P("row"),
        P("row", None, None),
        P("row", None, None),
    )
    return jax.shard_map(
        functools.partial(body, mesh.shape["row"], mesh.shape["col"]),
        mesh=mesh, in_specs=placed, out_specs=P(None, "row"), check_vma=False,
    )
```

```python
import functools

import jax
import jax.numpy as jnp
from jax import lax
from jax.experimental import pallas as pl
from jax.experimental.pallas import tpu as pltpu
from jax.sharding import PartitionSpec as P

epsilon = 1e-06
PIECES = 8
SCALE = 2.0 ** -13
f32 = jnp.float32
bf16 = jnp.bfloat16
MESH = pl.DeviceIdType.MESH
SYS = 8
GROUP = 4
HOPS = (2, 0)


def stacked(x):
    high = x.astype(bf16).astype(f32)
    return jnp.concatenate([high, x - high], axis=0).astype(bf16)


def times(x, mat):
    y = jnp.dot(stacked(x), mat, preferred_element_type=f32)
    n, c = x.shape[0], mat.shape[1] // 2
    y = y[:n] + y[n:]
    return y[:, :c] + y[:, c:]


def put_split(ref, rows, m):
    c = m.shape[1]
    high = m.astype(bf16)
    ref[rows, :c] = high
    ref[rows, c:] = (m - high.astype(f32)).astype(bf16)


def total(x):
    return jnp.sum(x, axis=1, keepdims=True)


def least_squares(beta, proj_one, norm_one, cross, proj_two, norm_two):
    radius_one = jnp.sqrt(proj_one * proj_one + norm_one * norm_one)
    cos_one = proj_one / radius_one
    sin_one = norm_one / radius_one
    upper = cos_one * cross + sin_one * proj_two
    middle = cos_one * proj_two - sin_one * cross
    radius_two = jnp.sqrt(middle * middle + norm_two * norm_two)
    weight_two = -(middle / radius_two) * sin_one * beta / radius_two
    weight_one = (cos_one * beta - upper * weight_two) / radius_one
    return (weight_one, weight_two)


def kernel(
    rows, cols, tile,
    rhs_hbm, flags, near_hbm, far_hbm, basis_hbm, selft_hbm, dinv_hbm, low_hbm, out,
    rhs, near, far, basis, selft, dinv, low, load,
    rbuf, sbuf, sol, roots, pres, blocks, s_q_send, s_q_recv, b_send, b_recv, s_r_send, s_r_recv, s_e_send, s_e_recv, s_p_send,
    dsp, mats, m0, crecv, csend, ebuf, prev, pcur, piece, gbuf, zbuf, pbuf, part, stile, gath, fsend, fin,
    m_send, m_recv, c_send, c_recv, p_send, p_recv, z_send, z_recv, q_send, q_recv, x_send, x_recv, r_send, r_recv, g_send, g_recv,
    f_send, f_recv,
):
    row = lax.axis_index("row")
    col = lax.axis_index("col")
    chip = row // 2
    core = row % 2
    last = rows // 2 - 1
    per = rows // cols
    home = row // per
    c = dinv.shape[-1]
    half = c // 2
    rank = basis.shape[0]
    group = chip // GROUP
    member = chip % GROUP
    groups = rows // 2 // GROUP
    at_end = jnp.logical_and(core == 1, member == GROUP - 1)
    gives = jnp.logical_and(core == 1, member < GROUP - 1)
    solver = 2 * GROUP * group + 2 * GROUP - 1

    loads = [
        pltpu.make_async_copy(source, target, load.at[n])
        for n, (source, target) in enumerate((
            (dinv_hbm.at[0], dinv), (low_hbm.at[0], low),
            (rhs_hbm.at[pl.ds(pl.multiple_of(col * SYS, SYS), SYS)], rhs),
            (near_hbm.at[0], near), (far_hbm.at[0], far), (basis_hbm.at[0], basis), (selft_hbm, selft),
        ))
    ]
    for copy in loads:
        copy.start()

    bar = pltpu.get_barrier_semaphore()

    def tell(r, k):
        pl.semaphore_signal(bar, inc=1, device_id=(r, k), device_id_type=MESH)

    @pl.loop(1, rows)
    def _(t):
        tell(lax.rem(row + t, rows), col)

    @pl.loop(1, cols)
    def _(t):
        tell(row, lax.rem(col + t, cols))

    def spread(turn):
        @pl.loop(1, rows)
        def _(t):
            pltpu.make_async_remote_copy(
                src_ref=stile.at[turn], dst_ref=gath.at[turn, t - 1],
                send_sem=g_send.at[turn], recv_sem=g_recv.at[turn],
                device_id=(lax.rem(row + t, rows), col), device_id_type=MESH,
            ).start()

    def arrive(turn):
        pltpu.make_async_copy(gath.at[turn], gath.at[turn], g_recv.at[turn]).wait()

    loads[0].wait()

    @pl.loop(0, c // tile)
    def _(t):
        at = pl.ds(pl.multiple_of(t * tile, tile), tile)
        put_split(dsp, at, dinv[at, :])

    place = 1 - core
    loads[1].wait()

    @pl.loop(0, c // tile)
    def _(t):
        at = pl.ds(pl.multiple_of(t * tile, tile), tile)
        put_split(mats.at[place], at, times(low[at, :], dsp[...]))

    loads[2].wait()
    v = rhs[...]
    stile[0] = jnp.broadcast_to(total(v * v), (SYS, 128))
    pl.semaphore_wait(bar, rows + cols - 2)

    def to_sibling(t):
        at = pl.ds(pl.multiple_of(t * tile, tile), tile)
        return pltpu.make_async_remote_copy(
            src_ref=mats.at[1, at], dst_ref=m0.at[at],
            send_sem=m_send.at[t], recv_sem=m_recv.at[t],
            device_id=(row - core + 1, col), device_id_type=MESH,
        )

    tiles = c // tile
    odd = lax.rem(col, 2)

    def tile_at(u):
        return lax.rem(u + odd * (tiles // 2), tiles)

    def offer():
        @pl.loop(0, tiles)
        def _(u):
            to_sibling(tile_at(u)).start()

    late = chip < GROUP // 2

    @pl.when(jnp.logical_and(core == 0, jnp.logical_not(late)))
    def _():
        offer()

    piece_rows = half // PIECES

    def part_rows(which, n):
        return pl.ds(pl.multiple_of(which * half + n * piece_rows, piece_rows), piece_rows)

    def matrix_copy(y, n):
        at = part_rows(odd, n)
        return pltpu.make_async_remote_copy(
            src_ref=mats.at[1, at], dst_ref=rbuf.at[y, at],
            send_sem=s_r_send, recv_sem=s_r_recv.at[y, n],
            device_id=(solver, col), device_id_type=MESH,
        )

    def form_pair():
        @pl.loop(0, tiles)
        def _(u):
            t = tile_at(u)
            to_sibling(t).wait_recv()
            at = pl.ds(pl.multiple_of(t * tile, tile), tile)
            both = jnp.concatenate([m0[at, :c], m0[at, c:]], axis=0)
            y = jnp.dot(both, mats[0], preferred_element_type=f32)
            y = y[:tile] + y[tile:]
            put_split(mats.at[1], at, y[:, :c] + y[:, c:])

            @pl.when(jnp.logical_and(u < tiles // 2, jnp.logical_and(gives, group > 0)))
            def _():
                each = PIECES // (tiles // 2)
                for n in range(each):
                    matrix_copy(member, u * each + n).start()

    @pl.when(jnp.logical_and(core == 1, jnp.logical_not(late)))
    def _():
        form_pair()

    def pass_copy(y, n):
        at = part_rows(odd, n)
        return pltpu.make_async_remote_copy(
            src_ref=rbuf.at[y, at], dst_ref=rbuf.at[y, at], send_sem=s_q_send,
            recv_sem=s_q_recv.at[y, n],
            device_id=(row, lax.rem(col + (1 if n % 2 == 0 else cols - 1), cols)), device_id_type=MESH,
        )

    def take_matrices():
        for n in range(PIECES):
            for y in range(GROUP - 1):
                matrix_copy(y, n).wait_recv()
                pass_copy(y, n).start()
        for n in range(PIECES):
            for y in range(GROUP - 1):
                there = rbuf.at[y, part_rows(1 - odd, n)]
                pltpu.make_async_copy(there, there, s_q_recv.at[y, n]).wait()

    sign = jnp.where(core == 0, -1.0, 1.0).astype(f32)

    def c_copy(app):
        return pltpu.make_async_remote_copy(
            src_ref=csend.at[app], dst_ref=crecv.at[app],
            send_sem=c_send.at[app], recv_sem=c_recv.at[app],
            device_id=(row - core + 1, col), device_id_type=MESH,
        )

    def p_copy(app, to):
        target = 2 * chip + 2 + to if to < 2 else solver + 2 * GROUP
        return pltpu.make_async_remote_copy(
            src_ref=pcur.at[app], dst_ref=prev.at[app],
            send_sem=p_send.at[app, to], recv_sem=p_recv.at[app],
            device_id=(target, col), device_id_type=MESH,
        )

    def term_copy(app, y):
        return pltpu.make_async_remote_copy(
            src_ref=ebuf.at[app], dst_ref=sbuf.at[app, y], send_sem=s_e_send.at[app],
            recv_sem=s_e_recv.at[app, y], device_id=(solver, col), device_id_type=MESH,
        )

    def step_copies(app, y):
        return [
            pltpu.make_async_remote_copy(
                src_ref=sol.at[app, y], dst_ref=prev.at[app],
                send_sem=s_p_send.at[app, 2 * y + k], recv_sem=p_recv.at[app],
                device_id=(2 * GROUP * group + 2 * y + 2 + k, col), device_id_type=MESH,
            )
            for k in range(2 if y < GROUP - 2 else 1)
        ]

    def both_of(a, b):
        return jnp.logical_and(a, b)

    def walked(app):
        return group < HOPS[app]

    def forwards(app):
        return both_of(chip < last, both_of(core == 1, jnp.logical_or(walked(app), at_end)))

    def forwards_to_one(app):
        return both_of(forwards(app), chip >= GROUP // 2 - 1) if app == 0 else forwards(app)

    def leaps(app):
        return both_of(forwards(app), both_of(at_end, group + 1 >= HOPS[app]))

    def chain(app, vec, between):
        own = times(vec, dsp[...])
        solved = jnp.logical_not(walked(app))

        @pl.when(core == 0)
        def _():
            csend[app] = own

            if app == 0:
                @pl.when(both_of(late, chip > 0))
                def _():
                    p_copy(app, 0).wait_recv()
                    csend[app] = own - times(prev[app], mats[1])

            c_copy(app).start()
            ebuf[app] = csend[app]

        @pl.when(core == 1)
        def _():
            c_copy(app).wait_recv()
            ebuf[app] = own - times(crecv[app], mats[0])

        @pl.when(both_of(gives, solved))
        def _():
            term_copy(app, member).start()

        between()

        @pl.when(both_of(at_end, solved))
        def _():
            if app == 0:
                take_matrices()

            for y in range(GROUP - 1):
                term_copy(app, y).wait_recv()

            @pl.when(group == 0)
            def _():
                sol[app, 0] = sbuf[app, 0]

            @pl.when(group > 0)
            def _():
                p_copy(app, 0).wait_recv()
                sol[app, 0] = sbuf[app, 0] + times(prev[app], rbuf[0])

            for y in range(GROUP - 1):
                @pl.when(group == groups - 1)
                def _():
                    for copy in step_copies(app, y):
                        copy.start()

                if y < GROUP - 2:
                    sol[app, y + 1] = sbuf[app, y + 1] + times(sol[app, y], rbuf[y + 1])
                else:
                    pcur[app] = ebuf[app] + times(sol[app, y], mats[1])

        @pl.when(jnp.logical_not(both_of(at_end, solved)))
        def _():
            ready = late if app == 0 else chip == 0

            @pl.when(ready)
            def _():
                pcur[app] = ebuf[app]

            @pl.when(jnp.logical_not(ready))
            def _():
                p_copy(app, 0).wait_recv()
                pcur[app] = ebuf[app] + sign * times(prev[app], mats[1])

        @pl.when(leaps(app))
        def _():
            p_copy(app, 2).start()

        @pl.when(forwards_to_one(app))
        def _():
            p_copy(app, 1).start()

        @pl.when(forwards(app))
        def _():
            p_copy(app, 0).start()

        @pl.when(both_of(both_of(at_end, solved), group < groups - 1))
        def _():
            for y in range(GROUP - 1):
                for copy in step_copies(app, y):
                    copy.start()

    chips = rows // 2
    count = per // 2
    side = lax.rem(row, per) // count

    def far_row(t):
        return 2 * lax.rem(chip + t + chips // 2, chips) + side

    def piece_copy(app, t):
        return pltpu.make_async_remote_copy(
            src_ref=piece.at[app], dst_ref=gbuf.at[app, home, lax.rem(row, count)],
            send_sem=z_send.at[app, t], recv_sem=z_recv.at[app, home],
            device_id=(far_row(t), col), device_id_type=MESH,
        )

    def own_piece_copy(app):
        return pltpu.make_async_copy(
            piece.at[app], gbuf.at[app, home, lax.rem(row, count)], z_recv.at[app, home]
        )

    def plane_copy(app, k):
        return pltpu.make_async_remote_copy(
            src_ref=gbuf.at[app, k], dst_ref=zbuf.at[app, core, col],
            send_sem=q_send.at[app], recv_sem=q_recv.at[app],
            device_id=(row, k), device_id_type=MESH,
        )

    far_first = sorted(range(1, cols), key=lambda t: -min(t, cols - t))

    def core_copy(app):
        return pltpu.make_async_remote_copy(
            src_ref=zbuf.at[app, core], dst_ref=zbuf.at[app, core],
            send_sem=x_send.at[app], recv_sem=x_recv.at[app],
            device_id=(row + 1 - 2 * core, col), device_id_type=MESH,
        )

    def r_copy(app, t):
        to = lax.rem(col + t, cols)
        return pltpu.make_async_remote_copy(
            src_ref=pbuf.at[app, to], dst_ref=part.at[app, t - 1],
            send_sem=r_send.at[app], recv_sem=r_recv.at[app],
            device_id=(row, to), device_id_type=MESH,
        )

    def send_blocks(app):
        for t in far_first:
            pltpu.make_async_remote_copy(
                src_ref=pres.at[app], dst_ref=blocks.at[app, t - 1],
                send_sem=b_send.at[app], recv_sem=b_recv.at[app],
                device_id=(row, lax.rem(col + t, cols)), device_id_type=MESH,
            ).start()

    def apply_matrix(app, pre, meanwhile):
        piece[app] = jnp.concatenate([pre[:, :half], pre[:, half:]], axis=0).astype(bf16)

        @pl.loop(0, chips)
        def _(t):
            @pl.when(far_row(t) != row)
            def _():
                piece_copy(app, t).start()

            @pl.when(far_row(t) == row)
            def _():
                own_piece_copy(app).start()

        meanwhile()

        @pl.loop(0, cols)
        def _(k):
            pltpu.make_async_copy(gbuf.at[app, k], gbuf.at[app, k], z_recv.at[app, k]).wait()

            @pl.when(k != col)
            def _():
                plane_copy(app, k).start()

            @pl.when(k == col)
            def _():
                pltpu.make_async_copy(gbuf.at[app, k], zbuf.at[app, core, col], q_recv.at[app]).start()

        def products(which):
            near_sum = jnp.zeros((SYS * cols, c), f32)
            far_sum = jnp.zeros((SYS * cols, rank), f32)
            for j in range(count):
                z = zbuf[app, which, :, j].astype(f32)
                z = jnp.concatenate(
                    [z[:, :SYS].reshape(SYS * cols, half), z[:, SYS:].reshape(SYS * cols, half)], axis=1
                )
                at = which * count + j
                near_in = z * flags[0, at].astype(f32)
                far_in = (z - near_in).astype(bf16)
                near_sum += jnp.dot(near_in.astype(bf16), near[at], preferred_element_type=f32)
                far_sum += lax.dot_general(
                    far_in, far[at], (((1,), (1,)), ((), ())), preferred_element_type=f32
                )
            return near_sum, far_sum

        pltpu.make_async_copy(zbuf.at[app, core], zbuf.at[app, core], q_recv.at[app]).wait()
        core_copy(app).start()
        near_sum, far_sum = products(core)
        core_copy(app).wait_recv()
        near_other, far_other = products(1 - core)
        near_sum += near_other
        far_sum += far_other
        pbuf[app, :, :, :c] = near_sum.reshape(cols, SYS, c)
        pbuf[app, :, :, c:] = jnp.concatenate(
            [far_sum, jnp.zeros((SYS * cols, 128 - rank), f32)], axis=1
        ).reshape(cols, SYS, 128)

        for t in far_first:
            r_copy(app, t).start()

        pltpu.make_async_copy(part.at[app], part.at[app], r_recv.at[app]).wait()
        both = pbuf[app, col]
        for t in range(cols - 1):
            both += part[app, t]
        far_part = jnp.dot(
            both[:, c:c + rank].astype(bf16), basis[...], preferred_element_type=f32
        )
        return selft[...] * pre + both[:, :c] + far_part

    lane = lax.broadcasted_iota(jnp.int32, (SYS, 128), 1)

    def spread_squares():
        @pl.when(group > 0)
        def _():
            spread(0)

    chain(0, v * SCALE, spread_squares)

    @pl.when(group == 0)
    def _():
        spread(0)


    @pl.when(both_of(late, core == 0))
    def _():
        offer()

    @pl.when(both_of(late, core == 1))
    def _():
        form_pair()

    @pl.when(both_of(gives, group == 0))
    def _():
        for n in range(PIECES):
            matrix_copy(member, n).start()

    arrive(0)
    own_square = stile[0]
    squares = own_square
    for t in range(rows - 1):
        squares += gath[0, t]
    beta_tile = jnp.sqrt(squares + epsilon)
    beta = beta_tile[:, :1]
    first = v / beta
    pre_one = pcur[0] * (1.0 / SCALE / beta)
    pres[0] = pre_one

    def wait_loads():
        for copy in loads[3:]:
            copy.wait()
        roots[rows - 1] = jnp.sqrt(own_square) / beta_tile
        for t in range(rows - 1):
            roots[t] = jnp.sqrt(gath[0, t]) / beta_tile

        @pl.when(both_of(at_end, walked(0)))
        def _():
            take_matrices()

    image = apply_matrix(0, pre_one, wait_loads)

    root = roots[rows - 1][:, :1]
    some = root > 1e-15
    unit_one = jnp.where(some, first / jnp.where(some, root, 1.0), 0.0)
    along = total(unit_one * image)
    left = image - along * unit_one
    rest = jnp.sqrt(total(left * left))

    def lanes(*values):
        tile = jnp.zeros((SYS, 128), f32)
        for at, value in values:
            tile = jnp.where(lane == at, value, tile)
        return tile

    stile[1] = lanes((0, total(first * image)), (1, along), (2, rest))

    first_solver = both_of(at_end, group == 0)

    def spread_heights():
        @pl.when(jnp.logical_not(first_solver))
        def _():
            spread(1)
            send_blocks(0)

    chain(1, image, spread_heights)

    @pl.when(first_solver)
    def _():
        spread(1)
        send_blocks(0)

    arrive(1)
    heights = stile[1]
    for t in range(rows - 1):
        heights += gath[1, t]
    proj_one = heights[:, :1]
    weight = jnp.where(lane == 1, proj_one, 0.0)
    keep = jnp.where(jnp.logical_or(lane == 1, lane == 2), 1.0, 0.0)

    def term(tile, size):
        y = (tile - weight * size) * keep
        return y * y

    squares = term(stile[1], roots[rows - 1])
    for t in range(rows - 1):
        squares += term(gath[1, t], roots[t])
    norm_one = jnp.sqrt(total(squares) + epsilon)
    second = (image - proj_one * first) / norm_one
    pre_two = (pcur[1] - proj_one * pre_one) / norm_one
    pres[1] = pre_two
    frame = []

    def local_frame():
        turn = total(unit_one * second)
        across = second - turn * unit_one
        again = total(unit_one * across)
        across = across - again * unit_one
        turn = turn + again
        size = jnp.sqrt(total(across * across))
        some = size > 1e-15
        unit_two = jnp.where(some, across / jnp.where(some, size, 1.0), 0.0)
        frame.extend((turn, size, unit_two))

    image = apply_matrix(1, pre_two, local_frame)
    turn, size, unit_two = frame
    along_one = total(unit_one * image)
    left = image - along_one * unit_one
    along_two = total(unit_two * left)
    left = left - along_two * unit_two
    stile[2] = lanes(
        (0, total(first * image)), (1, total(second * image)),
        (2, along_one), (4, along_two), (6, jnp.sqrt(total(left * left))),
        (66, turn), (68, size),
    )
    spread(2)
    send_blocks(1)
    arrive(2)
    heights = stile[2]
    for t in range(rows - 1):
        heights += gath[2, t]
    cross = heights[:, :1]
    proj_two = heights[:, 1:2]
    weight = jnp.where(lane == 2, cross, 0.0)
    keep = jnp.where(
        jnp.logical_or(lane == 2, jnp.logical_or(lane == 4, lane == 6)), 1.0, 0.0
    )

    def term_two(tile, size):
        y = (tile - weight * size - proj_two * pltpu.roll(tile, 64, 1)) * keep
        return y * y

    squares = term_two(stile[2], roots[rows - 1])
    for t in range(rows - 1):
        squares += term_two(gath[2, t], roots[t])
    norm_two = jnp.sqrt(total(squares) + epsilon)
    weight_one, weight_two = least_squares(beta, proj_one, norm_one, cross, proj_two, norm_two)
    fsend[...] = lanes((0, weight_one), (1, weight_two))

    def f_copy(t):
        return pltpu.make_async_remote_copy(
            src_ref=fsend, dst_ref=fin.at[t - 1], send_sem=f_send, recv_sem=f_recv,
            device_id=(row, lax.rem(col + t, cols)), device_id_type=MESH,
        )

    for t in far_first:
        f_copy(t).start()

    out[pl.ds(pl.multiple_of(col * SYS, SYS), SYS), :] = pre_one * weight_one + pre_two * weight_two

    @pl.when(core == 0)
    def _():
        @pl.loop(0, c // tile)
        def _(t):
            to_sibling(t).wait_send()

    @pl.when(gives)
    def _():
        given = rbuf.at[0, pl.ds(0, half)]
        pltpu.make_async_copy(given, given, s_r_send).wait()

    @pl.when(at_end)
    def _():
        passed = rbuf.at[:, pl.ds(0, half)]
        pltpu.make_async_copy(passed, passed, s_q_send).wait()

    for app in range(2):
        @pl.when(core == 0)
        def _():
            c_copy(app).wait_send()

        @pl.when(forwards(app))
        def _():
            p_copy(app, 0).wait_send()

        @pl.when(forwards_to_one(app))
        def _():
            p_copy(app, 1).wait_send()

        @pl.when(leaps(app))
        def _():
            p_copy(app, 2).wait_send()

        @pl.when(both_of(gives, jnp.logical_not(walked(app))))
        def _():
            term_copy(app, member).wait_send()

        @pl.when(both_of(at_end, jnp.logical_not(walked(app))))
        def _():
            for y in range(GROUP - 1):
                for copy in step_copies(app, y):
                    copy.wait_send()

        @pl.loop(0, chips)
        def _(t):
            @pl.when(far_row(t) != row)
            def _():
                piece_copy(app, t).wait_send()

        sent = zbuf.at[app, 0, pl.ds(0, cols - 1)]
        pltpu.make_async_copy(sent, sent, q_send.at[app]).wait()
        core_copy(app).wait_send()

        pltpu.make_async_copy(part.at[app], part.at[app], r_send.at[app]).wait()
        pltpu.make_async_copy(blocks.at[app], blocks.at[app], b_send.at[app]).wait()
        pltpu.make_async_copy(blocks.at[app], blocks.at[app], b_recv.at[app]).wait()

    for n in range(3):
        pltpu.make_async_copy(gath.at[n], gath.at[n], g_send.at[n]).wait()

    pltpu.make_async_copy(fin, fin, f_recv).wait()
    for t in range(1, cols):
        at = lax.rem(col + cols - t, cols)
        out[pl.ds(pl.multiple_of(at * SYS, SYS), SYS), :] = (
            blocks[0, t - 1] * fin[t - 1, :, 0:1] + blocks[1, t - 1] * fin[t - 1, :, 1:2]
        )
    pltpu.make_async_copy(fin, fin, f_send).wait()


def body(rows, cols, rhs, flags, near, far, basis, selft, dinv, low):
    c = dinv.shape[-1]
    per = rows // cols
    tile = min(128, c)
    vm = pltpu.VMEM
    dma = pltpu.SemaphoreType.DMA
    vmem = pl.BlockSpec(memory_space=pltpu.VMEM)
    smem = pl.BlockSpec(memory_space=pltpu.SMEM)
    hbm = pl.BlockSpec(memory_space=pl.ANY)
    rank = basis.shape[1]
    return pl.pallas_call(
        functools.partial(kernel, rows, cols, tile),
        out_shape=jax.ShapeDtypeStruct(rhs.shape, f32),
        in_specs=[hbm, smem] + [hbm] * 6,
        out_specs=vmem,
        scratch_shapes=[
            vm((SYS, c), f32), vm((per, c, c), bf16), vm((per, rank, c), bf16), vm((rank, c), bf16),
            vm((1, c), f32), vm((c, c), f32), vm((c, c), f32), dma((7,)),
            vm((GROUP - 1, c, 2 * c), bf16),
            vm((2, GROUP - 1, SYS, c), f32),
            vm((2, GROUP - 1, SYS, c), f32),
            vm((rows, SYS, 128), f32),
            vm((2, SYS, c), f32),
            vm((2, cols - 1, SYS, c), f32),
            dma(()), dma((GROUP - 1, PIECES)), dma((2,)), dma((2,)),
            dma(()), dma((GROUP - 1, PIECES)), dma((2,)), dma((2, GROUP - 1)), dma((2, 2 * GROUP)),
            vm((c, 2 * c), bf16),
            vm((2, c, 2 * c), bf16),
            vm((c, 2 * c), bf16),
            vm((2, SYS, c), f32),
            vm((2, SYS, c), f32),
            vm((2, SYS, c), f32),
            vm((2, SYS, c), f32),
            vm((2, SYS, c), f32),
            vm((2, 2 * SYS, c // 2), bf16),
            vm((2, cols, per // 2, 2 * SYS, c // 2), bf16),
            vm((2, 2, cols, per // 2, 2 * SYS, c // 2), bf16),
            vm((2, cols, SYS, c + 128), f32),
            vm((2, cols - 1, SYS, c + 128), f32),
            vm((3, SYS, 128), f32),
            vm((3, rows - 1, SYS, 128), f32),
            vm((SYS, 128), f32),
            vm((cols - 1, SYS, 128), f32),
            dma((c // tile,)), dma((c // tile,)),
            dma((2,)), dma((2,)),
            dma((2, 3)), dma((2,)),
            dma((2, rows // 2)), dma((2, cols)),
            dma((2,)), dma((2,)),
            dma((2,)), dma((2,)),
            dma((2,)), dma((2,)),
            dma((3,)), dma((3,)),
            dma(()), dma(()),
        ],
        compiler_params=pltpu.CompilerParams(
            collective_id=0, has_side_effects=True, vmem_limit_bytes=60 * 2**20
        ),
    )(rhs, flags, near, far, basis, selft.reshape(1, -1), dinv, low)


def solution(mesh):
    placed = (
        P(None, "row"),
        P("row", "col"),
        P("row", "col", None, None),
        P("row", "col", None, None),
        P("row", None, None),
        P("row"),
        P("row", None, None),
        P("row", None, None),
    )
    return jax.shard_map(
        functools.partial(body, mesh.shape["row"], mesh.shape["col"]),
        mesh=mesh, in_specs=placed, out_specs=P(None, "row"), check_vma=False,
    )
```
